32 devices in a mesh: tab: 4 (over y, core), row: 8 (over z, x).
Axes of the slice: x: 2, y: 2, z: 4, core: 2. Of those that a mesh axis runs over, the one named last changes fastest.
Arguments:
- ctx_feat: bfloat16 [8, 100, 2048], P('tab', None, 'row'), may hold values from -24 to 24
- qry_feat: bfloat16 [8, 100, 512], P('tab', None, 'row'), may hold values from -24 to 24
- feat_count: int32 [8], P('tab'), may hold values from 3 to 100, as said below
- ctx_count: int32 [8], P('tab'), may hold values from 1024 to 2048, as said below
- qry_count: int32 [8], P('tab'), may hold values from 256 to 512, as said below
- w_emb: bfloat16 [100, 768], replicated, may hold values from -0.625 to 0.625
- ln1_gain: float32 [768], replicated, may hold values from 0.1 to 1.9
- ln1_bias: float32 [768], replicated, may hold values from -3 to 3
- w_qkv: bfloat16 [768, 2304], replicated, may hold values from -0.21875 to 0.21875
- w_out: bfloat16 [768, 768], replicated, may hold values from -6 to 6
- ln2_gain: float32 [768], replicated, may hold values from 0.1 to 1.9
- ln2_bias: float32 [768], replicated, may hold values from -3 to 3
- w_up: bfloat16 [768, 3072], replicated, may hold values from -0.21875 to 0.21875
- b_up: float32 [3072], replicated, may hold values from -3 to 3
- w_down: bfloat16 [3072, 768], replicated, may hold values from -0.109375 to 0.109375
- ctx_cot: bfloat16 [8, 2048, 768], P('tab', 'row'), may hold values from -6 to 6
- qry_cot: bfloat16 [8, 512, 768], P('tab', 'row'), may hold values from -6 to 6
Outputs:
- ctx_out: bfloat16 [8, 2048, 768], P('tab', 'row')
- qry_out: bfloat16 [8, 512, 768], P('tab', 'row')
- ctx_feat_grad: bfloat16 [8, 100, 2048], P('tab', None, 'row')
- qry_feat_grad: bfloat16 [8, 100, 512], P('tab', None, 'row')
- grad_w_emb: float32 [100, 768], replicated
- grad_ln1_gain: float32 [768], P('row')
- grad_ln1_bias: float32 [768], P('row')
- grad_w_qkv: float32 [768, 2304], P('row')
- grad_w_out: float32 [768, 768], P('row')
- grad_ln2_gain: float32 [768], P('row')
- grad_ln2_bias: float32 [768], P('row')
- grad_w_up: float32 [768, 3072], P('row')
- grad_b_up: float32 [3072], P('row')
- grad_w_down: float32 [3072, 768], P('row')
- rms: float32 [4], replicated
The draws below stay inside these ranges and needn't reach their ends.
Inputs may be any that keep to these rules, and one draw needn't show every extreme that they name: `feat_count`: some table has all 100 slots real. `ctx_count`: among the 2 tables of each index of tab one has all 2048 context rows live. `qry_count`: among the 2 tables of each index of tab one has all 512 query rows live.
All inputs are finite; a program needn't handle non-finite values.
Results may differ from the reference program's by a relative error of at most 0.02.
Values may be sent and summed in bfloat16 or wider, within the bound.
A program may use at most 320 MiB of HBM per device.

```python
import jax
import jax.numpy as jnp
from jax import lax

D = 768
HEADS = 12
HEAD_DIM = 64
FF = 3072
F = 100
TAB_DEV = 2
TABLES = 8
CTX = 2048
QRY = 512


def ramped(values, length):
    ramp = 1.0 + 2.0 * jnp.arange(length, dtype=jnp.float32) / length
    return values * ramp


def full_in_groups(key, table_total, group_size, lowest, highest):
    counts = jax.random.randint(key, (table_total,), lowest, highest + 1)
    chosen = jax.random.randint(jax.random.fold_in(key, 1), (table_total // group_size,), 0, group_size)
    filled = jnp.arange(table_total // group_size) * group_size + chosen
    marked = jnp.any(jnp.arange(table_total)[:, None] == filled[None, :], axis=1)
    return jnp.where(marked, highest, counts).astype(jnp.int32)


def draw_ctx_feat(key, part):
    key = jax.random.fold_in(key, 11)
    base = jnp.clip(jax.random.normal(key, (TABLES, F, CTX), jnp.float32), -4.0, 4.0)
    return ramped(base, CTX).astype(jnp.bfloat16)


def draw_qry_feat(key, part):
    key = jax.random.fold_in(key, 12)
    base = jnp.clip(jax.random.normal(key, (TABLES, F, QRY), jnp.float32), -4.0, 4.0)
    return ramped(base, QRY).astype(jnp.bfloat16)


def draw_feat_count(key, part):
    key = jax.random.fold_in(key, 21)
    return full_in_groups(key, TABLES, TABLES, 3, F)


def draw_ctx_count(key, part):
    key = jax.random.fold_in(key, 22)
    return full_in_groups(key, TABLES, TAB_DEV, CTX // 2, CTX)


def draw_qry_count(key, part):
    key = jax.random.fold_in(key, 23)
    return full_in_groups(key, TABLES, TAB_DEV, QRY // 2, QRY)


def level_of(rng, shape, pieces, low, top_value):
    def one(axis_at, shards_of):
        steps = jax.random.uniform(jax.random.fold_in(jax.random.fold_in(rng, 6), axis_at), (shards_of,), jnp.float32, low / len(pieces), top_value / len(pieces))
        return jnp.repeat(jnp.exp(steps), shape[axis_at] // shards_of).reshape((-1,) + (1,) * (len(shape) - axis_at - 1))

    factor_of = one(*pieces[0])
    for cut in pieces[1:]:
        factor_of = factor_of * one(*cut)
    return factor_of


def noise(own_key, shape, deviation, reach, cuts=(), held_as=jnp.bfloat16):
    values = jax.random.normal(own_key, shape, jnp.float32) * deviation
    if len(cuts) > 0:
        values = level_of(own_key, shape, cuts, -0.22, 0.18) * values
    return jnp.clip(values, min=-reach, max=reach).astype(held_as)


def setup_inputs(seed: int = 0) -> dict:
    splits = jax.random.split(jax.random.key(seed), 18)
    ctx_feat = draw_ctx_feat(jax.random.fold_in(splits[17], 71), 0)
    qry_feat = draw_qry_feat(jax.random.fold_in(splits[17], 71), 0)
    feat_count = draw_feat_count(jax.random.fold_in(splits[17], 71), 0)
    ctx_count = draw_ctx_count(jax.random.fold_in(splits[17], 71), 0)
    qry_count = draw_qry_count(jax.random.fold_in(splits[17], 71), 0)
    w_emb = noise(splits[5], (F, D), F ** -0.5, 0.625)
    ln1_gain = jnp.clip(1.0 + 0.18 * jax.random.normal(splits[6], (D,), jnp.float32), 0.1, 1.9)
    ln1_bias = noise(splits[7], (D,), 0.5, 3.0, (), jnp.float32)
    w_qkv = noise(splits[8], (D, 3 * D), D ** -0.5, 0.21875)
    w_out = noise(splits[9], (D, D), ((CTX // D) ** 0.5 * 0.5 + 0.3), 6.0)
    ln2_gain = jnp.clip(1.0 + 0.18 * jax.random.normal(splits[10], (D,), jnp.float32), 0.1, 1.9)
    ln2_bias = noise(splits[11], (D,), 0.5, 3.0, (), jnp.float32)
    w_up = noise(splits[12], (D, FF), D ** -0.5, 0.21875)
    b_up = noise(splits[13], (FF,), 0.5, 3.0, (), jnp.float32)
    w_down = noise(splits[14], (FF, D), FF ** -0.5, 0.109375)
    ctx_cot = noise(splits[15], (TABLES, CTX, D), 1.0, 6.0, ((0, 4), (1, 8)))
    qry_cot = noise(splits[16], (TABLES, QRY, D), 1.0, 6.0, ((0, 4), (1, 8)))
    return {"ctx_feat": ctx_feat, "qry_feat": qry_feat, "feat_count": feat_count, "ctx_count": ctx_count, "qry_count": qry_count, "w_emb": w_emb, "ln1_gain": ln1_gain, "ln1_bias": ln1_bias, "w_qkv": w_qkv, "w_out": w_out, "ln2_gain": ln2_gain, "ln2_bias": ln2_bias, "w_up": w_up, "b_up": b_up, "w_down": w_down, "ctx_cot": ctx_cot, "qry_cot": qry_cot}


EPS = 1e-05
NEGATIVE = -1e+30
HIGH = lax.Precision.HIGHEST

@jax.custom_vjp
def low(v):
    return lax.optimization_barrier(v.astype(jnp.bfloat16)).astype(jnp.float32)

@jax.custom_vjp
def low_back(v):
    return v

def low_keep(v):
    return (low(v), None)

def low_pass(kept, grad):
    return (grad,)

def back_keep(v):
    return (v, None)

def back_low(kept, grad):
    return (low(grad),)
low.defvjp(low_keep, low_pass)
low_back.defvjp(back_keep, back_low)

def round_both(value):
    return low(low_back(value))

def layer_norm(values, gain, bias):
    center = values - lax.optimization_barrier(jnp.mean(values, axis=-1, keepdims=True))
    return center * lax.rsqrt(lax.optimization_barrier(jnp.mean(center * center, axis=-1, keepdims=True)) + EPS) * gain + bias

def table_forward(features, feat_live, ctx_live, qry_live, params):
    w_emb, ln1_gain, ln1_bias, w_qkv, w_out, ln2_gain, ln2_bias, w_up, b_up, w_down = params
    local_rows = CTX + QRY
    slot_mask = (jnp.arange(F) < feat_live).astype(jnp.float32)
    masked = (features * slot_mask[:, None]).T
    embed = low_back(jnp.dot(masked, w_emb, precision=HIGH))
    valid = jnp.concatenate([jnp.arange(CTX) < ctx_live, jnp.arange(QRY) < qry_live]).astype(jnp.float32)[:, None]
    attn_in = low(layer_norm(embed, ln1_gain, ln1_bias))
    projected = jnp.dot(attn_in, w_qkv, precision=HIGH)
    queries = round_both(projected[:, :D]).reshape(local_rows, HEADS, HEAD_DIM)
    key_heads = round_both(projected[:CTX, D:2 * D]).reshape(CTX, HEADS, HEAD_DIM)
    value_heads = round_both(projected[:CTX, 2 * D:]).reshape(CTX, HEADS, HEAD_DIM)
    scores = jnp.einsum('rhe,khe->hrk', queries, key_heads, precision=HIGH) * HEAD_DIM ** (-0.5)
    key_mask = (jnp.arange(CTX) < ctx_live)[None, None, :]
    scores = low_back(jnp.where(key_mask, scores, NEGATIVE))
    softened = low(jax.nn.softmax(scores, axis=-1))
    attended = jnp.einsum('hrk,khe->rhe', softened, value_heads, precision=HIGH).reshape(local_rows, D)
    attended = round_both(attended)
    branch = low_back(jnp.dot(attended, w_out, precision=HIGH))
    mixed = embed + branch
    mlp_in = low(layer_norm(mixed, ln2_gain, ln2_bias))
    hidden = low_back(jnp.dot(mlp_in, w_up, precision=HIGH) + b_up)
    active = low(jax.nn.gelu(hidden, approximate=False))
    mlp = low_back(jnp.dot(active, w_down, precision=HIGH))
    output = (mixed + mlp) * valid
    squares = jnp.stack([jnp.sum(valid * embed * embed), jnp.sum(valid * branch * branch), jnp.sum(valid * mlp * mlp), jnp.sum(valid * output * output)])
    return (output, squares, jnp.sum(valid))

def reference(ctx_feat, qry_feat, feat_count, ctx_count, qry_count, w_emb, ln1_gain, ln1_bias, w_qkv, w_out, ln2_gain, ln2_bias, w_up, b_up, w_down, ctx_cot, qry_cot):
    features = jnp.concatenate([ctx_feat, qry_feat], axis=2).astype(jnp.float32)
    params = tuple((weight.astype(jnp.float32) for weight in (w_emb, ln1_gain, ln1_bias, w_qkv, w_out, ln2_gain, ln2_bias, w_up, b_up, w_down)))

    def layer_all(features, params):

        def per_table(entry):
            table_feats, feat_live, ctx_live, qry_live = entry
            return table_forward(table_feats, feat_live, ctx_live, qry_live, params)
        outputs, squares, live_rows = lax.map(jax.checkpoint(per_table), (features, feat_count, ctx_count, qry_count))
        return (outputs, lax.optimization_barrier(jnp.sum(squares, axis=0)), jnp.sum(live_rows))
    (outputs, squares, live_rows), pullback = jax.vjp(layer_all, features, params)
    cotangent = jnp.concatenate([ctx_cot, qry_cot], axis=1).astype(jnp.float32)
    grad_features, grads = pullback((cotangent, jnp.zeros_like(squares), jnp.zeros_like(live_rows)))
    rms = jnp.sqrt(squares / (live_rows * D))
    return (outputs[:, :CTX].astype(jnp.bfloat16), outputs[:, CTX:].astype(jnp.bfloat16), grad_features[:, :, :CTX].astype(jnp.bfloat16), grad_features[:, :, CTX:].astype(jnp.bfloat16), grads[0], grads[1], grads[2], grads[3], grads[4], grads[5], grads[6], grads[7], grads[8], grads[9], rms)
```

```python
import functools
import math

import jax
import jax.numpy as jnp
from jax import lax
from jax.experimental import pallas as pl
from jax.experimental.pallas import tpu as pltpu
from jax.sharding import PartitionSpec as P

HEAD_DIM = 64


EPS = 1e-05
NEGATIVE = -1e30


def standardize(values):
    center = values - jnp.mean(values, axis=-1, keepdims=True)
    inverse = lax.rsqrt(jnp.mean(center * center, axis=-1, keepdims=True) + EPS)
    return (center * inverse, inverse)


def norm_back(grad_out, normed, inverse, gain):
    scaled = grad_out * gain
    inner = (
        scaled
        - jnp.mean(scaled, axis=-1, keepdims=True)
        - normed * jnp.mean(scaled * normed, axis=-1, keepdims=True)
    )
    grad_gain = jnp.sum(grad_out * normed, axis=(0, 1))
    grad_bias = jnp.sum(grad_out, axis=(0, 1))
    return (inverse * inner, grad_gain, grad_bias)


def gelu_exact(values):
    return jax.nn.gelu(values, approximate=False)


def block_scores(query_heads, key_rows, block_index, block_width, key_count, score_scale):
    table_count, local_rows, head_count, head_size = query_heads.shape
    dmodel = head_count * head_size
    block = lax.dynamic_slice_in_dim(key_rows, block_index * block_width, block_width, 1)
    key_block = block[..., :dmodel].reshape(table_count, block_width, head_count, head_size)
    value_block = block[..., dmodel:].reshape(table_count, block_width, head_count, head_size)
    scores = (
        jnp.einsum("trhe,tkhe->thrk", query_heads, key_block, preferred_element_type=jnp.float32)
        * score_scale
    )
    position = block_index * block_width + jnp.arange(block_width)
    live_keys = position[None, :] < key_count[:, None]
    scores = jnp.where(live_keys[:, None, None, :], scores, NEGATIVE)
    return (scores, key_block, value_block)


def local_by_rows(
    ctx_feat,
    qry_feat,
    feat_count,
    ctx_count,
    qry_count,
    w_emb,
    ln1_gain,
    ln1_bias,
    w_qkv,
    w_out,
    ln2_gain,
    ln2_bias,
    w_up,
    b_up,
    w_down,
    ctx_cot,
    qry_cot,
):
    table_count, slot_count, ctx_rows = ctx_feat.shape
    qry_rows = qry_feat.shape[2]
    local_rows = ctx_rows + qry_rows
    dmodel = w_out.shape[0]
    head_count = dmodel // HEAD_DIM
    score_scale = HEAD_DIM ** (-0.5)
    total_ctx = ctx_rows * lax.axis_size("row")
    row_index = lax.axis_index("row")
    slot_live = (jnp.arange(slot_count)[None, :] < feat_count[:, None]).astype(jnp.bfloat16)
    features = jnp.concatenate([ctx_feat, qry_feat], axis=2) * slot_live[:, :, None]
    ctx_live = (row_index * ctx_rows + jnp.arange(ctx_rows))[None, :] < ctx_count[:, None]
    qry_live = (row_index * qry_rows + jnp.arange(qry_rows))[None, :] < qry_count[:, None]
    valid = jnp.concatenate([ctx_live, qry_live], axis=1).astype(jnp.float32)[..., None]
    embed = jnp.einsum("tfr,fd->trd", features, w_emb, preferred_element_type=jnp.float32)
    normed1, inverse1 = standardize(embed)
    attn_in = (normed1 * ln1_gain + ln1_bias).astype(jnp.bfloat16)
    w_query = w_qkv[:, :dmodel]
    w_pair = w_qkv[:, dmodel:]
    query = jnp.einsum("trd,de->tre", attn_in, w_query, preferred_element_type=jnp.float32).astype(
        jnp.bfloat16
    )
    pairs = jnp.einsum(
        "trd,de->tre", attn_in[:, :ctx_rows], w_pair, preferred_element_type=jnp.float32
    ).astype(jnp.bfloat16)
    gathered = lax.all_gather(pairs, "row", axis=1, tiled=True)
    block_width = math.gcd(total_ctx, 512)
    block_total = total_ctx // block_width
    query_heads = query.reshape(table_count, local_rows, head_count, HEAD_DIM)

    def attend_step(carried, block_index):
        running_max, running_sum, summed = carried
        scores, _, value_block = block_scores(
            query_heads, gathered, block_index, block_width, ctx_count, score_scale
        )
        new_max = jnp.maximum(running_max, jnp.max(scores, axis=-1))
        factor = jnp.exp(running_max - new_max)
        weights = jnp.exp(scores - new_max[..., None])
        running_sum = running_sum * factor + jnp.sum(weights, axis=-1)
        summed = summed * jnp.transpose(factor, (0, 2, 1))[..., None] + jnp.einsum(
            "thrk,tkhe->trhe",
            weights.astype(jnp.bfloat16),
            value_block,
            preferred_element_type=jnp.float32,
        )
        return ((new_max, running_sum, summed), None)

    initial = jnp.full((table_count, head_count, local_rows), NEGATIVE, jnp.float32)
    start_sum = jnp.zeros((table_count, local_rows, head_count, HEAD_DIM), jnp.float32)
    (running_max, running_sum, summed), _ = lax.scan(
        attend_step, (initial, jnp.zeros_like(initial), start_sum), jnp.arange(block_total)
    )
    log_total = running_max + jnp.log(running_sum)
    attended = summed / jnp.transpose(running_sum, (0, 2, 1))[..., None]
    attn_low = attended.reshape(table_count, local_rows, dmodel).astype(jnp.bfloat16)
    branch = jnp.einsum("trd,de->tre", attn_low, w_out, preferred_element_type=jnp.float32)
    mixed = embed + branch
    normed2, inverse2 = standardize(mixed)
    mlp_in = (normed2 * ln2_gain + ln2_bias).astype(jnp.bfloat16)
    hidden = jnp.einsum("trd,de->tre", mlp_in, w_up, preferred_element_type=jnp.float32) + b_up
    activation, gelu_back = jax.vjp(gelu_exact, hidden)
    act_low = activation.astype(jnp.bfloat16)
    mlp = jnp.einsum("tre,ed->trd", act_low, w_down, preferred_element_type=jnp.float32)
    output = (mixed + mlp) * valid
    ctx_out = output[:, :ctx_rows].astype(jnp.bfloat16)
    qry_out = output[:, ctx_rows:].astype(jnp.bfloat16)
    squares = jnp.stack(
        [
            jnp.sum(valid * embed * embed),
            jnp.sum(valid * branch * branch),
            jnp.sum(valid * mlp * mlp),
            jnp.sum(valid * output * output),
        ]
    )
    live_rows = jnp.sum(valid)
    cotangent = jnp.concatenate([ctx_cot, qry_cot], axis=1)
    d_mlp = cotangent * valid.astype(jnp.bfloat16)
    grad_w_down = jnp.einsum("tre,trd->ed", act_low, d_mlp, preferred_element_type=jnp.float32)
    d_act = jnp.einsum("trd,ed->tre", d_mlp, w_down, preferred_element_type=jnp.float32)
    d_hidden = gelu_back(d_act)[0].astype(jnp.bfloat16)
    grad_b_up = jnp.sum(d_hidden.astype(jnp.float32), axis=(0, 1))
    grad_w_up = jnp.einsum("trd,tre->de", mlp_in, d_hidden, preferred_element_type=jnp.float32)
    d_mlp_in = jnp.einsum("tre,de->trd", d_hidden, w_up, preferred_element_type=jnp.float32)
    d_norm2, grad_ln2_gain, grad_ln2_bias = norm_back(d_mlp_in, normed2, inverse2, ln2_gain)
    d_mixed = d_mlp.astype(jnp.float32) + d_norm2
    d_branch = d_mixed.astype(jnp.bfloat16)
    grad_w_out = jnp.einsum("trd,tre->de", attn_low, d_branch, preferred_element_type=jnp.float32)
    d_attn = jnp.einsum("tre,de->trd", d_branch, w_out, preferred_element_type=jnp.float32).astype(
        jnp.bfloat16
    )
    d_attn_heads = d_attn.reshape(table_count, local_rows, head_count, HEAD_DIM)
    dots_rows = jnp.sum(d_attn_heads.astype(jnp.float32) * attended, axis=-1)
    row_dots = jnp.transpose(dots_rows, (0, 2, 1))

    def query_part(block_index):
        scores, key_block, value_block = block_scores(
            query_heads, gathered, block_index, block_width, ctx_count, score_scale
        )
        softened = jnp.exp(scores - log_total[..., None])
        d_soft = jnp.einsum(
            "trhe,tkhe->thrk", d_attn_heads, value_block, preferred_element_type=jnp.float32
        )
        d_scores = (softened * (d_soft - row_dots[..., None])).astype(jnp.bfloat16)
        d_part = (
            jnp.einsum("thrk,tkhe->trhe", d_scores, key_block, preferred_element_type=jnp.float32)
            * score_scale
        )
        return (softened, d_scores, d_part)

    start_query = jnp.zeros((table_count, local_rows, head_count, HEAD_DIM), jnp.float32)

    def grad_step(carried, block_index):
        d_query, d_pairs = carried
        softened, d_scores, d_part = query_part(block_index)
        d_values = jnp.einsum(
            "thrk,trhe->tkhe",
            softened.astype(jnp.bfloat16),
            d_attn_heads,
            preferred_element_type=jnp.float32,
        )
        d_keys = (
            jnp.einsum("thrk,trhe->tkhe", d_scores, query_heads, preferred_element_type=jnp.float32)
            * score_scale
        )
        grad_block = jnp.concatenate(
            [
                d_keys.reshape(table_count, block_width, dmodel),
                d_values.reshape(table_count, block_width, dmodel),
            ],
            axis=-1,
        )
        d_pairs = lax.dynamic_update_slice_in_dim(d_pairs, grad_block, block_index * block_width, 1)
        return ((d_query + d_part, d_pairs), None)

    start_pairs = jnp.zeros((table_count, total_ctx, 2 * dmodel), jnp.float32)
    (d_query, d_pairs), _ = lax.scan(grad_step, (start_query, start_pairs), jnp.arange(block_total))
    own_pairs = lax.psum_scatter(d_pairs, "row", scatter_dimension=1, tiled=True).astype(
        jnp.bfloat16
    )
    d_q = d_query.reshape(table_count, local_rows, dmodel).astype(jnp.bfloat16)
    grad_w_qkv = jnp.concatenate(
        [
            jnp.einsum("trd,tre->de", attn_in, d_q, preferred_element_type=jnp.float32),
            jnp.einsum(
                "trd,tre->de", attn_in[:, :ctx_rows], own_pairs, preferred_element_type=jnp.float32
            ),
        ],
        axis=1,
    )
    d_from_query = jnp.einsum("tre,de->trd", d_q, w_query, preferred_element_type=jnp.float32)
    d_from_pairs = jnp.einsum("tre,de->trd", own_pairs, w_pair, preferred_element_type=jnp.float32)
    d_attn_in = jnp.concatenate(
        [d_from_query[:, :ctx_rows] + d_from_pairs, d_from_query[:, ctx_rows:]], axis=1
    )
    d_norm1, grad_ln1_gain, grad_ln1_bias = norm_back(d_attn_in, normed1, inverse1, ln1_gain)
    d_embed = (d_mixed + d_norm1).astype(jnp.bfloat16)
    grad_w_emb = jnp.einsum("tfr,trd->fd", features, d_embed, preferred_element_type=jnp.float32)
    d_features = jnp.einsum("trd,fd->tfr", d_embed, w_emb, preferred_element_type=jnp.float32)
    d_features = (d_features * slot_live[:, :, None].astype(jnp.float32)).astype(jnp.bfloat16)
    ctx_feat_grad = d_features[:, :, :ctx_rows]
    qry_feat_grad = d_features[:, :, ctx_rows:]
    (
        qkv_part,
        out_part,
        up_part,
        down_part,
        gain1_part,
        bias1_part,
        gain2_part,
        bias2_part,
        upbias_part,
    ) = (
        lax.psum_scatter(grad_w_qkv, "row", scatter_dimension=0, tiled=True),
        lax.psum_scatter(grad_w_out, "row", scatter_dimension=0, tiled=True),
        lax.psum_scatter(grad_w_up, "row", scatter_dimension=0, tiled=True),
        lax.psum_scatter(grad_w_down, "row", scatter_dimension=0, tiled=True),
        lax.psum_scatter(grad_ln1_gain, "row", scatter_dimension=0, tiled=True),
        lax.psum_scatter(grad_ln1_bias, "row", scatter_dimension=0, tiled=True),
        lax.psum_scatter(grad_ln2_gain, "row", scatter_dimension=0, tiled=True),
        lax.psum_scatter(grad_ln2_bias, "row", scatter_dimension=0, tiled=True),
        lax.psum_scatter(grad_b_up, "row", scatter_dimension=0, tiled=True),
    )
    qkv_all, out_all, up_all, down_all, gain1_all, bias1_all, gain2_all, bias2_all, upbias_all = (
        lax.psum(qkv_part.astype(jnp.bfloat16), "tab").astype(jnp.float32),
        lax.psum(out_part.astype(jnp.bfloat16), "tab").astype(jnp.float32),
        lax.psum(up_part.astype(jnp.bfloat16), "tab").astype(jnp.float32),
        lax.psum(down_part.astype(jnp.bfloat16), "tab").astype(jnp.float32),
        lax.psum(gain1_part.astype(jnp.bfloat16), "tab").astype(jnp.float32),
        lax.psum(bias1_part.astype(jnp.bfloat16), "tab").astype(jnp.float32),
        lax.psum(gain2_part.astype(jnp.bfloat16), "tab").astype(jnp.float32),
        lax.psum(bias2_part.astype(jnp.bfloat16), "tab").astype(jnp.float32),
        lax.psum(upbias_part.astype(jnp.bfloat16), "tab").astype(jnp.float32),
    )
    embed_all, squares_all, count_all = lax.psum((grad_w_emb, squares, live_rows), ("tab", "row"))
    rms = jnp.sqrt(squares_all / (count_all * dmodel))
    return (
        ctx_out,
        qry_out,
        ctx_feat_grad,
        qry_feat_grad,
        embed_all,
        gain1_all,
        bias1_all,
        qkv_all,
        out_all,
        gain2_all,
        bias2_all,
        up_all,
        upbias_all,
        down_all,
        rms,
    )


MESH = pl.DeviceIdType.MESH
LANES = 128
NT = (((1,), (1,)), ((), ()))


def swap_rows(values, pick, collective_id):
    row_size = lax.axis_size("row")
    block = values.shape[1:]

    def kernel(src, dst, own_sem, send_sem, recv_sem):
        tab, row = lax.axis_index("tab"), lax.axis_index("row")
        barrier = pltpu.get_barrier_semaphore()
        peers = [(tab, lax.rem(row + k, row_size)) for k in range(1, row_size)]
        for peer in peers:
            pl.semaphore_signal(barrier, inc=1, device_id=peer, device_id_type=MESH)
        pl.semaphore_wait(barrier, row_size - 1)
        copies = []
        for k, peer in enumerate(peers):
            copy = pltpu.make_async_remote_copy(
                src_ref=src.at[pick(peer[1])],
                dst_ref=dst.at[row],
                send_sem=send_sem.at[k],
                recv_sem=recv_sem.at[k],
                device_id=peer,
                device_id_type=MESH,
            )
            copy.start()
            copies.append(copy)
        own = pltpu.make_async_copy(src.at[pick(row)], dst.at[row], own_sem)
        own.start()
        own.wait()
        for copy in copies:
            copy.wait()

    return pl.pallas_call(
        kernel,
        out_shape=jax.ShapeDtypeStruct((row_size,) + block, values.dtype),
        in_specs=[pl.BlockSpec(memory_space=pl.ANY)],
        out_specs=pl.BlockSpec(memory_space=pl.ANY),
        scratch_shapes=[
            pltpu.SemaphoreType.DMA,
            pltpu.SemaphoreType.DMA((row_size - 1,)),
            pltpu.SemaphoreType.DMA((row_size - 1,)),
        ],
        compiler_params=pltpu.CompilerParams(collective_id=collective_id, has_side_effects=True),
        name="swap_rows",
    )(values)


def pack_heads(values):
    rows, width = values.shape[-2:]
    whole = width // LANES
    parts = [values[..., i * LANES : (i + 1) * LANES] for i in range(whole)]
    if width % LANES:
        last = values[..., whole * LANES :]
        parts.append(jnp.concatenate([last[..., : rows // 2, :], last[..., rows // 2 :, :]], axis=-1))
    return jnp.concatenate(parts, axis=-2)


def unpack_heads(packed, rows, width):
    whole = width // LANES
    parts = [packed[..., i * rows : (i + 1) * rows, :] for i in range(whole)]
    if width % LANES:
        last = packed[..., whole * rows :, :]
        parts.append(jnp.concatenate([last[..., :HEAD_DIM], last[..., HEAD_DIM:]], axis=-2))
    return jnp.concatenate(parts, axis=-1)


def lane_of(shape):
    return lax.broadcasted_iota(jnp.int32, shape, len(shape) - 1)


def split_three(values):
    high = values.astype(jnp.bfloat16)
    rest = values - high.astype(jnp.float32)
    mid = rest.astype(jnp.bfloat16)
    tail = (rest - mid.astype(jnp.float32)).astype(jnp.bfloat16)
    return (high, mid, tail)


def set_lanes(values, first, columns):
    lane = lane_of(values.shape)
    values = values.astype(jnp.float32)
    for i, column in enumerate(columns):
        values = jnp.where(lane == first + i, column.astype(jnp.float32), values)
    return values.astype(jnp.bfloat16)


def attend_kernel(q_ref, k_ref, v_ref, out_ref, back_ref):
    scores = lax.dot_general(q_ref[0], k_ref[0], NT, preferred_element_type=jnp.float32)
    top = jnp.max(scores, axis=-1, keepdims=True)
    weights = jnp.exp(scores - top).astype(jnp.bfloat16)
    summed = jnp.dot(weights, v_ref[0], preferred_element_type=jnp.float32)
    total = summed[:, HEAD_DIM : HEAD_DIM + 1]
    out_ref[0] = (summed / total).astype(jnp.bfloat16)
    log_total = top + jnp.log(total)
    back_ref[0] = set_lanes(q_ref[0], HEAD_DIM + 1, split_three(-log_total))


def attend(queries, keys, values, block):
    heads, rows, _ = queries.shape
    total = keys.shape[1]
    by_query = pl.BlockSpec((1, block, LANES), lambda h, i: (h, i, 0))
    by_key = pl.BlockSpec((1, total, LANES), lambda h, i: (h, 0, 0))
    return pl.pallas_call(
        attend_kernel,
        grid=(heads, rows // block),
        in_specs=[by_query, by_key, by_key],
        out_specs=[by_query, by_query],
        out_shape=[jax.ShapeDtypeStruct((heads, rows, LANES), jnp.bfloat16)] * 2,
        compiler_params=pltpu.CompilerParams(vmem_limit_bytes=48 * 2**20),
        name="attend",
    )(queries, keys, values)


def attend_back_kernel(chunk, q_ref, k_ref, kt_ref, v_ref, o_ref, g_ref, dq_ref, dk_ref, dv_ref, dk_sum, dv_sum):
    step = pl.program_id(1)

    @pl.when(step == 0)
    def _():
        dk_sum[...] = jnp.zeros_like(dk_sum)
        dv_sum[...] = jnp.zeros_like(dv_sum)

    query, grad = q_ref[0], g_ref[0]
    inner = jnp.sum(
        jnp.where(lane_of(grad.shape) < HEAD_DIM, grad.astype(jnp.float32) * o_ref[0].astype(jnp.float32), 0.0),
        axis=-1,
        keepdims=True,
    )
    grad = set_lanes(grad, HEAD_DIM, split_three(-inner))
    total = k_ref.shape[1]
    d_query = jnp.zeros((HEAD_DIM, query.shape[0]), jnp.float32)
    for i in range(total // chunk):
        at = pl.ds(i * chunk, chunk)
        scores = lax.dot_general(k_ref[0, at], query, NT, preferred_element_type=jnp.float32)
        probs = jnp.exp(scores)
        d_probs = lax.dot_general(v_ref[0, at], grad, NT, preferred_element_type=jnp.float32)
        d_scores = (probs * d_probs).astype(jnp.bfloat16)
        dv_sum[at] += jnp.dot(probs.astype(jnp.bfloat16), grad, preferred_element_type=jnp.float32)
        dk_sum[at] += jnp.dot(d_scores, query, preferred_element_type=jnp.float32)
        d_query += jnp.dot(kt_ref[0, :, at], d_scores, preferred_element_type=jnp.float32)
    dq_ref[0] = (d_query * HEAD_DIM ** (-0.5)).T.astype(jnp.bfloat16)

    @pl.when(step == pl.num_programs(1) - 1)
    def _():
        dk_ref[0] = dk_sum[:, :HEAD_DIM].astype(jnp.bfloat16)
        dv_ref[0] = dv_sum[:, :HEAD_DIM].astype(jnp.bfloat16)


def attend_back(queries, keys, keys_t, values, outs, grads, block, chunk):
    heads, rows, _ = queries.shape
    total = keys.shape[1]
    by_query = pl.BlockSpec((1, block, LANES), lambda h, i: (h, i, 0))
    by_key = pl.BlockSpec((1, total, LANES), lambda h, i: (h, 0, 0))
    return pl.pallas_call(
        functools.partial(attend_back_kernel, chunk),
        grid=(heads, rows // block),
        in_specs=[
            by_query,
            by_key,
            pl.BlockSpec((1, HEAD_DIM, total), lambda h, i: (h, 0, 0)),
            by_key,
            by_query,
            by_query,
        ],
        out_specs=[
            pl.BlockSpec((1, block, HEAD_DIM), lambda h, i: (h, i, 0)),
            pl.BlockSpec((1, total, HEAD_DIM), lambda h, i: (h, 0, 0)),
            pl.BlockSpec((1, total, HEAD_DIM), lambda h, i: (h, 0, 0)),
        ],
        out_shape=[
            jax.ShapeDtypeStruct((heads, rows, HEAD_DIM), jnp.bfloat16),
            jax.ShapeDtypeStruct((heads, total, HEAD_DIM), jnp.bfloat16),
            jax.ShapeDtypeStruct((heads, total, HEAD_DIM), jnp.bfloat16),
        ],
        scratch_shapes=[pltpu.VMEM((total, LANES), jnp.float32)] * 2,
        compiler_params=pltpu.CompilerParams(vmem_limit_bytes=48 * 2**20),
        name="attend_back",
    )(queries, keys, keys_t, values, outs, grads)


def add_over_tab(part):
    return lax.psum(part.astype(jnp.bfloat16), "tab").astype(jnp.float32)


def scatter_add(grad):
    part = lax.psum_scatter(grad.astype(jnp.bfloat16), "row", scatter_dimension=0, tiled=True)
    return add_over_tab(part)


def local_by_heads(
    ctx_feat,
    qry_feat,
    feat_count,
    ctx_count,
    qry_count,
    w_emb,
    ln1_gain,
    ln1_bias,
    w_qkv,
    w_out,
    ln2_gain,
    ln2_bias,
    w_up,
    b_up,
    w_down,
    ctx_cot,
    qry_cot,
):
    table_count, slot_count, ctx_rows = ctx_feat.shape
    qry_rows = qry_feat.shape[2]
    local_rows = ctx_rows + qry_rows
    dmodel = w_out.shape[0]
    head_count = dmodel // HEAD_DIM
    score_scale = HEAD_DIM ** (-0.5)
    row_size = lax.axis_size("row")
    total_ctx = ctx_rows * row_size
    all_rows = local_rows * row_size
    row_index = lax.axis_index("row")
    groups = row_size // table_count
    heads = head_count // groups
    width = heads * HEAD_DIM
    table, group = row_index // groups, row_index % groups

    slot_live = (jnp.arange(slot_count)[None, :] < feat_count[:, None]).astype(jnp.bfloat16)
    features = jnp.concatenate([ctx_feat, qry_feat], axis=2) * slot_live[:, :, None]
    by_row = jnp.pad(jnp.transpose(features, (0, 2, 1)), ((0, 0), (0, 0), (0, LANES - slot_count)))
    w_emb_pad = jnp.pad(w_emb, ((0, LANES - slot_count), (0, 0)))
    ctx_live = (row_index * ctx_rows + jnp.arange(ctx_rows))[None, :] < ctx_count[:, None]
    qry_live = (row_index * qry_rows + jnp.arange(qry_rows))[None, :] < qry_count[:, None]
    valid = jnp.concatenate([ctx_live, qry_live], axis=1).astype(jnp.float32)[..., None]

    table_feat = swap_rows(by_row, lambda p: p // groups, 0)
    table_embed = jnp.einsum("prf,fd->prd", table_feat, w_emb_pad, preferred_element_type=jnp.float32)
    normed1, inverse1 = standardize(table_embed)
    attn_in = (normed1 * ln1_gain + ln1_bias).astype(jnp.bfloat16)
    w_three = w_qkv.reshape(dmodel, 3, head_count, HEAD_DIM)
    w_three = lax.dynamic_slice_in_dim(w_three, group * heads, heads, 2)
    w_lanes = jnp.pad(w_three, ((0, 0), (0, 0), (0, 0), (0, LANES - HEAD_DIM)))
    projected = jnp.einsum("prd,dnhe->nhpre", attn_in, w_lanes, preferred_element_type=jnp.float32)
    lane = jnp.arange(LANES)
    my_count = lax.dynamic_index_in_dim(ctx_count, table, 0, keepdims=False)
    live_keys = (jnp.arange(total_ctx) < my_count).reshape(row_size, ctx_rows)
    bias = jnp.where(live_keys, 0.0, NEGATIVE)[None, :, :, None]
    queries = jnp.where(lane == HEAD_DIM, 1.0, projected[0] * score_scale).astype(jnp.bfloat16)
    queries = queries.reshape(heads, all_rows, LANES)
    keys = jnp.where(lane == HEAD_DIM, bias, projected[1][:, :, :ctx_rows])
    keys = jnp.where((lane > HEAD_DIM) & (lane < HEAD_DIM + 4), 1.0, keys).astype(jnp.bfloat16)
    keys = keys.reshape(heads, total_ctx, LANES)
    values = jnp.where((lane >= HEAD_DIM) & (lane < HEAD_DIM + 3), 1.0, projected[2][:, :, :ctx_rows])
    values = values.astype(jnp.bfloat16).reshape(heads, total_ctx, LANES)
    outs, back_queries = attend(queries, keys, values, math.gcd(all_rows, 512))

    def to_rows(by_head):
        wide = jnp.transpose(by_head[..., :HEAD_DIM], (1, 0, 2)).reshape(row_size, local_rows, width)
        return swap_rows(pack_heads(wide), lambda p: p, 1)

    packed = to_rows(outs)
    attn_low = unpack_heads(packed, local_rows, width).reshape(table_count, groups, local_rows, width)
    attn_low = jnp.transpose(attn_low, (0, 2, 1, 3)).reshape(table_count, local_rows, dmodel)

    embed = jnp.einsum("trf,fd->trd", by_row, w_emb_pad, preferred_element_type=jnp.float32)
    branch = jnp.einsum("trd,de->tre", attn_low, w_out, preferred_element_type=jnp.float32)
    mixed = embed + branch
    normed2, inverse2 = standardize(mixed)
    mlp_in = (normed2 * ln2_gain + ln2_bias).astype(jnp.bfloat16)
    hidden = jnp.einsum("trd,de->tre", mlp_in, w_up, preferred_element_type=jnp.float32) + b_up
    activation, gelu_back = jax.vjp(gelu_exact, hidden)
    act_low = activation.astype(jnp.bfloat16)
    mlp = jnp.einsum("tre,ed->trd", act_low, w_down, preferred_element_type=jnp.float32)
    output = (mixed + mlp) * valid
    ctx_out = output[:, :ctx_rows].astype(jnp.bfloat16)
    qry_out = output[:, ctx_rows:].astype(jnp.bfloat16)
    squares = jnp.stack(
        [
            jnp.sum(valid * embed * embed),
            jnp.sum(valid * branch * branch),
            jnp.sum(valid * mlp * mlp),
            jnp.sum(valid * output * output),
        ]
    )
    live_rows = jnp.sum(valid)
    cotangent = jnp.concatenate([ctx_cot, qry_cot], axis=1)
    d_mlp = cotangent * valid.astype(jnp.bfloat16)
    grad_w_down = jnp.einsum("tre,trd->ed", act_low, d_mlp, preferred_element_type=jnp.float32)
    d_act = jnp.einsum("trd,ed->tre", d_mlp, w_down, preferred_element_type=jnp.float32)
    d_hidden = gelu_back(d_act)[0].astype(jnp.bfloat16)
    grad_b_up = jnp.sum(d_hidden.astype(jnp.float32), axis=(0, 1))
    grad_w_up = jnp.einsum("trd,tre->de", mlp_in, d_hidden, preferred_element_type=jnp.float32)
    d_mlp_in = jnp.einsum("tre,de->trd", d_hidden, w_up, preferred_element_type=jnp.float32)
    d_norm2, grad_ln2_gain, grad_ln2_bias = norm_back(d_mlp_in, normed2, inverse2, ln2_gain)
    d_mixed = d_mlp.astype(jnp.float32) + d_norm2
    d_branch = d_mixed.astype(jnp.bfloat16)
    grad_w_out = jnp.einsum("trd,tre->de", attn_low, d_branch, preferred_element_type=jnp.float32)
    d_attn = jnp.einsum("tre,de->trd", d_branch, w_out, preferred_element_type=jnp.float32).astype(
        jnp.bfloat16
    )

    d_attn = jnp.transpose(d_attn.reshape(table_count, local_rows, groups, width), (0, 2, 1, 3))
    d_attn = d_attn.reshape(row_size, local_rows, width)
    d_outs = unpack_heads(swap_rows(pack_heads(d_attn), lambda p: p, 2), local_rows, width)
    d_outs = jnp.transpose(d_outs.reshape(all_rows, heads, HEAD_DIM), (1, 0, 2))
    d_outs = jnp.pad(d_outs, ((0, 0), (0, 0), (0, LANES - HEAD_DIM)))
    keys_t = jnp.transpose(keys[..., :HEAD_DIM], (0, 2, 1))
    d_q, d_k, d_v = attend_back(
        back_queries, keys, keys_t, values, outs, d_outs, math.gcd(all_rows, 512), math.gcd(total_ctx, 512)
    )
    d_q = d_q.reshape(heads, row_size, local_rows, HEAD_DIM)
    d_k = d_k.reshape(heads, row_size, ctx_rows, HEAD_DIM)
    d_v = d_v.reshape(heads, row_size, ctx_rows, HEAD_DIM)
    over_qry = ((0, 0), (0, 0), (0, qry_rows), (0, 0))
    d_three = jnp.stack([d_q, jnp.pad(d_k, over_qry), jnp.pad(d_v, over_qry)])
    d_three = jnp.transpose(d_three, (2, 3, 0, 1, 4)).reshape(row_size, local_rows, 3 * width)
    w_mine = w_three.reshape(dmodel, 3 * width)
    grad_mine = jnp.einsum("prd,pre->de", attn_in, d_three, preferred_element_type=jnp.float32)
    d_attn_in = jnp.einsum("pre,de->prd", d_three, w_mine, preferred_element_type=jnp.float32)
    d_norm1, grad_ln1_gain, grad_ln1_bias = norm_back(d_attn_in, normed1, inverse1, ln1_gain)
    d_norm1 = d_norm1.astype(jnp.bfloat16)
    grad_w_emb = jnp.einsum("prf,prd->fd", table_feat, d_norm1, preferred_element_type=jnp.float32)
    grad_w_emb += jnp.einsum("trf,trd->fd", by_row, d_branch, preferred_element_type=jnp.float32)
    grad_w_emb = grad_w_emb[:slot_count]
    feat_terms = jnp.einsum("prd,fd->prf", d_norm1, w_emb_pad, preferred_element_type=jnp.float32)
    feat_terms = swap_rows(feat_terms.astype(jnp.bfloat16), lambda p: p, 3)
    feat_terms = feat_terms.reshape(table_count, groups, local_rows, LANES).astype(jnp.float32)
    own_term = jnp.einsum("trd,fd->trf", d_branch, w_emb_pad, preferred_element_type=jnp.float32)
    d_features = jnp.transpose(own_term + jnp.sum(feat_terms, axis=1), (0, 2, 1))[:, :slot_count]
    d_features = (d_features * slot_live[:, :, None].astype(jnp.float32)).astype(jnp.bfloat16)
    ctx_feat_grad = d_features[:, :, :ctx_rows]
    qry_feat_grad = d_features[:, :, ctx_rows:]

    shard = dmodel // row_size
    mine = swap_rows(grad_mine.astype(jnp.bfloat16).reshape(row_size, shard, 3 * width), lambda p: p, 4)
    mine = jnp.sum(mine.astype(jnp.float32).reshape(table_count, groups, shard, 3, width), axis=0)
    qkv_all = add_over_tab(jnp.transpose(mine, (1, 2, 0, 3)).reshape(shard, 3 * dmodel))
    out_all = scatter_add(grad_w_out)
    up_all = scatter_add(grad_w_up)
    down_all = scatter_add(grad_w_down)
    vectors = (grad_ln1_gain, grad_ln1_bias, grad_ln2_gain, grad_ln2_bias, grad_b_up)
    grad_w_emb, squares, live_rows, vectors = lax.psum(
        (grad_w_emb, squares, live_rows, vectors), ("tab", "row")
    )
    own_parts = [
        lax.dynamic_slice_in_dim(v, row_index * (v.shape[0] // row_size), v.shape[0] // row_size, 0)
        for v in vectors
    ]
    gain1_all, bias1_all, gain2_all, bias2_all, upbias_all = own_parts
    rms = jnp.sqrt(squares / (live_rows * dmodel))
    return (
        ctx_out,
        qry_out,
        ctx_feat_grad,
        qry_feat_grad,
        grad_w_emb,
        gain1_all,
        bias1_all,
        qkv_all,
        out_all,
        gain2_all,
        bias2_all,
        up_all,
        upbias_all,
        down_all,
        rms,
    )


def local(ctx_feat, qry_feat, *rest):
    table_count, slot_count, ctx_rows = ctx_feat.shape
    qry_rows = qry_feat.shape[2]
    head_count = rest[6].shape[0] // HEAD_DIM
    row_size = lax.axis_size("row")
    even = row_size % table_count == 0 and head_count % (row_size // table_count) == 0
    whole = slot_count <= LANES and ctx_rows % LANES == 0 and qry_rows % 32 == 0
    inner = local_by_heads if even and whole else local_by_rows
    return inner(ctx_feat, qry_feat, *rest)


def solution(mesh):
    in_specs = (
        P("tab", None, "row"),
        P("tab", None, "row"),
        P("tab"),
        P("tab"),
        P("tab"),
        P(),
        P(),
        P(),
        P(),
        P(),
        P(),
        P(),
        P(),
        P(),
        P(),
        P("tab", "row", None),
        P("tab", "row", None),
    )
    out_specs = (
        P("tab", "row", None),
        P("tab", "row", None),
        P("tab", None, "row"),
        P("tab", None, "row"),
        P(),
        P("row"),
        P("row"),
        P("row", None),
        P("row", None),
        P("row"),
        P("row"),
        P("row", None),
        P("row"),
        P("row", None),
        P(),
    )
    return jax.shard_map(local, mesh=mesh, in_specs=in_specs, out_specs=out_specs, check_vma=False)
```

```python
import functools
import math

import jax
import jax.numpy as jnp
from jax import lax
from jax.experimental import pallas as pl
from jax.experimental.pallas import tpu as pltpu
from jax.sharding import PartitionSpec as P

HEAD_DIM = 64


EPS = 1e-05
NEGATIVE = -1e30


def standardize(values):
    center = values - jnp.mean(values, axis=-1, keepdims=True)
    inverse = lax.rsqrt(jnp.mean(center * center, axis=-1, keepdims=True) + EPS)
    return (center * inverse, inverse)


def norm_back(grad_out, normed, inverse, gain):
    scaled = grad_out * gain
    inner = (
        scaled
        - jnp.mean(scaled, axis=-1, keepdims=True)
        - normed * jnp.mean(scaled * normed, axis=-1, keepdims=True)
    )
    grad_gain = jnp.sum(grad_out * normed, axis=(0, 1))
    grad_bias = jnp.sum(grad_out, axis=(0, 1))
    return (inverse * inner, grad_gain, grad_bias)


def gelu_exact(values):
    return jax.nn.gelu(values, approximate=False)


def block_scores(query_heads, key_rows, block_index, block_width, key_count, score_scale):
    table_count, local_rows, head_count, head_size = query_heads.shape
    dmodel = head_count * head_size
    block = lax.dynamic_slice_in_dim(key_rows, block_index * block_width, block_width, 1)
    key_block = block[..., :dmodel].reshape(table_count, block_width, head_count, head_size)
    value_block = block[..., dmodel:].reshape(table_count, block_width, head_count, head_size)
    scores = (
        jnp.einsum("trhe,tkhe->thrk", query_heads, key_block, preferred_element_type=jnp.float32)
        * score_scale
    )
    position = block_index * block_width + jnp.arange(block_width)
    live_keys = position[None, :] < key_count[:, None]
    scores = jnp.where(live_keys[:, None, None, :], scores, NEGATIVE)
    return (scores, key_block, value_block)


def local_by_rows(
    ctx_feat,
    qry_feat,
    feat_count,
    ctx_count,
    qry_count,
    w_emb,
    ln1_gain,
    ln1_bias,
    w_qkv,
    w_out,
    ln2_gain,
    ln2_bias,
    w_up,
    b_up,
    w_down,
    ctx_cot,
    qry_cot,
):
    table_count, slot_count, ctx_rows = ctx_feat.shape
    qry_rows = qry_feat.shape[2]
    local_rows = ctx_rows + qry_rows
    dmodel = w_out.shape[0]
    head_count = dmodel // HEAD_DIM
    score_scale = HEAD_DIM ** (-0.5)
    total_ctx = ctx_rows * lax.axis_size("row")
    row_index = lax.axis_index("row")
    slot_live = (jnp.arange(slot_count)[None, :] < feat_count[:, None]).astype(jnp.bfloat16)
    features = jnp.concatenate([ctx_feat, qry_feat], axis=2) * slot_live[:, :, None]
    ctx_live = (row_index * ctx_rows + jnp.arange(ctx_rows))[None, :] < ctx_count[:, None]
    qry_live = (row_index * qry_rows + jnp.arange(qry_rows))[None, :] < qry_count[:, None]
    valid = jnp.concatenate([ctx_live, qry_live], axis=1).astype(jnp.float32)[..., None]
    embed = jnp.einsum("tfr,fd->trd", features, w_emb, preferred_element_type=jnp.float32)
    normed1, inverse1 = standardize(embed)
    attn_in = (normed1 * ln1_gain + ln1_bias).astype(jnp.bfloat16)
    w_query = w_qkv[:, :dmodel]
    w_pair = w_qkv[:, dmodel:]
    query = jnp.einsum("trd,de->tre", attn_in, w_query, preferred_element_type=jnp.float32).astype(
        jnp.bfloat16
    )
    pairs = jnp.einsum(
        "trd,de->tre", attn_in[:, :ctx_rows], w_pair, preferred_element_type=jnp.float32
    ).astype(jnp.bfloat16)
    gathered = lax.all_gather(pairs, "row", axis=1, tiled=True)
    block_width = math.gcd(total_ctx, 512)
    block_total = total_ctx // block_width
    query_heads = query.reshape(table_count, local_rows, head_count, HEAD_DIM)

    def attend_step(carried, block_index):
        running_max, running_sum, summed = carried
        scores, _, value_block = block_scores(
            query_heads, gathered, block_index, block_width, ctx_count, score_scale
        )
        new_max = jnp.maximum(running_max, jnp.max(scores, axis=-1))
        factor = jnp.exp(running_max - new_max)
        weights = jnp.exp(scores - new_max[..., None])
        running_sum = running_sum * factor + jnp.sum(weights, axis=-1)
        summed = summed * jnp.transpose(factor, (0, 2, 1))[..., None] + jnp.einsum(
            "thrk,tkhe->trhe",
            weights.astype(jnp.bfloat16),
            value_block,
            preferred_element_type=jnp.float32,
        )
        return ((new_max, running_sum, summed), None)

    initial = jnp.full((table_count, head_count, local_rows), NEGATIVE, jnp.float32)
    start_sum = jnp.zeros((table_count, local_rows, head_count, HEAD_DIM), jnp.float32)
    (running_max, running_sum, summed), _ = lax.scan(
        attend_step, (initial, jnp.zeros_like(initial), start_sum), jnp.arange(block_total)
    )
    log_total = running_max + jnp.log(running_sum)
    attended = summed / jnp.transpose(running_sum, (0, 2, 1))[..., None]
    attn_low = attended.reshape(table_count, local_rows, dmodel).astype(jnp.bfloat16)
    branch = jnp.einsum("trd,de->tre", attn_low, w_out, preferred_element_type=jnp.float32)
    mixed = embed + branch
    normed2, inverse2 = standardize(mixed)
    mlp_in = (normed2 * ln2_gain + ln2_bias).astype(jnp.bfloat16)
    hidden = jnp.einsum("trd,de->tre", mlp_in, w_up, preferred_element_type=jnp.float32) + b_up
    activation, gelu_back = jax.vjp(gelu_exact, hidden)
    act_low = activation.astype(jnp.bfloat16)
    mlp = jnp.einsum("tre,ed->trd", act_low, w_down, preferred_element_type=jnp.float32)
    output = (mixed + mlp) * valid
    ctx_out = output[:, :ctx_rows].astype(jnp.bfloat16)
    qry_out = output[:, ctx_rows:].astype(jnp.bfloat16)
    squares = jnp.stack(
        [
            jnp.sum(valid * embed * embed),
            jnp.sum(valid * branch * branch),
            jnp.sum(valid * mlp * mlp),
            jnp.sum(valid * output * output),
        ]
    )
    live_rows = jnp.sum(valid)
    cotangent = jnp.concatenate([ctx_cot, qry_cot], axis=1)
    d_mlp = cotangent * valid.astype(jnp.bfloat16)
    grad_w_down = jnp.einsum("tre,trd->ed", act_low, d_mlp, preferred_element_type=jnp.float32)
    d_act = jnp.einsum("trd,ed->tre", d_mlp, w_down, preferred_element_type=jnp.float32)
    d_hidden = gelu_back(d_act)[0].astype(jnp.bfloat16)
    grad_b_up = jnp.sum(d_hidden.astype(jnp.float32), axis=(0, 1))
    grad_w_up = jnp.einsum("trd,tre->de", mlp_in, d_hidden, preferred_element_type=jnp.float32)
    d_mlp_in = jnp.einsum("tre,de->trd", d_hidden, w_up, preferred_element_type=jnp.float32)
    d_norm2, grad_ln2_gain, grad_ln2_bias = norm_back(d_mlp_in, normed2, inverse2, ln2_gain)
    d_mixed = d_mlp.astype(jnp.float32) + d_norm2
    d_branch = d_mixed.astype(jnp.bfloat16)
    grad_w_out = jnp.einsum("trd,tre->de", attn_low, d_branch, preferred_element_type=jnp.float32)
    d_attn = jnp.einsum("tre,de->trd", d_branch, w_out, preferred_element_type=jnp.float32).astype(
        jnp.bfloat16
    )
    d_attn_heads = d_attn.reshape(table_count, local_rows, head_count, HEAD_DIM)
    dots_rows = jnp.sum(d_attn_heads.astype(jnp.float32) * attended, axis=-1)
    row_dots = jnp.transpose(dots_rows, (0, 2, 1))

    def query_part(block_index):
        scores, key_block, value_block = block_scores(
            query_heads, gathered, block_index, block_width, ctx_count, score_scale
        )
        softened = jnp.exp(scores - log_total[..., None])
        d_soft = jnp.einsum(
            "trhe,tkhe->thrk", d_attn_heads, value_block, preferred_element_type=jnp.float32
        )
        d_scores = (softened * (d_soft - row_dots[..., None])).astype(jnp.bfloat16)
        d_part = (
            jnp.einsum("thrk,tkhe->trhe", d_scores, key_block, preferred_element_type=jnp.float32)
            * score_scale
        )
        return (softened, d_scores, d_part)

    start_query = jnp.zeros((table_count, local_rows, head_count, HEAD_DIM), jnp.float32)

    def grad_step(carried, block_index):
        d_query, d_pairs = carried
        softened, d_scores, d_part = query_part(block_index)
        d_values = jnp.einsum(
            "thrk,trhe->tkhe",
            softened.astype(jnp.bfloat16),
            d_attn_heads,
            preferred_element_type=jnp.float32,
        )
        d_keys = (
            jnp.einsum("thrk,trhe->tkhe", d_scores, query_heads, preferred_element_type=jnp.float32)
            * score_scale
        )
        grad_block = jnp.concatenate(
            [
                d_keys.reshape(table_count, block_width, dmodel),
                d_values.reshape(table_count, block_width, dmodel),
            ],
            axis=-1,
        )
        d_pairs = lax.dynamic_update_slice_in_dim(d_pairs, grad_block, block_index * block_width, 1)
        return ((d_query + d_part, d_pairs), None)

    start_pairs = jnp.zeros((table_count, total_ctx, 2 * dmodel), jnp.float32)
    (d_query, d_pairs), _ = lax.scan(grad_step, (start_query, start_pairs), jnp.arange(block_total))
    own_pairs = lax.psum_scatter(d_pairs, "row", scatter_dimension=1, tiled=True).astype(
        jnp.bfloat16
    )
    d_q = d_query.reshape(table_count, local_rows, dmodel).astype(jnp.bfloat16)
    grad_w_qkv = jnp.concatenate(
        [
            jnp.einsum("trd,tre->de", attn_in, d_q, preferred_element_type=jnp.float32),
            jnp.einsum(
                "trd,tre->de", attn_in[:, :ctx_rows], own_pairs, preferred_element_type=jnp.float32
            ),
        ],
        axis=1,
    )
    d_from_query = jnp.einsum("tre,de->trd", d_q, w_query, preferred_element_type=jnp.float32)
    d_from_pairs = jnp.einsum("tre,de->trd", own_pairs, w_pair, preferred_element_type=jnp.float32)
    d_attn_in = jnp.concatenate(
        [d_from_query[:, :ctx_rows] + d_from_pairs, d_from_query[:, ctx_rows:]], axis=1
    )
    d_norm1, grad_ln1_gain, grad_ln1_bias = norm_back(d_attn_in, normed1, inverse1, ln1_gain)
    d_embed = (d_mixed + d_norm1).astype(jnp.bfloat16)
    grad_w_emb = jnp.einsum("tfr,trd->fd", features, d_embed, preferred_element_type=jnp.float32)
    d_features = jnp.einsum("trd,fd->tfr", d_embed, w_emb, preferred_element_type=jnp.float32)
    d_features = (d_features * slot_live[:, :, None].astype(jnp.float32)).astype(jnp.bfloat16)
    ctx_feat_grad = d_features[:, :, :ctx_rows]
    qry_feat_grad = d_features[:, :, ctx_rows:]
    (
        qkv_part,
        out_part,
        up_part,
        down_part,
        gain1_part,
        bias1_part,
        gain2_part,
        bias2_part,
        upbias_part,
    ) = (
        lax.psum_scatter(grad_w_qkv, "row", scatter_dimension=0, tiled=True),
        lax.psum_scatter(grad_w_out, "row", scatter_dimension=0, tiled=True),
        lax.psum_scatter(grad_w_up, "row", scatter_dimension=0, tiled=True),
        lax.psum_scatter(grad_w_down, "row", scatter_dimension=0, tiled=True),
        lax.psum_scatter(grad_ln1_gain, "row", scatter_dimension=0, tiled=True),
        lax.psum_scatter(grad_ln1_bias, "row", scatter_dimension=0, tiled=True),
        lax.psum_scatter(grad_ln2_gain, "row", scatter_dimension=0, tiled=True),
        lax.psum_scatter(grad_ln2_bias, "row", scatter_dimension=0, tiled=True),
        lax.psum_scatter(grad_b_up, "row", scatter_dimension=0, tiled=True),
    )
    qkv_all, out_all, up_all, down_all, gain1_all, bias1_all, gain2_all, bias2_all, upbias_all = (
        lax.psum(qkv_part.astype(jnp.bfloat16), "tab").astype(jnp.float32),
        lax.psum(out_part.astype(jnp.bfloat16), "tab").astype(jnp.float32),
        lax.psum(up_part.astype(jnp.bfloat16), "tab").astype(jnp.float32),
        lax.psum(down_part.astype(jnp.bfloat16), "tab").astype(jnp.float32),
        lax.psum(gain1_part.astype(jnp.bfloat16), "tab").astype(jnp.float32),
        lax.psum(bias1_part.astype(jnp.bfloat16), "tab").astype(jnp.float32),
        lax.psum(gain2_part.astype(jnp.bfloat16), "tab").astype(jnp.float32),
        lax.psum(bias2_part.astype(jnp.bfloat16), "tab").astype(jnp.float32),
        lax.psum(upbias_part.astype(jnp.bfloat16), "tab").astype(jnp.float32),
    )
    embed_all, squares_all, count_all = lax.psum((grad_w_emb, squares, live_rows), ("tab", "row"))
    rms = jnp.sqrt(squares_all / (count_all * dmodel))
    return (
        ctx_out,
        qry_out,
        ctx_feat_grad,
        qry_feat_grad,
        embed_all,
        gain1_all,
        bias1_all,
        qkv_all,
        out_all,
        gain2_all,
        bias2_all,
        up_all,
        upbias_all,
        down_all,
        rms,
    )


MESH = pl.DeviceIdType.MESH
LANES = 128
NT = (((1,), (1,)), ((), ()))


def swap_rows(values, pick, collective_id):
    row_size = lax.axis_size("row")
    block = values.shape[1:]

    def kernel(src, dst, own_sem, send_sem, recv_sem):
        tab, row = lax.axis_index("tab"), lax.axis_index("row")
        barrier = pltpu.get_barrier_semaphore()
        peers = [(tab, lax.rem(row + k, row_size)) for k in range(1, row_size)]
        for peer in peers:
            pl.semaphore_signal(barrier, inc=1, device_id=peer, device_id_type=MESH)
        pl.semaphore_wait(barrier, row_size - 1)
        copies = []
        for k, peer in enumerate(peers):
            copy = pltpu.make_async_remote_copy(
                src_ref=src.at[pick(peer[1])],
                dst_ref=dst.at[row],
                send_sem=send_sem.at[k],
                recv_sem=recv_sem.at[k],
                device_id=peer,
                device_id_type=MESH,
            )
            copy.start()
            copies.append(copy)
        own = pltpu.make_async_copy(src.at[pick(row)], dst.at[row], own_sem)
        own.start()
        own.wait()
        for copy in copies:
            copy.wait()

    return pl.pallas_call(
        kernel,
        out_shape=jax.ShapeDtypeStruct((row_size,) + block, values.dtype),
        in_specs=[pl.BlockSpec(memory_space=pl.ANY)],
        out_specs=pl.BlockSpec(memory_space=pl.ANY),
        scratch_shapes=[
            pltpu.SemaphoreType.DMA,
            pltpu.SemaphoreType.DMA((row_size - 1,)),
            pltpu.SemaphoreType.DMA((row_size - 1,)),
        ],
        compiler_params=pltpu.CompilerParams(collective_id=collective_id, has_side_effects=True),
        name="swap_rows",
    )(values)


def pack_heads(values):
    rows, width = values.shape[-2:]
    whole = width // LANES
    parts = [values[..., i * LANES : (i + 1) * LANES] for i in range(whole)]
    if width % LANES:
        last = values[..., whole * LANES :]
        parts.append(jnp.concatenate([last[..., : rows // 2, :], last[..., rows // 2 :, :]], axis=-1))
    return jnp.concatenate(parts, axis=-2)


def unpack_heads(packed, rows, width):
    whole = width // LANES
    parts = [packed[..., i * rows : (i + 1) * rows, :] for i in range(whole)]
    if width % LANES:
        last = packed[..., whole * rows :, :]
        parts.append(jnp.concatenate([last[..., :HEAD_DIM], last[..., HEAD_DIM:]], axis=-2))
    return jnp.concatenate(parts, axis=-1)


def lane_of(shape):
    return lax.broadcasted_iota(jnp.int32, shape, len(shape) - 1)


def split_three(values):
    high = values.astype(jnp.bfloat16)
    rest = values - high.astype(jnp.float32)
    mid = rest.astype(jnp.bfloat16)
    tail = (rest - mid.astype(jnp.float32)).astype(jnp.bfloat16)
    return (high, mid, tail)


def set_lanes(values, first, columns):
    lane = lane_of(values.shape)
    values = values.astype(jnp.float32)
    for i, column in enumerate(columns):
        values = jnp.where(lane == first + i, column.astype(jnp.float32), values)
    return values.astype(jnp.bfloat16)


def attend_kernel(chunk, q_ref, k_ref, v_ref, out_ref, back_ref):
    query = q_ref[0]
    for i in range(k_ref.shape[1] // chunk):
        at = pl.ds(i * chunk, chunk)
        scores = lax.dot_general(query, k_ref[0, at], NT, preferred_element_type=jnp.float32)
        top = jnp.max(scores, axis=-1, keepdims=True)
        if i:
            top = jnp.maximum(top, before)
        weights = jnp.exp(scores - top).astype(jnp.bfloat16)
        term = jnp.dot(weights, v_ref[0, at], preferred_element_type=jnp.float32)
        summed = summed * jnp.exp(before - top) + term if i else term
        before = top
    total = summed[:, HEAD_DIM : HEAD_DIM + 1]
    out_ref[0] = (summed / total).astype(jnp.bfloat16)
    back_ref[0] = set_lanes(query, HEAD_DIM + 1, split_three(-(top + jnp.log(total))))


def attend(queries, keys, values, block, chunk):
    heads, rows, _ = queries.shape
    total = keys.shape[1]
    by_query = pl.BlockSpec((1, block, LANES), lambda h, i: (h, i, 0))
    by_key = pl.BlockSpec((1, total, LANES), lambda h, i: (h, 0, 0))
    return pl.pallas_call(
        functools.partial(attend_kernel, chunk),
        grid=(heads, rows // block),
        in_specs=[by_query, by_key, by_key],
        out_specs=[by_query, by_query],
        out_shape=[jax.ShapeDtypeStruct((heads, rows, LANES), jnp.bfloat16)] * 2,
        compiler_params=pltpu.CompilerParams(vmem_limit_bytes=48 * 2**20),
        name="attend",
    )(queries, keys, values)


def greet(peers):
    barrier = pltpu.get_barrier_semaphore()
    for peer in peers:
        pl.semaphore_signal(barrier, inc=1, device_id=peer, device_id_type=MESH)
    pl.semaphore_wait(barrier, len(peers))


def tile_sum(parts):
    total = parts[0]
    for part in parts[1:]:
        total = total + part
    return total


def back_kernel(
    dims, g_hbm, up, down, out, queries, keys, values, outs, feat, w_emb, w_mine, gain, bias, own_feat, d_branch,
    vectors, sums, live,
    ctx_grad, qry_grad, emb_all, sums_all, qkv_all, out_all, up_all, down_all,
    up0, down0, out0, up_in0, down_in0, out_in0, up1, down1, out1, up2, down2, out2,
    up3, down3, out3, up4, down4, out4,
    g_in, grads, d_q, d_kt, d_vt, d_k, d_v, terms, terms_in, d_qkv, d_emb, d_gain, d_bias,
    qkv_own, emb_own, qkv_in0, emb_in0, sums_in0, sums0, qkv_in1, emb_in1, sums_in1,
    qkv1, emb1, sums1, qkv_in2, emb_in2, sums_in2, qkv2, emb2, emb3,
    load_sem, send_sem, recv_sem,
):
    row_size, x_size, chunk, ctx_rows, local_rows = dims
    z_size = row_size // x_size
    heads, total, _ = keys.shape
    pair = x_size * local_rows
    tab, row = lax.axis_index("tab"), lax.axis_index("row")
    core, y = lax.rem(tab, 2), tab // 2
    x, z = lax.rem(row, x_size), row // x_size
    core_peer, y_peer, x_peer = (tab ^ 1, row), (tab ^ 2, row), (tab, row ^ 1)
    row_peers = [(tab, lax.rem(row + k, row_size)) for k in range(1, row_size)]
    z_peers = [(tab, lax.rem(z + k, z_size) * x_size + x) for k in range(1, z_size)]
    numbers = {}

    def remote(name, src, dst, peer):
        i = numbers.setdefault(name, len(numbers))
        return pltpu.make_async_remote_copy(
            src_ref=src, dst_ref=dst, send_sem=send_sem.at[i], recv_sem=recv_sem.at[i],
            device_id=peer, device_id_type=MESH,
        )

    def half(rows, which):
        return pl.ds(pl.multiple_of(which * (rows // 2), 16), rows // 2)

    def columns(ref, which):
        wide = ref.shape[-1] // 2
        return pl.ds(pl.multiple_of(which * wide, LANES), wide)

    def by_z(ref):
        return ref.reshape(z_size, x_size, *ref.shape[1:])

    def g_copy(k):
        peer = row_peers[k]
        return remote(("g", k), g_hbm.at[peer[1]], g_in.at[row], peer)

    big = (("up", up, up0, up_in0), ("down", down, down0, down_in0), ("out", out, out0, out_in0))

    def core_copies():
        return [
            remote(("core", n), src.at[:, half(src.shape[1], 1 - core)], taken, core_peer)
            for n, src, _, taken in big
        ]

    def own_copies():
        return [
            pltpu.make_async_copy(src.at[:, half(src.shape[1], core)], mine, load_sem.at[i])
            for i, (_, src, mine, _) in enumerate(big)
        ]

    def own_g():
        return pltpu.make_async_copy(g_hbm.at[row], g_in.at[row], load_sem.at[3])

    def up_y():
        return [remote("up_y", up0.at[:, :, columns(up0, 1 - y)], up1, y_peer)]

    def down_x():
        return [
            remote("down_x", by_z(down0).at[:, 1 - x], down1, x_peer),
            remote("out_x", by_z(out0).at[:, 1 - x], out1, x_peer),
        ]

    def up_x():
        return [remote("up_x", by_z(up1).at[:, 1 - x], up2, x_peer)]

    def down_y():
        return [
            remote("down_y", down1.at[:, :, columns(down1, 1 - y)], down2, y_peer),
            remote("out_y", out1.at[:, :, columns(out1, 1 - y)], out2, y_peer),
        ]

    def over_z(name, src, dst):
        return [
            remote((name, k), src.at[lax.rem(z + k + 1, z_size)], dst.at[k], peer)
            for k, peer in enumerate(z_peers)
        ]

    def up_z():
        return over_z("up_z", up2, up3)

    def down_z():
        return over_z("down_z", down2, down3) + over_z("out_z", out2, out3)

    lasts = (up4, down4, out4)

    def to_y():
        return [remote(("to_y", i), last.at[core, y], last.at[core, y], y_peer) for i, last in enumerate(lasts)]

    def to_core(which):
        at = y if which == 0 else 1 - y
        return [
            remote(("to_core", which, i), last.at[core, at], last.at[core, at], core_peer)
            for i, last in enumerate(lasts)
        ]

    def start(copies):
        for copy in copies:
            copy.start()

    def wait(copies):
        for copy in copies:
            copy.wait()

    greet([core_peer, y_peer] + row_peers)
    start([own_g()])
    start([g_copy(k) for k in range(row_size - 1)])
    start(own_copies())
    start(core_copies())

    def core_done():
        wait(own_copies())
        wait(core_copies())
        for _, _, mine, taken in big:

            @pl.loop(0, mine.shape[0])
            def _(p):
                mine[p] = mine[p] + taken[p]

        start(up_y())
        start(down_x())

    def up_y_done():
        wait(up_y())

        @pl.loop(0, row_size)
        def _(p):
            up1[p] = up1[p] + up0[p, :, columns(up0, y)]

        start(up_x())

    def down_x_done():
        wait(down_x())

        @pl.loop(0, z_size)
        def _(p):
            down1[p] = down1[p] + down0[p * x_size + x]
            out1[p] = out1[p] + out0[p * x_size + x]

        start(down_y())

    def up_x_done():
        wait(up_x())

        @pl.loop(0, z_size)
        def _(p):
            up2[p] = up2[p] + up1[p * x_size + x]

        start(up_z())

    def down_y_done():
        wait(down_y())

        @pl.loop(0, z_size)
        def _(p):
            down2[p] = down2[p] + down1[p, :, columns(down1, y)]
            out2[p] = out2[p] + out1[p, :, columns(out1, y)]

        start(down_z())

    d_kt[...] = jnp.zeros_like(d_kt)
    d_vt[...] = jnp.zeros_like(d_vt)
    whole = heads // 2

    def unpack(p, at):
        packed = g_in[p]
        parts = []
        for h in range(whole):
            tile = packed[h * local_rows : (h + 1) * local_rows]
            parts += [tile[:, :HEAD_DIM], tile[:, HEAD_DIM:]]
        if heads % 2:
            tile = packed[whole * local_rows :]
            parts.append(jnp.concatenate([tile[:, :HEAD_DIM], tile[:, HEAD_DIM:]], axis=0))
        rows = pl.ds(pl.multiple_of(p * local_rows, 16), local_rows)
        for h, part in enumerate(parts):
            part = part.astype(jnp.float32)
            result = outs[h, rows, :HEAD_DIM].astype(jnp.float32)
            inner = jnp.sum(part * result, axis=-1, keepdims=True)
            wide = jnp.concatenate([part, jnp.zeros_like(part)], axis=-1)
            grads[h, rows] = set_lanes(wide, HEAD_DIM, split_three(-inner))

    def segment(step, _):
        k, h = step // heads, lax.rem(step, heads)
        there = lax.rem(z + k, z_size)
        rows = pl.ds(pl.multiple_of(there * pair, LANES), pair)

        @pl.when(h == 0)
        def _():
            for other in range(x_size):
                p = there * x_size + other
                shift = lax.rem(p - row + row_size, row_size)
                for s in range(1, row_size):

                    @pl.when(shift == s)
                    def _():
                        g_copy(row_size - s - 1).wait_recv()

                @pl.when(shift == 0)
                def _():
                    own_g().wait()

                unpack(p, there)

        for at, act in ((heads, core_done), (3 * heads, up_y_done)):

            @pl.when(step == at)
            def _():
                act()

        query, grad = queries[h, rows], grads[h, rows]
        query_t = query[:, :HEAD_DIM].T
        grad_t = grad[:, :HEAD_DIM].T
        d_query = jnp.zeros((pair, LANES), jnp.float32)
        for i in range(total // chunk):
            at = pl.ds(i * chunk, chunk)
            key, value = keys[h, at], values[h, at]
            probs = jnp.exp(lax.dot_general(query, key, NT, preferred_element_type=jnp.float32))
            d_probs = lax.dot_general(grad, value, NT, preferred_element_type=jnp.float32)
            d_scores = (probs * d_probs).astype(jnp.bfloat16)
            d_vt[h, :, at] += jnp.dot(grad_t, probs.astype(jnp.bfloat16), preferred_element_type=jnp.float32)
            d_kt[h, :, at] += jnp.dot(query_t, d_scores, preferred_element_type=jnp.float32)
            d_query += jnp.dot(d_scores, key, preferred_element_type=jnp.float32)
        d_q[h, rows] = (d_query[:, :HEAD_DIM] * HEAD_DIM ** (-0.5)).astype(jnp.bfloat16)
        return 0

    lax.fori_loop(0, z_size * heads, segment, 0)
    for k in range(row_size - 1):
        g_copy(k).wait_send()
    down_x_done()
    for h in range(heads):
        d_k[h] = d_kt[h].T.astype(jnp.bfloat16)
        d_v[h] = d_vt[h].T.astype(jnp.bfloat16)

    d_qkv[...] = jnp.zeros_like(d_qkv)
    d_emb[...] = jnp.zeros_like(d_emb)
    d_gain[...] = jnp.zeros_like(d_gain)
    d_bias[...] = jnp.zeros_like(d_bias)

    def term_copy(shift):
        p = lax.rem(row + shift, row_size)
        return remote(("term", shift), terms.at[p], terms_in.at[row], (tab, p))

    def project(step, _):
        shift = lax.rem(step + 1, z_size)
        there = lax.rem(z + shift, z_size)
        pieces, embeds = [], []
        for other in range(x_size):
            p = there * x_size + other
            rows = pl.ds(pl.multiple_of(p * local_rows, 16), local_rows)
            key_rows = pl.ds(pl.multiple_of(p * ctx_rows, 16), ctx_rows)
            parts = [d_q[h, rows] for h in range(heads)]
            nothing = jnp.zeros((local_rows - ctx_rows, HEAD_DIM), jnp.bfloat16)
            for ref in (d_k, d_v):
                parts += [jnp.concatenate([ref[h, key_rows], nothing], axis=0) for h in range(heads)]
            pieces.append(jnp.concatenate(parts, axis=1))
            embeds.append(feat[p])
        d_three = jnp.concatenate(pieces, axis=0)
        rows_feat = jnp.concatenate(embeds, axis=0)
        embed = jnp.dot(rows_feat, w_emb[...], preferred_element_type=jnp.float32)
        center = embed - jnp.mean(embed, axis=-1, keepdims=True)
        inverse = lax.rsqrt(jnp.mean(center * center, axis=-1, keepdims=True) + EPS)
        normed = center * inverse
        attn_in = (normed * gain[...] + bias[...]).astype(jnp.bfloat16)
        d_in = lax.dot_general(d_three, w_mine[...], NT, preferred_element_type=jnp.float32)
        d_gain[...] += jnp.sum(d_in * normed, axis=0, keepdims=True)
        d_bias[...] += jnp.sum(d_in, axis=0, keepdims=True)
        scaled = d_in * gain[...]
        inner = (
            scaled
            - jnp.mean(scaled, axis=-1, keepdims=True)
            - normed * jnp.mean(scaled * normed, axis=-1, keepdims=True)
        )
        d_norm = (inverse * inner).astype(jnp.bfloat16)
        term = lax.dot_general(d_norm, w_emb[...], NT, preferred_element_type=jnp.float32).astype(jnp.bfloat16)
        d_emb[...] += jnp.dot(rows_feat.T, d_norm, preferred_element_type=jnp.float32)
        d_qkv[...] += jnp.dot(attn_in.T, d_three, preferred_element_type=jnp.float32)
        for other in range(x_size):
            p = there * x_size + other
            terms[p] = term[other * local_rows : (other + 1) * local_rows]
            ahead = lax.rem(p - row + row_size, row_size)
            for s in range(1, row_size):

                @pl.when(ahead == s)
                def _():
                    term_copy(s).start()

        for at, act in ((1, up_x_done), (2, down_y_done)):

            @pl.when(step == at)
            def _():
                act()

        return 0

    lax.fori_loop(0, z_size, project, 0)

    shard = qkv_own.shape[1]
    for p in range(row_size):
        qkv_own[p] = d_qkv[p * shard : (p + 1) * shard].astype(jnp.bfloat16)
    own_rows = jnp.concatenate([own_feat[t] for t in range(own_feat.shape[0])], axis=0)
    own_d = jnp.concatenate([d_branch[t] for t in range(own_feat.shape[0])], axis=0)
    d_own = d_emb[...] + jnp.dot(own_rows.T, own_d, preferred_element_type=jnp.float32)
    slots = d_own.shape[0]
    spare = lax.broadcasted_iota(jnp.int32, d_own.shape, 0) - (slots - vectors.shape[0])
    d_own = jnp.where(spare == 0, d_gain[...], d_own)
    d_own = jnp.where(spare == 1, d_bias[...], d_own)
    for i in range(2, vectors.shape[0]):
        d_own = jnp.where(spare == i, vectors[i : i + 1], d_own)
    emb_rows = emb_own.shape[1]
    for p in range(row_size):
        emb_own[p] = d_own[p * emb_rows : (p + 1) * emb_rows].astype(jnp.bfloat16)

    def tail_core():
        return [
            remote("qkv_core", qkv_own.at[:, half(shard, 1 - core)], qkv_in0, core_peer),
            remote("emb_core", emb_own.at[:, :, columns(emb_own, 1 - core)], emb_in0, core_peer),
            remote("sums_core", sums, sums_in0, core_peer),
        ]

    def tail_row():
        copies = []
        for k, peer in enumerate(row_peers):
            copies += [
                remote(("qkv_row", k), qkv_in0.at[peer[1]], qkv_in1.at[row], peer),
                remote(("emb_row", k), emb_in0.at[peer[1]], emb_in1.at[row], peer),
                remote(("sums_row", k), sums0, sums_in1.at[row], peer),
            ]
        return copies

    start(tail_core())
    wait(tail_core())
    qkv_in0[...] = qkv_in0[...] + qkv_own[:, half(shard, core)]
    emb_in0[...] = emb_in0[...] + emb_own[:, :, columns(emb_own, core)]
    sums0[...] = sums[...] + sums_in0[...]
    start(tail_row())
    qkv_in1[row] = qkv_in0[row]
    emb_in1[row] = emb_in0[row]
    sums_in1[row] = sums0[...]

    terms_in[row] = terms[row]
    for s in range(1, row_size):
        term_copy(s).wait()
    groups = qkv1.shape[0]
    for t in range(own_feat.shape[0]):
        term = lax.dot_general(d_branch[t], w_emb[...], NT, preferred_element_type=jnp.float32)
        for g in range(groups):
            term = term + terms_in[t * groups + g].astype(jnp.float32)
        by_slot = (term.T * live[t]).astype(jnp.bfloat16)[: ctx_grad.shape[1]]
        ctx_grad[t] = by_slot[:, :ctx_rows]
        qry_grad[t] = by_slot[:, ctx_rows:]

    wait(up_z())
    wait(down_z())
    for part, taken, last in ((up2, up3, up4), (down2, down3, down4), (out2, out3, out4)):
        whole_sum = part[z].astype(jnp.float32)
        for k in range(z_size - 1):
            whole_sum = whole_sum + taken[k].astype(jnp.float32)
        last[core, y] = whole_sum.astype(jnp.bfloat16)
    start(to_y())
    start(to_core(0))

    wait(tail_row())
    for g in range(groups):
        qkv1[g] = tile_sum(
            [qkv_in1[g + t * groups].astype(jnp.float32) for t in range(row_size // groups)]
        ).astype(jnp.bfloat16)
    emb1[...] = tile_sum([emb_in1[p].astype(jnp.float32) for p in range(row_size)]).astype(jnp.bfloat16)
    sums1[...] = tile_sum([sums_in1[p] for p in range(row_size)])
    tail_y = [
        remote("qkv_y", qkv1, qkv_in2, y_peer),
        remote("emb_y", emb1, emb_in2, y_peer),
        remote("sums_y", sums1, sums_in2, y_peer),
    ]
    start(tail_y)
    wait(to_y())
    start(to_core(1))
    wait(tail_y)
    qkv2[core] = qkv1[...] + qkv_in2[...]
    emb2[:, columns(emb_own, core)] = emb1[...] + emb_in2[...]
    sums_all[...] = sums1[...] + sums_in2[...]
    at_core = columns(emb_own, core)
    tail_last = [
        remote("qkv_last", qkv2.at[core], qkv2.at[core], core_peer),
        remote("emb_last", emb2.at[:, at_core], emb2.at[:, at_core], core_peer),
    ]
    start(tail_last)
    wait(to_core(0))
    wait(to_core(1))
    wait(tail_last)
    emb_row = [remote(("emb_all", k), emb2, emb3.at[row], peer) for k, peer in enumerate(row_peers)]
    start(emb_row)
    emb3[row] = emb2[...]
    for last, result in ((up4, up_all), (down4, down_all), (out4, out_all)):
        rows, wide = last.shape[2:]
        for i in range(2):
            for j in range(2):
                result[i * rows : (i + 1) * rows, j * wide : (j + 1) * wide] = last[i, j].astype(jnp.float32)
    width = heads * HEAD_DIM
    for i in range(2):
        parts = [
            qkv2[i, g][:, n * width : (n + 1) * width].astype(jnp.float32) for n in range(3) for g in range(groups)
        ]
        qkv_all[i * (shard // 2) : (i + 1) * (shard // 2)] = jnp.concatenate(parts, axis=1)
    wait(emb_row)
    for p in range(row_size):
        emb_all[p * emb_rows : (p + 1) * emb_rows] = emb3[p].astype(jnp.float32)


def back(g_packed, weight_grads, queries, keys, values, outs, feat, w_emb, w_mine, gain, bias, own_feat, d_branch,
         vectors, sums, live, slot_count, ctx_rows, groups, chunk, collective_id):
    row_size, local_rows, slots = feat.shape
    heads, total, _ = keys.shape
    all_rows = queries.shape[1]
    dmodel = w_emb.shape[1]
    width = heads * HEAD_DIM
    x_size = 2
    z_size = row_size // x_size
    shapes = [(g.shape[0] // row_size, g.shape[1]) for g in weight_grads]
    split = [g.reshape(row_size, *s) for g, s in zip(weight_grads, shapes)]
    bf16 = lambda *shape: pltpu.VMEM(shape, jnp.bfloat16)
    f32 = lambda *shape: pltpu.VMEM(shape, jnp.float32)
    stage0 = [bf16(row_size, r // 2, w) for r, w in shapes]
    (ru, wu), (rd, wd), (ro, wo) = shapes
    stage1 = [bf16(row_size, ru // 2, wu // 2), bf16(z_size, rd // 2, wd), bf16(z_size, ro // 2, wo)]
    stage2 = [bf16(z_size, r // 2, w // 2) for r, w in shapes]
    stage3 = [bf16(z_size - 1, r // 2, w // 2) for r, w in shapes]
    stage4 = [bf16(2, 2, r // 2, w // 2) for r, w in shapes]
    by_head = bf16(heads, all_rows, LANES)
    shard, emb_rows = dmodel // row_size, slots // row_size
    attention = [
        bf16(*g_packed.shape), by_head, bf16(heads, all_rows, HEAD_DIM),
        f32(heads, HEAD_DIM, total), f32(heads, HEAD_DIM, total),
        bf16(heads, total, HEAD_DIM), bf16(heads, total, HEAD_DIM),
        bf16(*feat.shape), bf16(*feat.shape),
        f32(dmodel, 3 * width), f32(slots, dmodel), f32(1, dmodel), f32(1, dmodel),
    ]
    half_qkv, half_emb = (row_size, shard // 2, 3 * width), (row_size, emb_rows, dmodel // 2)
    tail = [
        bf16(row_size, shard, 3 * width), bf16(row_size, emb_rows, dmodel),
        bf16(*half_qkv), bf16(*half_emb), f32(*sums.shape), f32(*sums.shape),
        bf16(*half_qkv), bf16(*half_emb), f32(row_size, *sums.shape),
        bf16(groups, shard // 2, 3 * width), bf16(emb_rows, dmodel // 2), f32(*sums.shape),
        bf16(groups, shard // 2, 3 * width), bf16(emb_rows, dmodel // 2), f32(*sums.shape),
        bf16(2, groups, shard // 2, 3 * width), bf16(emb_rows, dmodel), bf16(row_size, emb_rows, dmodel),
    ]
    sends = 3 + 6 + 3 * (z_size - 1) + 9 + 8 + 6 * (row_size - 1)
    vmem = pl.BlockSpec(memory_space=pltpu.VMEM)
    anywhere = pl.BlockSpec(memory_space=pl.ANY)
    f32_out = lambda *shape: jax.ShapeDtypeStruct(shape, jnp.float32)
    return pl.pallas_call(
        functools.partial(back_kernel, (row_size, x_size, chunk, ctx_rows, local_rows)),
        out_shape=[
            jax.ShapeDtypeStruct((own_feat.shape[0], slot_count, ctx_rows), jnp.bfloat16),
            jax.ShapeDtypeStruct((own_feat.shape[0], slot_count, local_rows - ctx_rows), jnp.bfloat16),
            f32_out(slots, dmodel),
            f32_out(*sums.shape),
            f32_out(shard, 3 * dmodel),
            f32_out(ro, wo),
            f32_out(ru, wu),
            f32_out(rd, wd),
        ],
        in_specs=[anywhere] * 4 + [vmem] * 14,
        out_specs=[vmem] * 8,
        scratch_shapes=stage0 + stage0 + stage1 + stage2 + stage3 + stage4 + attention + tail + [
            pltpu.SemaphoreType.DMA((4,)),
            pltpu.SemaphoreType.DMA((sends,)),
            pltpu.SemaphoreType.DMA((sends,)),
        ],
        compiler_params=pltpu.CompilerParams(
            collective_id=collective_id, has_side_effects=True, vmem_limit_bytes=62 * 2**20
        ),
        name="back",
    )(g_packed, split[0], split[1], split[2], queries, keys, values, outs, feat, w_emb, w_mine, gain, bias,
      own_feat, d_branch, vectors, sums, live)


def local_by_heads(
    ctx_feat,
    qry_feat,
    feat_count,
    ctx_count,
    qry_count,
    w_emb,
    ln1_gain,
    ln1_bias,
    w_qkv,
    w_out,
    ln2_gain,
    ln2_bias,
    w_up,
    b_up,
    w_down,
    ctx_cot,
    qry_cot,
):
    table_count, slot_count, ctx_rows = ctx_feat.shape
    qry_rows = qry_feat.shape[2]
    local_rows = ctx_rows + qry_rows
    dmodel = w_out.shape[0]
    head_count = dmodel // HEAD_DIM
    score_scale = HEAD_DIM ** (-0.5)
    row_size = lax.axis_size("row")
    total_ctx = ctx_rows * row_size
    all_rows = local_rows * row_size
    row_index = lax.axis_index("row")
    groups = row_size // table_count
    heads = head_count // groups
    width = heads * HEAD_DIM
    table, group = row_index // groups, row_index % groups

    slot_live = (jnp.arange(slot_count)[None, :] < feat_count[:, None]).astype(jnp.bfloat16)
    features = jnp.concatenate([ctx_feat, qry_feat], axis=2) * slot_live[:, :, None]
    by_row = jnp.pad(jnp.transpose(features, (0, 2, 1)), ((0, 0), (0, 0), (0, LANES - slot_count)))
    w_emb_pad = jnp.pad(w_emb, ((0, LANES - slot_count), (0, 0)))
    ctx_live = (row_index * ctx_rows + jnp.arange(ctx_rows))[None, :] < ctx_count[:, None]
    qry_live = (row_index * qry_rows + jnp.arange(qry_rows))[None, :] < qry_count[:, None]
    valid = jnp.concatenate([ctx_live, qry_live], axis=1).astype(jnp.float32)[..., None]

    table_feat = swap_rows(by_row, lambda p: p // groups, 0)
    table_embed = jnp.einsum("prf,fd->prd", table_feat, w_emb_pad, preferred_element_type=jnp.float32)
    normed1, inverse1 = standardize(table_embed)
    attn_in = (normed1 * ln1_gain + ln1_bias).astype(jnp.bfloat16)
    w_three = w_qkv.reshape(dmodel, 3, head_count, HEAD_DIM)
    w_three = lax.dynamic_slice_in_dim(w_three, group * heads, heads, 2)
    w_lanes = jnp.pad(w_three, ((0, 0), (0, 0), (0, 0), (0, LANES - HEAD_DIM)))
    projected = jnp.einsum("prd,dnhe->nhpre", attn_in, w_lanes, preferred_element_type=jnp.float32)
    lane = jnp.arange(LANES)
    my_count = lax.dynamic_index_in_dim(ctx_count, table, 0, keepdims=False)
    live_keys = (jnp.arange(total_ctx) < my_count).reshape(row_size, ctx_rows)
    bias = jnp.where(live_keys, 0.0, NEGATIVE)[None, :, :, None]
    queries = jnp.where(lane == HEAD_DIM, 1.0, projected[0] * score_scale).astype(jnp.bfloat16)
    queries = queries.reshape(heads, all_rows, LANES)
    keys = jnp.where(lane == HEAD_DIM, bias, projected[1][:, :, :ctx_rows])
    keys = jnp.where((lane > HEAD_DIM) & (lane < HEAD_DIM + 4), 1.0, keys).astype(jnp.bfloat16)
    keys = keys.reshape(heads, total_ctx, LANES)
    values = jnp.where((lane >= HEAD_DIM) & (lane < HEAD_DIM + 3), 1.0, projected[2][:, :, :ctx_rows])
    values = values.astype(jnp.bfloat16).reshape(heads, total_ctx, LANES)
    outs, back_queries = attend(queries, keys, values, 2 * local_rows, math.gcd(total_ctx, 1024))

    def to_rows(by_head):
        wide = jnp.transpose(by_head[..., :HEAD_DIM], (1, 0, 2)).reshape(row_size, local_rows, width)
        return swap_rows(pack_heads(wide), lambda p: p, 1)

    packed = to_rows(outs)
    attn_low = unpack_heads(packed, local_rows, width).reshape(table_count, groups, local_rows, width)
    attn_low = jnp.transpose(attn_low, (0, 2, 1, 3)).reshape(table_count, local_rows, dmodel)

    embed = jnp.einsum("trf,fd->trd", by_row, w_emb_pad, preferred_element_type=jnp.float32)
    branch = jnp.einsum("trd,de->tre", attn_low, w_out, preferred_element_type=jnp.float32)
    mixed = embed + branch
    normed2, inverse2 = standardize(mixed)
    mlp_in = (normed2 * ln2_gain + ln2_bias).astype(jnp.bfloat16)
    hidden = jnp.einsum("trd,de->tre", mlp_in, w_up, preferred_element_type=jnp.float32) + b_up
    activation, gelu_back = jax.vjp(gelu_exact, hidden)
    act_low = activation.astype(jnp.bfloat16)
    mlp = jnp.einsum("tre,ed->trd", act_low, w_down, preferred_element_type=jnp.float32)
    output = (mixed + mlp) * valid
    ctx_out = output[:, :ctx_rows].astype(jnp.bfloat16)
    qry_out = output[:, ctx_rows:].astype(jnp.bfloat16)
    squares = jnp.stack(
        [
            jnp.sum(valid * embed * embed),
            jnp.sum(valid * branch * branch),
            jnp.sum(valid * mlp * mlp),
            jnp.sum(valid * output * output),
        ]
    )
    live_rows = jnp.sum(valid)
    cotangent = jnp.concatenate([ctx_cot, qry_cot], axis=1)
    d_mlp = cotangent * valid.astype(jnp.bfloat16)
    grad_w_down = jnp.einsum("tre,trd->ed", act_low, d_mlp, preferred_element_type=jnp.float32)
    d_act = jnp.einsum("trd,ed->tre", d_mlp, w_down, preferred_element_type=jnp.float32)
    d_hidden = gelu_back(d_act)[0].astype(jnp.bfloat16)
    grad_b_up = jnp.sum(d_hidden.astype(jnp.float32), axis=(0, 1))
    grad_w_up = jnp.einsum("trd,tre->de", mlp_in, d_hidden, preferred_element_type=jnp.float32)
    d_mlp_in = jnp.einsum("tre,de->trd", d_hidden, w_up, preferred_element_type=jnp.float32)
    d_norm2, grad_ln2_gain, grad_ln2_bias = norm_back(d_mlp_in, normed2, inverse2, ln2_gain)
    d_mixed = d_mlp.astype(jnp.float32) + d_norm2
    d_branch = d_mixed.astype(jnp.bfloat16)
    grad_w_out = jnp.einsum("trd,tre->de", attn_low, d_branch, preferred_element_type=jnp.float32)
    d_attn = jnp.einsum("tre,de->trd", d_branch, w_out, preferred_element_type=jnp.float32).astype(
        jnp.bfloat16
    )

    d_attn = jnp.transpose(d_attn.reshape(table_count, local_rows, groups, width), (0, 2, 1, 3))
    d_attn = d_attn.reshape(row_size, local_rows, width)
    low = lambda grad: grad.astype(jnp.bfloat16)
    nothing = jnp.zeros((2, dmodel), jnp.float32)
    vectors = jnp.concatenate(
        [nothing, grad_ln2_gain[None], grad_ln2_bias[None], grad_b_up.reshape(-1, dmodel)], axis=0
    )
    sums = jnp.pad(jnp.concatenate([squares, live_rows[None]])[None], ((0, 7), (0, LANES - 5)))
    live_pad = jnp.pad(slot_live.astype(jnp.float32), ((0, 0), (0, LANES - slot_count)))[..., None]
    ctx_feat_grad, qry_feat_grad, emb_all, sums, qkv_all, out_all, up_all, down_all = back(
        pack_heads(d_attn),
        (low(grad_w_up), low(grad_w_down), low(grad_w_out)),
        back_queries,
        keys,
        values,
        outs,
        table_feat,
        w_emb_pad,
        w_three.reshape(dmodel, 3 * width),
        ln1_gain[None],
        ln1_bias[None],
        by_row,
        d_branch,
        vectors,
        sums,
        live_pad,
        slot_count,
        ctx_rows,
        groups,
        math.gcd(total_ctx, 512),
        2,
    )
    grad_w_emb = emb_all[:slot_count]
    vectors = emb_all[LANES - vectors.shape[0] :]

    def own(vector):
        size = vector.size // row_size
        return lax.dynamic_slice_in_dim(vector.reshape(-1), row_index * size, size, 0)

    gain1_all, bias1_all, gain2_all, bias2_all = (own(vectors[i]) for i in range(4))
    upbias_all = own(vectors[4:])
    squares, live_rows = sums[0, :4], sums[0, 4]
    rms = jnp.sqrt(squares / (live_rows * dmodel))
    return (
        ctx_out,
        qry_out,
        ctx_feat_grad,
        qry_feat_grad,
        grad_w_emb,
        gain1_all,
        bias1_all,
        qkv_all,
        out_all,
        gain2_all,
        bias2_all,
        up_all,
        upbias_all,
        down_all,
        rms,
    )


def local(ctx_feat, qry_feat, *rest):
    table_count, slot_count, ctx_rows = ctx_feat.shape
    qry_rows = qry_feat.shape[2]
    head_count = rest[6].shape[0] // HEAD_DIM
    row_size = lax.axis_size("row")
    even = row_size % table_count == 0 and head_count % (row_size // table_count) == 0
    whole = slot_count + 4 + rest[10].shape[1] // rest[6].shape[0] <= LANES and row_size % 2 == 0 and ctx_rows % LANES == 0 and qry_rows % 32 == 0
    inner = local_by_heads if even and whole else local_by_rows
    return inner(ctx_feat, qry_feat, *rest)


def solution(mesh):
    in_specs = (
        P("tab", None, "row"),
        P("tab", None, "row"),
        P("tab"),
        P("tab"),
        P("tab"),
        P(),
        P(),
        P(),
        P(),
        P(),
        P(),
        P(),
        P(),
        P(),
        P(),
        P("tab", "row", None),
        P("tab", "row", None),
    )
    out_specs = (
        P("tab", "row", None),
        P("tab", "row", None),
        P("tab", None, "row"),
        P("tab", None, "row"),
        P(),
        P("row"),
        P("row"),
        P("row", None),
        P("row", None),
        P("row"),
        P("row"),
        P("row", None),
        P("row"),
        P("row", None),
        P(),
    )
    return jax.shard_map(local, mesh=mesh, in_specs=in_specs, out_specs=out_specs, check_vma=False)
```

```python
import functools
import math

import jax
import jax.numpy as jnp
from jax import lax
from jax.experimental import pallas as pl
from jax.experimental.pallas import tpu as pltpu
from jax.sharding import PartitionSpec as P

HEAD_DIM = 64


EPS = 1e-05
NEGATIVE = -1e30


def standardize(values):
    center = values - jnp.mean(values, axis=-1, keepdims=True)
    inverse = lax.rsqrt(jnp.mean(center * center, axis=-1, keepdims=True) + EPS)
    return (center * inverse, inverse)


def norm_back(grad_out, normed, inverse, gain):
    scaled = grad_out * gain
    inner = (
        scaled
        - jnp.mean(scaled, axis=-1, keepdims=True)
        - normed * jnp.mean(scaled * normed, axis=-1, keepdims=True)
    )
    grad_gain = jnp.sum(grad_out * normed, axis=(0, 1))
    grad_bias = jnp.sum(grad_out, axis=(0, 1))
    return (inverse * inner, grad_gain, grad_bias)


def gelu_exact(values):
    return jax.nn.gelu(values, approximate=False)


def block_scores(query_heads, key_rows, block_index, block_width, key_count, score_scale):
    table_count, local_rows, head_count, head_size = query_heads.shape
    dmodel = head_count * head_size
    block = lax.dynamic_slice_in_dim(key_rows, block_index * block_width, block_width, 1)
    key_block = block[..., :dmodel].reshape(table_count, block_width, head_count, head_size)
    value_block = block[..., dmodel:].reshape(table_count, block_width, head_count, head_size)
    scores = (
        jnp.einsum("trhe,tkhe->thrk", query_heads, key_block, preferred_element_type=jnp.float32)
        * score_scale
    )
    position = block_index * block_width + jnp.arange(block_width)
    live_keys = position[None, :] < key_count[:, None]
    scores = jnp.where(live_keys[:, None, None, :], scores, NEGATIVE)
    return (scores, key_block, value_block)


def local_by_rows(
    ctx_feat,
    qry_feat,
    feat_count,
    ctx_count,
    qry_count,
    w_emb,
    ln1_gain,
    ln1_bias,
    w_qkv,
    w_out,
    ln2_gain,
    ln2_bias,
    w_up,
    b_up,
    w_down,
    ctx_cot,
    qry_cot,
):
    table_count, slot_count, ctx_rows = ctx_feat.shape
    qry_rows = qry_feat.shape[2]
    local_rows = ctx_rows + qry_rows
    dmodel = w_out.shape[0]
    head_count = dmodel // HEAD_DIM
    score_scale = HEAD_DIM ** (-0.5)
    total_ctx = ctx_rows * lax.axis_size("row")
    row_index = lax.axis_index("row")
    slot_live = (jnp.arange(slot_count)[None, :] < feat_count[:, None]).astype(jnp.bfloat16)
    features = jnp.concatenate([ctx_feat, qry_feat], axis=2) * slot_live[:, :, None]
    ctx_live = (row_index * ctx_rows + jnp.arange(ctx_rows))[None, :] < ctx_count[:, None]
    qry_live = (row_index * qry_rows + jnp.arange(qry_rows))[None, :] < qry_count[:, None]
    valid = jnp.concatenate([ctx_live, qry_live], axis=1).astype(jnp.float32)[..., None]
    embed = jnp.einsum("tfr,fd->trd", features, w_emb, preferred_element_type=jnp.float32)
    normed1, inverse1 = standardize(embed)
    attn_in = (normed1 * ln1_gain + ln1_bias).astype(jnp.bfloat16)
    w_query = w_qkv[:, :dmodel]
    w_pair = w_qkv[:, dmodel:]
    query = jnp.einsum("trd,de->tre", attn_in, w_query, preferred_element_type=jnp.float32).astype(
        jnp.bfloat16
    )
    pairs = jnp.einsum(
        "trd,de->tre", attn_in[:, :ctx_rows], w_pair, preferred_element_type=jnp.float32
    ).astype(jnp.bfloat16)
    gathered = lax.all_gather(pairs, "row", axis=1, tiled=True)
    block_width = math.gcd(total_ctx, 512)
    block_total = total_ctx // block_width
    query_heads = query.reshape(table_count, local_rows, head_count, HEAD_DIM)

    def attend_step(carried, block_index):
        running_max, running_sum, summed = carried
        scores, _, value_block = block_scores(
            query_heads, gathered, block_index, block_width, ctx_count, score_scale
        )
        new_max = jnp.maximum(running_max, jnp.max(scores, axis=-1))
        factor = jnp.exp(running_max - new_max)
        weights = jnp.exp(scores - new_max[..., None])
        running_sum = running_sum * factor + jnp.sum(weights, axis=-1)
        summed = summed * jnp.transpose(factor, (0, 2, 1))[..., None] + jnp.einsum(
            "thrk,tkhe->trhe",
            weights.astype(jnp.bfloat16),
            value_block,
            preferred_element_type=jnp.float32,
        )
        return ((new_max, running_sum, summed), None)

    initial = jnp.full((table_count, head_count, local_rows), NEGATIVE, jnp.float32)
    start_sum = jnp.zeros((table_count, local_rows, head_count, HEAD_DIM), jnp.float32)
    (running_max, running_sum, summed), _ = lax.scan(
        attend_step, (initial, jnp.zeros_like(initial), start_sum), jnp.arange(block_total)
    )
    log_total = running_max + jnp.log(running_sum)
    attended = summed / jnp.transpose(running_sum, (0, 2, 1))[..., None]
    attn_low = attended.reshape(table_count, local_rows, dmodel).astype(jnp.bfloat16)
    branch = jnp.einsum("trd,de->tre", attn_low, w_out, preferred_element_type=jnp.float32)
    mixed = embed + branch
    normed2, inverse2 = standardize(mixed)
    mlp_in = (normed2 * ln2_gain + ln2_bias).astype(jnp.bfloat16)
    hidden = jnp.einsum("trd,de->tre", mlp_in, w_up, preferred_element_type=jnp.float32) + b_up
    activation, gelu_back = jax.vjp(gelu_exact, hidden)
    act_low = activation.astype(jnp.bfloat16)
    mlp = jnp.einsum("tre,ed->trd", act_low, w_down, preferred_element_type=jnp.float32)
    output = (mixed + mlp) * valid
    ctx_out = output[:, :ctx_rows].astype(jnp.bfloat16)
    qry_out = output[:, ctx_rows:].astype(jnp.bfloat16)
    squares = jnp.stack(
        [
            jnp.sum(valid * embed * embed),
            jnp.sum(valid * branch * branch),
            jnp.sum(valid * mlp * mlp),
            jnp.sum(valid * output * output),
        ]
    )
    live_rows = jnp.sum(valid)
    cotangent = jnp.concatenate([ctx_cot, qry_cot], axis=1)
    d_mlp = cotangent * valid.astype(jnp.bfloat16)
    grad_w_down = jnp.einsum("tre,trd->ed", act_low, d_mlp, preferred_element_type=jnp.float32)
    d_act = jnp.einsum("trd,ed->tre", d_mlp, w_down, preferred_element_type=jnp.float32)
    d_hidden = gelu_back(d_act)[0].astype(jnp.bfloat16)
    grad_b_up = jnp.sum(d_hidden.astype(jnp.float32), axis=(0, 1))
    grad_w_up = jnp.einsum("trd,tre->de", mlp_in, d_hidden, preferred_element_type=jnp.float32)
    d_mlp_in = jnp.einsum("tre,de->trd", d_hidden, w_up, preferred_element_type=jnp.float32)
    d_norm2, grad_ln2_gain, grad_ln2_bias = norm_back(d_mlp_in, normed2, inverse2, ln2_gain)
    d_mixed = d_mlp.astype(jnp.float32) + d_norm2
    d_branch = d_mixed.astype(jnp.bfloat16)
    grad_w_out = jnp.einsum("trd,tre->de", attn_low, d_branch, preferred_element_type=jnp.float32)
    d_attn = jnp.einsum("tre,de->trd", d_branch, w_out, preferred_element_type=jnp.float32).astype(
        jnp.bfloat16
    )
    d_attn_heads = d_attn.reshape(table_count, local_rows, head_count, HEAD_DIM)
    dots_rows = jnp.sum(d_attn_heads.astype(jnp.float32) * attended, axis=-1)
    row_dots = jnp.transpose(dots_rows, (0, 2, 1))

    def query_part(block_index):
        scores, key_block, value_block = block_scores(
            query_heads, gathered, block_index, block_width, ctx_count, score_scale
        )
        softened = jnp.exp(scores - log_total[..., None])
        d_soft = jnp.einsum(
            "trhe,tkhe->thrk", d_attn_heads, value_block, preferred_element_type=jnp.float32
        )
        d_scores = (softened * (d_soft - row_dots[..., None])).astype(jnp.bfloat16)
        d_part = (
            jnp.einsum("thrk,tkhe->trhe", d_scores, key_block, preferred_element_type=jnp.float32)
            * score_scale
        )
        return (softened, d_scores, d_part)

    start_query = jnp.zeros((table_count, local_rows, head_count, HEAD_DIM), jnp.float32)

    def grad_step(carried, block_index):
        d_query, d_pairs = carried
        softened, d_scores, d_part = query_part(block_index)
        d_values = jnp.einsum(
            "thrk,trhe->tkhe",
            softened.astype(jnp.bfloat16),
            d_attn_heads,
            preferred_element_type=jnp.float32,
        )
        d_keys = (
            jnp.einsum("thrk,trhe->tkhe", d_scores, query_heads, preferred_element_type=jnp.float32)
            * score_scale
        )
        grad_block = jnp.concatenate(
            [
                d_keys.reshape(table_count, block_width, dmodel),
                d_values.reshape(table_count, block_width, dmodel),
            ],
            axis=-1,
        )
        d_pairs = lax.dynamic_update_slice_in_dim(d_pairs, grad_block, block_index * block_width, 1)
        return ((d_query + d_part, d_pairs), None)

    start_pairs = jnp.zeros((table_count, total_ctx, 2 * dmodel), jnp.float32)
    (d_query, d_pairs), _ = lax.scan(grad_step, (start_query, start_pairs), jnp.arange(block_total))
    own_pairs = lax.psum_scatter(d_pairs, "row", scatter_dimension=1, tiled=True).astype(
        jnp.bfloat16
    )
    d_q = d_query.reshape(table_count, local_rows, dmodel).astype(jnp.bfloat16)
    grad_w_qkv = jnp.concatenate(
        [
            jnp.einsum("trd,tre->de", attn_in, d_q, preferred_element_type=jnp.float32),
            jnp.einsum(
                "trd,tre->de", attn_in[:, :ctx_rows], own_pairs, preferred_element_type=jnp.float32
            ),
        ],
        axis=1,
    )
    d_from_query = jnp.einsum("tre,de->trd", d_q, w_query, preferred_element_type=jnp.float32)
    d_from_pairs = jnp.einsum("tre,de->trd", own_pairs, w_pair, preferred_element_type=jnp.float32)
    d_attn_in = jnp.concatenate(
        [d_from_query[:, :ctx_rows] + d_from_pairs, d_from_query[:, ctx_rows:]], axis=1
    )
    d_norm1, grad_ln1_gain, grad_ln1_bias = norm_back(d_attn_in, normed1, inverse1, ln1_gain)
    d_embed = (d_mixed + d_norm1).astype(jnp.bfloat16)
    grad_w_emb = jnp.einsum("tfr,trd->fd", features, d_embed, preferred_element_type=jnp.float32)
    d_features = jnp.einsum("trd,fd->tfr", d_embed, w_emb, preferred_element_type=jnp.float32)
    d_features = (d_features * slot_live[:, :, None].astype(jnp.float32)).astype(jnp.bfloat16)
    ctx_feat_grad = d_features[:, :, :ctx_rows]
    qry_feat_grad = d_features[:, :, ctx_rows:]
    (
        qkv_part,
        out_part,
        up_part,
        down_part,
        gain1_part,
        bias1_part,
        gain2_part,
        bias2_part,
        upbias_part,
    ) = (
        lax.psum_scatter(grad_w_qkv, "row", scatter_dimension=0, tiled=True),
        lax.psum_scatter(grad_w_out, "row", scatter_dimension=0, tiled=True),
        lax.psum_scatter(grad_w_up, "row", scatter_dimension=0, tiled=True),
        lax.psum_scatter(grad_w_down, "row", scatter_dimension=0, tiled=True),
        lax.psum_scatter(grad_ln1_gain, "row", scatter_dimension=0, tiled=True),
        lax.psum_scatter(grad_ln1_bias, "row", scatter_dimension=0, tiled=True),
        lax.psum_scatter(grad_ln2_gain, "row", scatter_dimension=0, tiled=True),
        lax.psum_scatter(grad_ln2_bias, "row", scatter_dimension=0, tiled=True),
        lax.psum_scatter(grad_b_up, "row", scatter_dimension=0, tiled=True),
    )
    qkv_all, out_all, up_all, down_all, gain1_all, bias1_all, gain2_all, bias2_all, upbias_all = (
        lax.psum(qkv_part.astype(jnp.bfloat16), "tab").astype(jnp.float32),
        lax.psum(out_part.astype(jnp.bfloat16), "tab").astype(jnp.float32),
        lax.psum(up_part.astype(jnp.bfloat16), "tab").astype(jnp.float32),
        lax.psum(down_part.astype(jnp.bfloat16), "tab").astype(jnp.float32),
        lax.psum(gain1_part.astype(jnp.bfloat16), "tab").astype(jnp.float32),
        lax.psum(bias1_part.astype(jnp.bfloat16), "tab").astype(jnp.float32),
        lax.psum(gain2_part.astype(jnp.bfloat16), "tab").astype(jnp.float32),
        lax.psum(bias2_part.astype(jnp.bfloat16), "tab").astype(jnp.float32),
        lax.psum(upbias_part.astype(jnp.bfloat16), "tab").astype(jnp.float32),
    )
    embed_all, squares_all, count_all = lax.psum((grad_w_emb, squares, live_rows), ("tab", "row"))
    rms = jnp.sqrt(squares_all / (count_all * dmodel))
    return (
        ctx_out,
        qry_out,
        ctx_feat_grad,
        qry_feat_grad,
        embed_all,
        gain1_all,
        bias1_all,
        qkv_all,
        out_all,
        gain2_all,
        bias2_all,
        up_all,
        upbias_all,
        down_all,
        rms,
    )


MESH = pl.DeviceIdType.MESH
LANES = 128
NT = (((1,), (1,)), ((), ()))


def lane_of(shape):
    return lax.broadcasted_iota(jnp.int32, shape, len(shape) - 1)


def split_three(values):
    high = values.astype(jnp.bfloat16)
    rest = values - high.astype(jnp.float32)
    mid = rest.astype(jnp.bfloat16)
    tail = (rest - mid.astype(jnp.float32)).astype(jnp.bfloat16)
    return (high, mid, tail)


def set_lanes(values, first, columns):
    lane = lane_of(values.shape)
    values = values.astype(jnp.float32)
    for i, column in enumerate(columns):
        values = jnp.where(lane == first + i, column.astype(jnp.float32), values)
    return values.astype(jnp.bfloat16)


def greet(peers):
    barrier = pltpu.get_barrier_semaphore()
    for peer in peers:
        pl.semaphore_signal(barrier, inc=1, device_id=peer, device_id_type=MESH)
    pl.semaphore_wait(barrier, len(peers))


def front_kernel(
    dims, counts, own_feat, w_emb, gain, bias, w_qkv,
    out_in, queries_out, keys_out, values_out, outs_out, feat_out, w_out,
    feat_in, window, w_lanes, w_mine, queries, keys, values, outs, packed, load_sem, store_sem, send_sem, recv_sem,
):
    row_size, x_size, chunk, ctx_rows, local_rows, heads, groups = dims
    z_size = row_size // x_size
    total = keys.shape[1]
    pair = x_size * local_rows
    dmodel = w_emb.shape[1]
    width = heads * HEAD_DIM
    tab, row = lax.axis_index("tab"), lax.axis_index("row")
    z = row // x_size
    table, group = row // groups, lax.rem(row, groups)
    row_peers = [(tab, lax.rem(row + k, row_size)) for k in range(1, row_size)]
    numbers = {}

    def remote(name, src, dst, peer):
        i = numbers.setdefault(name, len(numbers))
        return pltpu.make_async_remote_copy(
            src_ref=src, dst_ref=dst, send_sem=send_sem.at[i], recv_sem=recv_sem.at[i],
            device_id=peer, device_id_type=MESH,
        )

    def feat_copy(k):
        peer = row_peers[k]
        return remote(("feat", k), own_feat.at[peer[1] // groups], feat_in.at[row], peer)

    def out_copy(shift):
        p = lax.rem(row + shift, row_size)
        return remote(("out", shift), packed.at[p], out_in.at[row], (tab, p))

    span = window.shape[2]
    first = (group * width) // LANES * LANES

    def window_copy(n):
        at = pl.ds(pl.multiple_of(n * dmodel + first, LANES), span)
        return pltpu.make_async_copy(w_qkv.at[:, at], window.at[n], load_sem.at[n])

    for n in range(3):
        window_copy(n).start()
    greet(row_peers)
    for k in range(row_size - 1):
        feat_copy(k).start()
    feat_in[row] = own_feat[table]
    offset = group * width - first
    for n in range(3):
        window_copy(n).wait()
        wide = window[n]
        mine = wide[:, :width]
        for shift in range(HEAD_DIM, span - width + 1, HEAD_DIM):
            mine = jnp.where(offset == shift, wide[:, shift : shift + width], mine)
        w_mine[:, n * width : (n + 1) * width] = mine
        for h in range(heads):
            one = mine[:, h * HEAD_DIM : (h + 1) * HEAD_DIM]
            at = (n * heads + h) * LANES
            w_lanes[:, at : at + LANES] = jnp.concatenate([one, jnp.zeros_like(one)], axis=1)
    w_store = pltpu.make_async_copy(w_mine, w_out, store_sem.at[0])
    w_store.start()
    count = counts[table]

    def project(step, _):
        there = lax.rem(z + step, z_size)
        embeds = []
        for other in range(x_size):
            p = there * x_size + other
            shift = lax.rem(p - row + row_size, row_size)
            for s in range(1, row_size):

                @pl.when(shift == s)
                def _():
                    feat_copy(row_size - s - 1).wait_recv()

            embeds.append(feat_in[p])
        rows_feat = jnp.concatenate(embeds, axis=0)
        embed = jnp.dot(rows_feat, w_emb[...], preferred_element_type=jnp.float32)
        center = embed - jnp.mean(embed, axis=-1, keepdims=True)
        inverse = lax.rsqrt(jnp.mean(center * center, axis=-1, keepdims=True) + EPS)
        attn_in = (center * inverse * gain[...] + bias[...]).astype(jnp.bfloat16)
        projected = jnp.dot(attn_in, w_lanes[...], preferred_element_type=jnp.float32)
        rows = pl.ds(pl.multiple_of(there * pair, LANES), pair)
        lane = lane_of((pair, LANES))
        for h in range(heads):
            query = projected[:, h * LANES : (h + 1) * LANES] * HEAD_DIM ** (-0.5)
            queries[h, rows] = jnp.where(lane == HEAD_DIM, 1.0, query).astype(jnp.bfloat16)
        lane = lane_of((ctx_rows, LANES))
        for other in range(x_size):
            p = there * x_size + other
            key_rows = pl.ds(pl.multiple_of(p * ctx_rows, LANES), ctx_rows)
            position = p * ctx_rows + lax.broadcasted_iota(jnp.int32, (ctx_rows, LANES), 0)
            mask = jnp.where(position < count, 0.0, NEGATIVE)
            for h in range(heads):
                at = (heads + h) * LANES
                key = projected[other * local_rows : other * local_rows + ctx_rows, at : at + LANES]
                key = jnp.where(lane == HEAD_DIM, mask, key)
                key = jnp.where((lane > HEAD_DIM) & (lane < HEAD_DIM + 4), 1.0, key)
                keys[h, key_rows] = key.astype(jnp.bfloat16)
                at = (2 * heads + h) * LANES
                value = projected[other * local_rows : other * local_rows + ctx_rows, at : at + LANES]
                value = jnp.where((lane >= HEAD_DIM) & (lane < HEAD_DIM + 3), 1.0, value)
                values[h, key_rows] = value.astype(jnp.bfloat16)
        return 0

    lax.fori_loop(0, z_size, project, 0)
    stores = [
        pltpu.make_async_copy(src, dst, store_sem.at[i + 1])
        for i, (src, dst) in enumerate(((keys, keys_out), (values, values_out), (feat_in, feat_out)))
    ]
    for store in stores:
        store.start()
    whole = heads // 2

    def segment(step, _):
        k, h = step // heads, lax.rem(step, heads)
        there = lax.rem(z + k + 1, z_size)
        rows = pl.ds(pl.multiple_of(there * pair, LANES), pair)
        query = queries[h, rows]
        for i in range(total // chunk):
            at = pl.ds(i * chunk, chunk)
            scores = lax.dot_general(query, keys[h, at], NT, preferred_element_type=jnp.float32)
            top = jnp.max(scores, axis=-1, keepdims=True)
            if i:
                top = jnp.maximum(top, before)
            weights = jnp.exp(scores - top).astype(jnp.bfloat16)
            term = jnp.dot(weights, values[h, at], preferred_element_type=jnp.float32)
            summed = summed * jnp.exp(before - top) + term if i else term
            before = top
        sum_all = summed[:, HEAD_DIM : HEAD_DIM + 1]
        outs[h, rows] = (summed / sum_all).astype(jnp.bfloat16)
        queries[h, rows] = set_lanes(query, HEAD_DIM + 1, split_three(-(top + jnp.log(sum_all))))

        @pl.when(h == heads - 1)
        def _():
            for other in range(x_size):
                p = there * x_size + other
                at = pl.ds(pl.multiple_of(p * local_rows, 16), local_rows)
                parts = [outs[i, at, :HEAD_DIM] for i in range(heads)]
                for i in range(whole):
                    both = jnp.concatenate([parts[2 * i], parts[2 * i + 1]], axis=1)
                    packed[p, i * local_rows : (i + 1) * local_rows] = both
                if heads % 2:
                    last = parts[-1]
                    both = jnp.concatenate([last[: local_rows // 2], last[local_rows // 2 :]], axis=1)
                    packed[p, whole * local_rows :] = both
                ahead = lax.rem(p - row + row_size, row_size)
                for s in range(1, row_size):

                    @pl.when(ahead == s)
                    def _():
                        out_copy(s).start()

        return 0

    lax.fori_loop(0, z_size * heads, segment, 0)
    last = [
        pltpu.make_async_copy(queries, queries_out, store_sem.at[4]),
        pltpu.make_async_copy(outs, outs_out, store_sem.at[5]),
        pltpu.make_async_copy(packed.at[row], out_in.at[row], store_sem.at[6]),
    ]
    for store in last:
        store.start()
    for k in range(row_size - 1):
        feat_copy(k).wait_send()
    for store in [w_store] + stores + last:
        store.wait()
    for s in range(1, row_size):
        out_copy(s).wait()


def front(counts, own_feat, w_emb, gain, bias, w_qkv, total_ctx, heads, groups, chunk, collective_id):
    row_size = lax.axis_size("row")
    _, local_rows, slots = own_feat.shape
    dmodel = w_emb.shape[1]
    ctx_rows = total_ctx // row_size
    width = heads * HEAD_DIM
    x_size = 2
    span = -(-(width + (HEAD_DIM if width % LANES else 0)) // LANES) * LANES
    bf16 = lambda *shape: (shape, jnp.bfloat16)
    by_query, by_key = (heads, row_size * local_rows, LANES), (heads, total_ctx, LANES)
    block = (row_size, -(-heads * local_rows // 2), LANES)
    feat = (row_size, local_rows, slots)
    vmem = pl.BlockSpec(memory_space=pltpu.VMEM)
    anywhere = pl.BlockSpec(memory_space=pl.ANY)
    scratch = [
        feat, (3, dmodel, span), (dmodel, 3 * heads * LANES), (dmodel, 3 * width),
        by_query, by_key, by_key, by_query, block,
    ]
    return pl.pallas_call(
        functools.partial(front_kernel, (row_size, x_size, chunk, ctx_rows, local_rows, heads, groups)),
        out_shape=[
            jax.ShapeDtypeStruct(s, jnp.bfloat16)
            for s in (block, by_query, by_key, by_key, by_query, feat, (dmodel, 3 * width))
        ],
        in_specs=[pl.BlockSpec(memory_space=pltpu.SMEM)] + [vmem] * 4 + [anywhere],
        out_specs=[anywhere] * 7,
        scratch_shapes=[pltpu.VMEM(s, jnp.bfloat16) for s in scratch] + [
            pltpu.SemaphoreType.DMA((3,)),
            pltpu.SemaphoreType.DMA((7,)),
            pltpu.SemaphoreType.DMA((2 * (row_size - 1),)),
            pltpu.SemaphoreType.DMA((2 * (row_size - 1),)),
        ],
        compiler_params=pltpu.CompilerParams(
            collective_id=collective_id, has_side_effects=True, vmem_limit_bytes=60 * 2**20
        ),
        name="front",
    )(counts, own_feat, w_emb, gain, bias, w_qkv)


def gelu_parts(values):
    below = 0.5 + 0.5 * lax.erf(values * math.sqrt(0.5))
    return (below, values * jnp.exp(-0.5 * values * values) * (1.0 / math.sqrt(2.0 * math.pi)))


def middle_kernel(
    dims, ctx_count, qry_count, own_feat, w_emb, gain, bias, b_up, out_in, w_out_hbm, w_up_hbm, w_down_hbm, ctx_cot, qry_cot,
    ctx_out, qry_out, g_in, up_half, down_half, out_half, d_branch_out, vectors, sums,
    w_out, w_up, w_down, attn_in, cot, attn_low, mlp_in, mlp_in_t, mixed, normed, d_mlp_in, act, d_hidden, d_up_bias,
    packed, up, down, out, up_in0, down_in0, out_in0, load_sem, store_sem, send_sem, recv_sem,
):
    row_size, ctx_rows, local_rows, tables, groups, heads, tile = dims
    rows = tables * local_rows
    qry_rows = local_rows - ctx_rows
    dmodel, hidden_size = w_up.shape
    tiles = hidden_size // tile
    tab, row = lax.axis_index("tab"), lax.axis_index("row")
    core = lax.rem(tab, 2)
    core_peer = (tab ^ 1, row)
    row_peers = [(tab, lax.rem(row + k, row_size)) for k in range(1, row_size)]
    numbers = {}

    def remote(name, src, dst, peer):
        i = numbers.setdefault(name, len(numbers))
        return pltpu.make_async_remote_copy(
            src_ref=src, dst_ref=dst, send_sem=send_sem.at[i], recv_sem=recv_sem.at[i],
            device_id=peer, device_id_type=MESH,
        )

    loads = [
        pltpu.make_async_copy(src, dst, load_sem.at[i])
        for i, (src, dst) in enumerate(
            [(out_in, attn_in), (w_out_hbm, w_out), (w_up_hbm, w_up), (w_down_hbm, w_down)]
            + [(ctx_cot.at[t], cot.at[pl.ds(t * local_rows, ctx_rows)]) for t in range(tables)]
            + [(qry_cot.at[t], cot.at[pl.ds(t * local_rows + ctx_rows, qry_rows)]) for t in range(tables)]
        )
    ]
    for load in loads:
        load.start()
    greet([core_peer] + row_peers)

    at = lax.broadcasted_iota(jnp.int32, (local_rows, 1), 0)
    live = []
    for t in range(tables):
        place = jnp.where(at < ctx_rows, row * ctx_rows + at, row * qry_rows + at - ctx_rows)
        limit = jnp.where(at < ctx_rows, ctx_count[t], qry_count[t])
        live.append(jnp.where(place < limit, 1.0, 0.0))
    valid = jnp.concatenate(live, axis=0)
    own_rows = jnp.concatenate([own_feat[t] for t in range(tables)], axis=0)
    embed = jnp.dot(own_rows, w_emb[...], preferred_element_type=jnp.float32)

    whole = heads // 2
    loads[0].wait()
    for t in range(tables):
        parts = []
        for g in range(groups):
            block = attn_in[t * groups + g]
            for h in range(whole):
                parts.append(block[h * local_rows : (h + 1) * local_rows])
            if heads % 2:
                last = block[whole * local_rows :]
                parts.append(jnp.concatenate([last[:, :HEAD_DIM], last[:, HEAD_DIM:]], axis=0))
        attn_low[t * local_rows : (t + 1) * local_rows] = jnp.concatenate(parts, axis=1)
    loads[1].wait()
    branch = jnp.dot(attn_low[...], w_out[...], preferred_element_type=jnp.float32)
    summed = embed + branch
    mixed[...] = summed
    square_embed = jnp.sum(valid * embed * embed)
    square_branch = jnp.sum(valid * branch * branch)
    center = summed - jnp.mean(summed, axis=-1, keepdims=True)
    inverse = lax.rsqrt(jnp.mean(center * center, axis=-1, keepdims=True) + EPS)
    normed[...] = center * inverse
    mlp_in[...] = (normed[...] * gain[...] + bias[...]).astype(jnp.bfloat16)
    for load in loads[2:]:
        load.wait()
    cot[...] = (cot[...].astype(jnp.float32) * valid).astype(jnp.bfloat16)
    d_mlp_in[...] = jnp.zeros_like(d_mlp_in)

    def columns(i):
        return pl.ds(pl.multiple_of(i * tile, LANES), tile)

    def first(i, _):
        at = columns(i)
        hidden = jnp.dot(mlp_in[...], w_up[:, at], preferred_element_type=jnp.float32) + b_up[:, at]
        d_act = lax.dot_general(cot[...], w_down[at], NT, preferred_element_type=jnp.float32)
        below, slope = gelu_parts(hidden)
        act[:, at] = (hidden * below).astype(jnp.bfloat16)
        grad = (d_act * (below + slope)).astype(jnp.bfloat16)
        d_hidden[:, at] = grad
        d_up_bias[:, at] = jnp.sum(grad.astype(jnp.float32), axis=0, keepdims=True)
        d_mlp_in[...] += lax.dot_general(grad, w_up[:, at], NT, preferred_element_type=jnp.float32)
        return 0

    lax.fori_loop(0, tiles, first, 0)
    grad_in = d_mlp_in[...]
    scaled = grad_in * gain[...]
    inner = (
        scaled
        - jnp.mean(scaled, axis=-1, keepdims=True)
        - normed[...] * jnp.mean(scaled * normed[...], axis=-1, keepdims=True)
    )
    vectors[...] = jnp.zeros_like(vectors)
    vectors[2:3] = jnp.sum(grad_in * normed[...], axis=0, keepdims=True)
    vectors[3:4] = jnp.sum(grad_in, axis=0, keepdims=True)
    for i in range(hidden_size // dmodel):
        vectors[4 + i : 5 + i] = d_up_bias[:, i * dmodel : (i + 1) * dmodel]
    d_branch = (cot[...].astype(jnp.float32) + inverse * inner).astype(jnp.bfloat16)
    for t in range(tables):
        d_branch_out[t] = d_branch[t * local_rows : (t + 1) * local_rows]
    d_attn = lax.dot_general(d_branch, w_out[...], NT, preferred_element_type=jnp.float32).astype(jnp.bfloat16)
    width = heads * HEAD_DIM
    for t in range(tables):
        for g in range(groups):
            block = d_attn[t * local_rows : (t + 1) * local_rows, g * width : (g + 1) * width]
            p = t * groups + g
            for h in range(whole):
                packed[p, h * local_rows : (h + 1) * local_rows] = block[:, h * LANES : (h + 1) * LANES]
            if heads % 2:
                last = block[:, whole * LANES :]
                both = jnp.concatenate([last[: local_rows // 2], last[local_rows // 2 :]], axis=1)
                packed[p, whole * local_rows :] = both
    own_g = pltpu.make_async_copy(packed.at[row], g_in.at[row], store_sem.at[0])
    own_g.start()
    g_copies = [remote(("g", k), packed.at[peer[1]], g_in.at[row], peer) for k, peer in enumerate(row_peers)]
    for copy in g_copies:
        copy.start()

    def half(ref, which):
        size = ref.shape[1] // 2
        return pl.ds(pl.multiple_of(which * size, 16), size)

    shard = dmodel // row_size
    d_out = jnp.dot(attn_low[...].T, d_branch, preferred_element_type=jnp.float32).astype(jnp.bfloat16)
    for p in range(row_size):
        out[p] = d_out[p * shard : (p + 1) * shard]
    out_copy = remote("out", out.at[:, half(out, 1 - core)], out_in0, core_peer)
    out_copy.start()
    mlp_in_t[...] = mlp_in[...].T
    d_mlp_in[...] = jnp.zeros_like(d_mlp_in)
    per = hidden_size // row_size

    def second(p, _):
        at = pl.ds(pl.multiple_of(p * per, LANES), per)
        piece = act[:, at]
        d_mlp_in[...] += jnp.dot(piece, w_down[at], preferred_element_type=jnp.float32)
        down[p] = jnp.dot(piece.T, cot[...], preferred_element_type=jnp.float32).astype(jnp.bfloat16)
        d_up = jnp.dot(mlp_in_t[...], d_hidden[:, at], preferred_element_type=jnp.float32).astype(jnp.bfloat16)
        for q in range(row_size):
            up[q, :, at] = d_up[q * shard : (q + 1) * shard]
        return 0

    lax.fori_loop(0, row_size, second, 0)
    copies = [
        remote("up", up.at[:, half(up, 1 - core)], up_in0, core_peer),
        remote("down", down.at[:, half(down, 1 - core)], down_in0, core_peer),
    ]
    for copy in copies:
        copy.start()
    mlp = d_mlp_in[...]
    result = (mixed[...] + mlp) * valid
    square_mlp = jnp.sum(valid * mlp * mlp)
    square_result = jnp.sum(result * result)
    low = result.astype(jnp.bfloat16)
    for t in range(tables):
        ctx_out[t] = low[t * local_rows : t * local_rows + ctx_rows]
        qry_out[t] = low[t * local_rows + ctx_rows : (t + 1) * local_rows]
    lane = lane_of(sums.shape)
    parts = (square_embed, square_branch, square_mlp, square_result, jnp.sum(valid))
    total = jnp.zeros(sums.shape, jnp.float32)
    for i, part in enumerate(parts):
        total = jnp.where(lane == i, part, total)
    sums[...] = total
    stores = []
    for i, (copy, mine, taken, result_hbm) in enumerate(
        ((out_copy, out, out_in0, out_half), (copies[1], down, down_in0, down_half), (copies[0], up, up_in0, up_half))
    ):
        copy.wait()

        @pl.loop(0, row_size)
        def _(p):
            taken[p] = taken[p] + mine[p, half(mine, core)]

        store = pltpu.make_async_copy(taken, result_hbm, store_sem.at[i + 1])
        store.start()
        stores.append(store)
    for store in stores + [own_g]:
        store.wait()
    for copy in g_copies:
        copy.wait()


def middle(ctx_count, qry_count, own_feat, w_emb, gain, bias, b_up, out_in, w_out, w_up, w_down, ctx_cot, qry_cot,
           groups, heads, tile, collective_id):
    row_size = lax.axis_size("row")
    tables, local_rows, _ = own_feat.shape
    ctx_rows = ctx_cot.shape[1]
    rows = tables * local_rows
    dmodel, hidden_size = w_up.shape
    shard, per = dmodel // row_size, hidden_size // row_size
    halves = [(row_size, shard // 2, hidden_size), (row_size, per // 2, dmodel), (row_size, shard // 2, dmodel)]
    vmem = pl.BlockSpec(memory_space=pltpu.VMEM)
    smem = pl.BlockSpec(memory_space=pltpu.SMEM)
    anywhere = pl.BlockSpec(memory_space=pl.ANY)
    bf16 = lambda *shape: pltpu.VMEM(shape, jnp.bfloat16)
    f32 = lambda *shape: pltpu.VMEM(shape, jnp.float32)
    sends = row_size - 1 + 3
    return pl.pallas_call(
        functools.partial(middle_kernel, (row_size, ctx_rows, local_rows, tables, groups, heads, tile)),
        out_shape=[jax.ShapeDtypeStruct(s, jnp.bfloat16) for s in (ctx_cot.shape, qry_cot.shape, out_in.shape, *halves)]
        + [jax.ShapeDtypeStruct((tables, local_rows, dmodel), jnp.bfloat16)]
        + [jax.ShapeDtypeStruct((4 + hidden_size // dmodel, dmodel), jnp.float32)]
        + [jax.ShapeDtypeStruct((8, LANES), jnp.float32)],
        in_specs=[smem] * 2 + [vmem] * 5 + [anywhere] * 6,
        out_specs=[vmem] * 2 + [anywhere] * 4 + [vmem] * 3,
        scratch_shapes=[
            bf16(*w_out.shape), bf16(*w_up.shape), bf16(*w_down.shape), bf16(*out_in.shape), bf16(rows, dmodel),
            bf16(rows, dmodel), bf16(rows, dmodel), bf16(dmodel, rows),
            f32(rows, dmodel), f32(rows, dmodel), f32(rows, dmodel),
            bf16(rows, hidden_size), bf16(rows, hidden_size), f32(1, hidden_size),
            bf16(*out_in.shape),
            bf16(row_size, shard, hidden_size), bf16(row_size, per, dmodel), bf16(row_size, shard, dmodel),
            *[bf16(*s) for s in halves],
            pltpu.SemaphoreType.DMA((4 + 2 * tables,)),
            pltpu.SemaphoreType.DMA((4,)),
            pltpu.SemaphoreType.DMA((sends,)),
            pltpu.SemaphoreType.DMA((sends,)),
        ],
        compiler_params=pltpu.CompilerParams(
            collective_id=collective_id, has_side_effects=True, vmem_limit_bytes=62 * 2**20
        ),
        name="middle",
    )(ctx_count, qry_count, own_feat, w_emb, gain, bias, b_up, out_in, w_out, w_up, w_down, ctx_cot, qry_cot)


def tile_sum(parts):
    total = parts[0]
    for part in parts[1:]:
        total = total + part
    return total


def back_kernel(
    dims, counts, up0, down0, out0, queries_hbm, keys_hbm, values_hbm, outs_hbm, g_in, feat, w_emb, w_mine, gain, bias,
    own_feat, d_branch, vectors, sums,
    ctx_grad, qry_grad, emb_all, sums_all, qkv_all, out_all, up_all, down_all,
    queries, keys, values, outs, up_own, down_own, out_own, up1, down1, out1, up2, down2, out2,
    up3, down3, out3, up4, down4, out4, grads, d_q, d_kt, d_vt, d_k, d_v, terms, terms_in, d_qkv, d_emb, d_gain, d_bias,
    qkv_own, emb_own, qkv_in0, emb_in0, sums_in0, sums0, qkv_in1, emb_in1, sums_in1,
    qkv1, emb1, sums1, qkv_in2, emb_in2, sums_in2, qkv2, emb2, emb3,
    load_sem, send_sem, recv_sem,
):
    row_size, x_size, chunk, ctx_rows, local_rows = dims
    z_size = row_size // x_size
    heads, total, _ = keys.shape
    pair = x_size * local_rows
    tab, row = lax.axis_index("tab"), lax.axis_index("row")
    core, y = lax.rem(tab, 2), tab // 2
    x, z = lax.rem(row, x_size), row // x_size
    core_peer, y_peer, x_peer = (tab ^ 1, row), (tab ^ 2, row), (tab, row ^ 1)
    row_peers = [(tab, lax.rem(row + k, row_size)) for k in range(1, row_size)]
    z_peers = [(tab, lax.rem(z + k, z_size) * x_size + x) for k in range(1, z_size)]
    numbers = {}

    def remote(name, src, dst, peer):
        i = numbers.setdefault(name, len(numbers))
        return pltpu.make_async_remote_copy(
            src_ref=src, dst_ref=dst, send_sem=send_sem.at[i], recv_sem=recv_sem.at[i],
            device_id=peer, device_id_type=MESH,
        )

    def half(rows, which):
        return pl.ds(pl.multiple_of(which * (rows // 2), 16), rows // 2)

    def columns(ref, which):
        wide = ref.shape[-1] // 2
        return pl.ds(pl.multiple_of(which * wide, LANES), wide)

    def by_z(ref):
        return ref.reshape(z_size, x_size, *ref.shape[1:])

    loads = [
        pltpu.make_async_copy(src, dst, load_sem.at[i])
        for i, (src, dst) in enumerate(
            (
                (queries_hbm, queries),
                (keys_hbm, keys),
                (values_hbm, values),
                (outs_hbm, outs),
                (up0.at[:, :, columns(up0, y)], up_own),
                (by_z(down0).at[:, x], down_own),
                (by_z(out0).at[:, x], out_own),
            )
        )
    ]

    def up_y():
        return [remote("up_y", up0.at[:, :, columns(up0, 1 - y)], up1, y_peer)]

    def down_x():
        return [
            remote("down_x", by_z(down0).at[:, 1 - x], down1, x_peer),
            remote("out_x", by_z(out0).at[:, 1 - x], out1, x_peer),
        ]

    def up_x():
        return [remote("up_x", by_z(up1).at[:, 1 - x], up2, x_peer)]

    def down_y():
        return [
            remote("down_y", down1.at[:, :, columns(down1, 1 - y)], down2, y_peer),
            remote("out_y", out1.at[:, :, columns(out1, 1 - y)], out2, y_peer),
        ]

    def over_z(name, src, dst):
        return [
            remote((name, k), src.at[lax.rem(z + k + 1, z_size)], dst.at[k], peer)
            for k, peer in enumerate(z_peers)
        ]

    def up_z():
        return over_z("up_z", up2, up3)

    def down_z():
        return over_z("down_z", down2, down3) + over_z("out_z", out2, out3)

    lasts = (up4, down4, out4)

    def to_y():
        return [remote(("to_y", i), last.at[core, y], last.at[core, y], y_peer) for i, last in enumerate(lasts)]

    def to_core(which):
        at = y if which == 0 else 1 - y
        return [
            remote(("to_core", which, i), last.at[core, at], last.at[core, at], core_peer)
            for i, last in enumerate(lasts)
        ]

    def start(copies):
        for copy in copies:
            copy.start()

    def wait(copies):
        for copy in copies:
            copy.wait()

    start(loads)
    greet([core_peer, y_peer] + row_peers)
    start(up_y())
    start(down_x())

    def up_y_done():
        wait(loads[4:5])
        wait(up_y())

        @pl.loop(0, row_size)
        def _(p):
            up1[p] = up1[p] + up_own[p]

        start(up_x())

    def down_x_done():
        wait(loads[5:])
        wait(down_x())

        @pl.loop(0, z_size)
        def _(p):
            down1[p] = down1[p] + down_own[p]
            out1[p] = out1[p] + out_own[p]

        start(down_y())

    def up_x_done():
        wait(up_x())

        @pl.loop(0, z_size)
        def _(p):
            up2[p] = up2[p] + up1[p * x_size + x]

        start(up_z())

    def down_y_done():
        wait(down_y())

        @pl.loop(0, z_size)
        def _(p):
            down2[p] = down2[p] + down1[p, :, columns(down1, y)]
            out2[p] = out2[p] + out1[p, :, columns(out1, y)]

        start(down_z())

    d_kt[...] = jnp.zeros_like(d_kt)
    d_vt[...] = jnp.zeros_like(d_vt)
    whole = heads // 2

    def unpack(p):
        packed = g_in[p]
        parts = []
        for h in range(whole):
            tile = packed[h * local_rows : (h + 1) * local_rows]
            parts += [tile[:, :HEAD_DIM], tile[:, HEAD_DIM:]]
        if heads % 2:
            tile = packed[whole * local_rows :]
            parts.append(jnp.concatenate([tile[:, :HEAD_DIM], tile[:, HEAD_DIM:]], axis=0))
        rows = pl.ds(pl.multiple_of(p * local_rows, 16), local_rows)
        for h, part in enumerate(parts):
            part = part.astype(jnp.float32)
            result = outs[h, rows, :HEAD_DIM].astype(jnp.float32)
            inner = jnp.sum(part * result, axis=-1, keepdims=True)
            wide = jnp.concatenate([part, jnp.zeros_like(part)], axis=-1)
            grads[h, rows] = set_lanes(wide, HEAD_DIM, split_three(-inner))

    def segment(step, _):
        k, h = step // heads, lax.rem(step, heads)
        there = lax.rem(z + k, z_size)
        rows = pl.ds(pl.multiple_of(there * pair, LANES), pair)

        @pl.when(h == 0)
        def _():
            for other in range(x_size):
                p = there * x_size + other
                unpack(p)

        @pl.when(step == 2 * heads + 2)
        def _():
            up_y_done()

        query, grad = queries[h, rows], grads[h, rows]
        query_t = query[:, :HEAD_DIM].T
        grad_t = grad[:, :HEAD_DIM].T
        d_query = jnp.zeros((pair, LANES), jnp.float32)
        for i in range(total // chunk):
            at = pl.ds(i * chunk, chunk)
            key, value = keys[h, at], values[h, at]
            probs = jnp.exp(lax.dot_general(query, key, NT, preferred_element_type=jnp.float32))
            d_probs = lax.dot_general(grad, value, NT, preferred_element_type=jnp.float32)
            d_scores = (probs * d_probs).astype(jnp.bfloat16)
            d_vt[h, :, at] += jnp.dot(grad_t, probs.astype(jnp.bfloat16), preferred_element_type=jnp.float32)
            d_kt[h, :, at] += jnp.dot(query_t, d_scores, preferred_element_type=jnp.float32)
            d_query += jnp.dot(d_scores, key, preferred_element_type=jnp.float32)
        d_q[h, rows] = (d_query[:, :HEAD_DIM] * HEAD_DIM ** (-0.5)).astype(jnp.bfloat16)
        return 0

    wait(loads[:4])
    lax.fori_loop(0, z_size * heads, segment, 0)
    down_x_done()
    for h in range(heads):
        d_k[h] = d_kt[h].T.astype(jnp.bfloat16)
        d_v[h] = d_vt[h].T.astype(jnp.bfloat16)

    d_qkv[...] = jnp.zeros_like(d_qkv)
    d_emb[...] = jnp.zeros_like(d_emb)
    d_gain[...] = jnp.zeros_like(d_gain)
    d_bias[...] = jnp.zeros_like(d_bias)

    def term_copy(shift):
        p = lax.rem(row + shift, row_size)
        return remote(("term", shift), terms.at[p], terms_in.at[row], (tab, p))

    def project(step, _):
        shift = lax.rem(step + 1, z_size)
        there = lax.rem(z + shift, z_size)
        pieces, embeds = [], []
        for other in range(x_size):
            p = there * x_size + other
            rows = pl.ds(pl.multiple_of(p * local_rows, 16), local_rows)
            key_rows = pl.ds(pl.multiple_of(p * ctx_rows, 16), ctx_rows)
            parts = [d_q[h, rows] for h in range(heads)]
            nothing = jnp.zeros((local_rows - ctx_rows, HEAD_DIM), jnp.bfloat16)
            for ref in (d_k, d_v):
                parts += [jnp.concatenate([ref[h, key_rows], nothing], axis=0) for h in range(heads)]
            pieces.append(jnp.concatenate(parts, axis=1))
            embeds.append(feat[p])
        d_three = jnp.concatenate(pieces, axis=0)
        rows_feat = jnp.concatenate(embeds, axis=0)
        embed = jnp.dot(rows_feat, w_emb[...], preferred_element_type=jnp.float32)
        center = embed - jnp.mean(embed, axis=-1, keepdims=True)
        inverse = lax.rsqrt(jnp.mean(center * center, axis=-1, keepdims=True) + EPS)
        normed = center * inverse
        attn_in = (normed * gain[...] + bias[...]).astype(jnp.bfloat16)
        d_in = lax.dot_general(d_three, w_mine[...], NT, preferred_element_type=jnp.float32)
        d_gain[...] += jnp.sum(d_in * normed, axis=0, keepdims=True)
        d_bias[...] += jnp.sum(d_in, axis=0, keepdims=True)
        scaled = d_in * gain[...]
        inner = (
            scaled
            - jnp.mean(scaled, axis=-1, keepdims=True)
            - normed * jnp.mean(scaled * normed, axis=-1, keepdims=True)
        )
        d_norm = (inverse * inner).astype(jnp.bfloat16)
        term = lax.dot_general(d_norm, w_emb[...], NT, preferred_element_type=jnp.float32).astype(jnp.bfloat16)
        d_emb[...] += jnp.dot(rows_feat.T, d_norm, preferred_element_type=jnp.float32)
        d_qkv[...] += jnp.dot(attn_in.T, d_three, preferred_element_type=jnp.float32)
        for other in range(x_size):
            p = there * x_size + other
            terms[p] = term[other * local_rows : (other + 1) * local_rows]
            ahead = lax.rem(p - row + row_size, row_size)
            for s in range(1, row_size):

                @pl.when(ahead == s)
                def _():
                    term_copy(s).start()

        for at, act in ((1, up_x_done), (2, down_y_done)):

            @pl.when(step == at)
            def _():
                act()

        return 0

    lax.fori_loop(0, z_size, project, 0)

    shard = qkv_own.shape[1]
    for p in range(row_size):
        qkv_own[p] = d_qkv[p * shard : (p + 1) * shard].astype(jnp.bfloat16)
    own_rows = jnp.concatenate([own_feat[t] for t in range(own_feat.shape[0])], axis=0)
    own_d = jnp.concatenate([d_branch[t] for t in range(own_feat.shape[0])], axis=0)
    d_own = d_emb[...] + jnp.dot(own_rows.T, own_d, preferred_element_type=jnp.float32)
    slots = d_own.shape[0]
    spare = lax.broadcasted_iota(jnp.int32, d_own.shape, 0) - (slots - vectors.shape[0])
    d_own = jnp.where(spare == 0, d_gain[...], d_own)
    d_own = jnp.where(spare == 1, d_bias[...], d_own)
    for i in range(2, vectors.shape[0]):
        d_own = jnp.where(spare == i, vectors[i : i + 1], d_own)
    emb_rows = emb_own.shape[1]
    for p in range(row_size):
        emb_own[p] = d_own[p * emb_rows : (p + 1) * emb_rows].astype(jnp.bfloat16)

    def tail_core():
        return [
            remote("qkv_core", qkv_own.at[:, half(shard, 1 - core)], qkv_in0, core_peer),
            remote("emb_core", emb_own.at[:, :, columns(emb_own, 1 - core)], emb_in0, core_peer),
            remote("sums_core", sums, sums_in0, core_peer),
        ]

    def tail_row():
        copies = []
        for k, peer in enumerate(row_peers):
            copies += [
                remote(("qkv_row", k), qkv_in0.at[peer[1]], qkv_in1.at[row], peer),
                remote(("emb_row", k), emb_in0.at[peer[1]], emb_in1.at[row], peer),
                remote(("sums_row", k), sums0, sums_in1.at[row], peer),
            ]
        return copies

    start(tail_core())
    wait(tail_core())
    qkv_in0[...] = qkv_in0[...] + qkv_own[:, half(shard, core)]
    emb_in0[...] = emb_in0[...] + emb_own[:, :, columns(emb_own, core)]
    sums0[...] = sums[...] + sums_in0[...]
    start(tail_row())
    qkv_in1[row] = qkv_in0[row]
    emb_in1[row] = emb_in0[row]
    sums_in1[row] = sums0[...]

    terms_in[row] = terms[row]
    for s in range(1, row_size):
        term_copy(s).wait()
    groups = qkv1.shape[0]
    for t in range(own_feat.shape[0]):
        term = lax.dot_general(d_branch[t], w_emb[...], NT, preferred_element_type=jnp.float32)
        for g in range(groups):
            term = term + terms_in[t * groups + g].astype(jnp.float32)
        slot = lax.broadcasted_iota(jnp.int32, (term.shape[1], 1), 0)
        by_slot = (term.T * jnp.where(slot < counts[t], 1.0, 0.0)).astype(jnp.bfloat16)[: ctx_grad.shape[1]]
        ctx_grad[t] = by_slot[:, :ctx_rows]
        qry_grad[t] = by_slot[:, ctx_rows:]

    wait(up_z())
    wait(down_z())
    for part, taken, last in ((up2, up3, up4), (down2, down3, down4), (out2, out3, out4)):
        whole_sum = part[z].astype(jnp.float32)
        for k in range(z_size - 1):
            whole_sum = whole_sum + taken[k].astype(jnp.float32)
        last[core, y] = whole_sum.astype(jnp.bfloat16)
    start(to_y())
    start(to_core(0))

    wait(tail_row())
    for g in range(groups):
        qkv1[g] = tile_sum(
            [qkv_in1[g + t * groups].astype(jnp.float32) for t in range(row_size // groups)]
        ).astype(jnp.bfloat16)
    emb1[...] = tile_sum([emb_in1[p].astype(jnp.float32) for p in range(row_size)]).astype(jnp.bfloat16)
    sums1[...] = tile_sum([sums_in1[p] for p in range(row_size)])
    tail_y = [
        remote("qkv_y", qkv1, qkv_in2, y_peer),
        remote("emb_y", emb1, emb_in2, y_peer),
        remote("sums_y", sums1, sums_in2, y_peer),
    ]
    start(tail_y)
    wait(to_y())
    start(to_core(1))
    wait(tail_y)
    qkv2[core] = qkv1[...] + qkv_in2[...]
    emb2[:, columns(emb_own, core)] = emb1[...] + emb_in2[...]
    sums_all[...] = sums1[...] + sums_in2[...]
    at_core = columns(emb_own, core)
    tail_last = [
        remote("qkv_last", qkv2.at[core], qkv2.at[core], core_peer),
        remote("emb_last", emb2.at[:, at_core], emb2.at[:, at_core], core_peer),
    ]
    start(tail_last)
    wait(to_core(0))
    wait(to_core(1))
    wait(tail_last)
    emb_row = [remote(("emb_all", k), emb2, emb3.at[row], peer) for k, peer in enumerate(row_peers)]
    start(emb_row)
    emb3[row] = emb2[...]
    for last, result in ((up4, up_all), (down4, down_all), (out4, out_all)):
        rows, wide = last.shape[2:]
        for i in range(2):
            for j in range(2):
                result[i * rows : (i + 1) * rows, j * wide : (j + 1) * wide] = last[i, j].astype(jnp.float32)
    width = heads * HEAD_DIM
    for i in range(2):
        parts = [
            qkv2[i, g][:, n * width : (n + 1) * width].astype(jnp.float32) for n in range(3) for g in range(groups)
        ]
        qkv_all[i * (shard // 2) : (i + 1) * (shard // 2)] = jnp.concatenate(parts, axis=1)
    wait(emb_row)
    for p in range(row_size):
        emb_all[p * emb_rows : (p + 1) * emb_rows] = emb3[p].astype(jnp.float32)


def back(counts, halves, queries, keys, values, outs, g_in, feat, w_emb, w_mine, gain, bias, own_feat, d_branch,
         vectors, sums, slot_count, ctx_rows, groups, chunk, collective_id):
    row_size, local_rows, slots = feat.shape
    heads, total, _ = keys.shape
    all_rows = queries.shape[1]
    dmodel = w_emb.shape[1]
    width = heads * HEAD_DIM
    x_size = 2
    z_size = row_size // x_size
    shapes = [(2 * h.shape[1], h.shape[2]) for h in halves]
    bf16 = lambda *shape: pltpu.VMEM(shape, jnp.bfloat16)
    f32 = lambda *shape: pltpu.VMEM(shape, jnp.float32)
    (ru, wu), (rd, wd), (ro, wo) = shapes
    stage1 = [bf16(row_size, ru // 2, wu // 2), bf16(z_size, rd // 2, wd), bf16(z_size, ro // 2, wo)]
    stage2 = [bf16(z_size, r // 2, w // 2) for r, w in shapes]
    stage3 = [bf16(z_size - 1, r // 2, w // 2) for r, w in shapes]
    stage4 = [bf16(2, 2, r // 2, w // 2) for r, w in shapes]
    by_head = bf16(heads, all_rows, LANES)
    shard, emb_rows = dmodel // row_size, slots // row_size
    inputs = [by_head, bf16(*keys.shape), bf16(*keys.shape), by_head]
    attention = [
        by_head, bf16(heads, all_rows, HEAD_DIM),
        f32(heads, HEAD_DIM, total), f32(heads, HEAD_DIM, total),
        bf16(heads, total, HEAD_DIM), bf16(heads, total, HEAD_DIM),
        bf16(*feat.shape), bf16(*feat.shape),
        f32(dmodel, 3 * width), f32(slots, dmodel), f32(1, dmodel), f32(1, dmodel),
    ]
    half_qkv, half_emb = (row_size, shard // 2, 3 * width), (row_size, emb_rows, dmodel // 2)
    tail = [
        bf16(row_size, shard, 3 * width), bf16(row_size, emb_rows, dmodel),
        bf16(*half_qkv), bf16(*half_emb), f32(*sums.shape), f32(*sums.shape),
        bf16(*half_qkv), bf16(*half_emb), f32(row_size, *sums.shape),
        bf16(groups, shard // 2, 3 * width), bf16(emb_rows, dmodel // 2), f32(*sums.shape),
        bf16(groups, shard // 2, 3 * width), bf16(emb_rows, dmodel // 2), f32(*sums.shape),
        bf16(2, groups, shard // 2, 3 * width), bf16(emb_rows, dmodel), bf16(row_size, emb_rows, dmodel),
    ]
    sends = 6 + 3 * (z_size - 1) + 9 + 8 + 5 * (row_size - 1)
    vmem = pl.BlockSpec(memory_space=pltpu.VMEM)
    anywhere = pl.BlockSpec(memory_space=pl.ANY)
    f32_out = lambda *shape: jax.ShapeDtypeStruct(shape, jnp.float32)
    return pl.pallas_call(
        functools.partial(back_kernel, (row_size, x_size, chunk, ctx_rows, local_rows)),
        out_shape=[
            jax.ShapeDtypeStruct((own_feat.shape[0], slot_count, ctx_rows), jnp.bfloat16),
            jax.ShapeDtypeStruct((own_feat.shape[0], slot_count, local_rows - ctx_rows), jnp.bfloat16),
            f32_out(slots, dmodel),
            f32_out(*sums.shape),
            f32_out(shard, 3 * dmodel),
            f32_out(ro, wo),
            f32_out(ru, wu),
            f32_out(rd, wd),
        ],
        in_specs=[pl.BlockSpec(memory_space=pltpu.SMEM)] + [anywhere] * 7 + [vmem] * 10,
        out_specs=[vmem] * 8,
        scratch_shapes=inputs + stage1 + stage1 + stage2 + stage3 + stage4 + attention + tail + [
            pltpu.SemaphoreType.DMA((7,)),
            pltpu.SemaphoreType.DMA((sends,)),
            pltpu.SemaphoreType.DMA((sends,)),
        ],
        compiler_params=pltpu.CompilerParams(
            collective_id=collective_id, has_side_effects=True, vmem_limit_bytes=62 * 2**20
        ),
        name="back",
    )(counts, *halves, queries, keys, values, outs, g_in, feat, w_emb, w_mine, gain, bias, own_feat, d_branch,
      vectors, sums)


def local_by_heads(
    ctx_feat,
    qry_feat,
    feat_count,
    ctx_count,
    qry_count,
    w_emb,
    ln1_gain,
    ln1_bias,
    w_qkv,
    w_out,
    ln2_gain,
    ln2_bias,
    w_up,
    b_up,
    w_down,
    ctx_cot,
    qry_cot,
):
    table_count, slot_count, ctx_rows = ctx_feat.shape
    qry_rows = qry_feat.shape[2]
    local_rows = ctx_rows + qry_rows
    dmodel = w_out.shape[0]
    head_count = dmodel // HEAD_DIM
    row_size = lax.axis_size("row")
    total_ctx = ctx_rows * row_size
    row_index = lax.axis_index("row")
    groups = row_size // table_count
    heads = head_count // groups
    width = heads * HEAD_DIM

    slot_live = (jnp.arange(slot_count)[None, :] < feat_count[:, None]).astype(jnp.bfloat16)
    features = jnp.concatenate([ctx_feat, qry_feat], axis=2) * slot_live[:, :, None]
    by_row = jnp.pad(jnp.transpose(features, (0, 2, 1)), ((0, 0), (0, 0), (0, LANES - slot_count)))
    w_emb_pad = jnp.pad(w_emb, ((0, LANES - slot_count), (0, 0)))
    packed, back_queries, keys, values, outs, table_feat, w_mine = front(
        ctx_count,
        by_row,
        w_emb_pad,
        ln1_gain[None],
        ln1_bias[None],
        w_qkv,
        total_ctx,
        heads,
        groups,
        math.gcd(total_ctx, 1024),
        0,
    )
    ctx_out, qry_out, g_in, up_half, down_half, out_half, d_branch, vectors, sums = middle(
        ctx_count,
        qry_count,
        by_row,
        w_emb_pad,
        ln2_gain[None],
        ln2_bias[None],
        b_up[None],
        packed,
        w_out,
        w_up,
        w_down,
        ctx_cot,
        qry_cot,
        groups,
        heads,
        math.gcd(w_up.shape[1], 512),
        1,
    )
    ctx_feat_grad, qry_feat_grad, emb_all, sums, qkv_all, out_all, up_all, down_all = back(
        feat_count,
        (up_half, down_half, out_half),
        back_queries,
        keys,
        values,
        outs,
        g_in,
        table_feat,
        w_emb_pad,
        w_mine,
        ln1_gain[None],
        ln1_bias[None],
        by_row,
        d_branch,
        vectors,
        sums,
        slot_count,
        ctx_rows,
        groups,
        math.gcd(total_ctx, 512),
        2,
    )
    grad_w_emb = emb_all[:slot_count]
    vectors = emb_all[LANES - vectors.shape[0] :]

    def own(vector):
        size = vector.size // row_size
        return lax.dynamic_slice_in_dim(vector.reshape(-1), row_index * size, size, 0)

    gain1_all, bias1_all, gain2_all, bias2_all = (own(vectors[i]) for i in range(4))
    upbias_all = own(vectors[4:])
    squares, live_rows = sums[0, :4], sums[0, 4]
    rms = jnp.sqrt(squares / (live_rows * dmodel))
    return (
        ctx_out,
        qry_out,
        ctx_feat_grad,
        qry_feat_grad,
        grad_w_emb,
        gain1_all,
        bias1_all,
        qkv_all,
        out_all,
        gain2_all,
        bias2_all,
        up_all,
        upbias_all,
        down_all,
        rms,
    )


def local(ctx_feat, qry_feat, *rest):
    table_count, slot_count, ctx_rows = ctx_feat.shape
    qry_rows = qry_feat.shape[2]
    head_count = rest[6].shape[0] // HEAD_DIM
    row_size = lax.axis_size("row")
    even = row_size % table_count == 0 and head_count % (row_size // table_count) == 0
    whole = slot_count + 4 + rest[10].shape[1] // rest[6].shape[0] <= LANES and row_size % 2 == 0 and ctx_rows % LANES == 0 and qry_rows % 32 == 0
    inner = local_by_heads if even and whole else local_by_rows
    return inner(ctx_feat, qry_feat, *rest)


def solution(mesh):
    in_specs = (
        P("tab", None, "row"),
        P("tab", None, "row"),
        P("tab"),
        P("tab"),
        P("tab"),
        P(),
        P(),
        P(),
        P(),
        P(),
        P(),
        P(),
        P(),
        P(),
        P(),
        P("tab", "row", None),
        P("tab", "row", None),
    )
    out_specs = (
        P("tab", "row", None),
        P("tab", "row", None),
        P("tab", None, "row"),
        P("tab", None, "row"),
        P(),
        P("row"),
        P("row"),
        P("row", None),
        P("row", None),
        P("row"),
        P("row"),
        P("row", None),
        P("row"),
        P("row", None),
        P(),
    )
    return jax.shard_map(local, mesh=mesh, in_specs=in_specs, out_specs=out_specs, check_vma=False)
```

```python
import functools
import math

import jax
import jax.numpy as jnp
from jax import lax
from jax.experimental import pallas as pl
from jax.experimental.pallas import tpu as pltpu
from jax.sharding import PartitionSpec as P

HEAD_DIM = 64


EPS = 1e-05
NEGATIVE = -1e30


def standardize(values):
    center = values - jnp.mean(values, axis=-1, keepdims=True)
    inverse = lax.rsqrt(jnp.mean(center * center, axis=-1, keepdims=True) + EPS)
    return (center * inverse, inverse)


def norm_back(grad_out, normed, inverse, gain):
    scaled = grad_out * gain
    inner = (
        scaled
        - jnp.mean(scaled, axis=-1, keepdims=True)
        - normed * jnp.mean(scaled * normed, axis=-1, keepdims=True)
    )
    grad_gain = jnp.sum(grad_out * normed, axis=(0, 1))
    grad_bias = jnp.sum(grad_out, axis=(0, 1))
    return (inverse * inner, grad_gain, grad_bias)


def gelu_exact(values):
    return jax.nn.gelu(values, approximate=False)


def block_scores(query_heads, key_rows, block_index, block_width, key_count, score_scale):
    table_count, local_rows, head_count, head_size = query_heads.shape
    dmodel = head_count * head_size
    block = lax.dynamic_slice_in_dim(key_rows, block_index * block_width, block_width, 1)
    key_block = block[..., :dmodel].reshape(table_count, block_width, head_count, head_size)
    value_block = block[..., dmodel:].reshape(table_count, block_width, head_count, head_size)
    scores = (
        jnp.einsum("trhe,tkhe->thrk", query_heads, key_block, preferred_element_type=jnp.float32)
        * score_scale
    )
    position = block_index * block_width + jnp.arange(block_width)
    live_keys = position[None, :] < key_count[:, None]
    scores = jnp.where(live_keys[:, None, None, :], scores, NEGATIVE)
    return (scores, key_block, value_block)


def local_by_rows(
    ctx_feat,
    qry_feat,
    feat_count,
    ctx_count,
    qry_count,
    w_emb,
    ln1_gain,
    ln1_bias,
    w_qkv,
    w_out,
    ln2_gain,
    ln2_bias,
    w_up,
    b_up,
    w_down,
    ctx_cot,
    qry_cot,
):
    table_count, slot_count, ctx_rows = ctx_feat.shape
    qry_rows = qry_feat.shape[2]
    local_rows = ctx_rows + qry_rows
    dmodel = w_out.shape[0]
    head_count = dmodel // HEAD_DIM
    score_scale = HEAD_DIM ** (-0.5)
    total_ctx = ctx_rows * lax.axis_size("row")
    row_index = lax.axis_index("row")
    slot_live = (jnp.arange(slot_count)[None, :] < feat_count[:, None]).astype(jnp.bfloat16)
    features = jnp.concatenate([ctx_feat, qry_feat], axis=2) * slot_live[:, :, None]
    ctx_live = (row_index * ctx_rows + jnp.arange(ctx_rows))[None, :] < ctx_count[:, None]
    qry_live = (row_index * qry_rows + jnp.arange(qry_rows))[None, :] < qry_count[:, None]
    valid = jnp.concatenate([ctx_live, qry_live], axis=1).astype(jnp.float32)[..., None]
    embed = jnp.einsum("tfr,fd->trd", features, w_emb, preferred_element_type=jnp.float32)
    normed1, inverse1 = standardize(embed)
    attn_in = (normed1 * ln1_gain + ln1_bias).astype(jnp.bfloat16)
    w_query = w_qkv[:, :dmodel]
    w_pair = w_qkv[:, dmodel:]
    query = jnp.einsum("trd,de->tre", attn_in, w_query, preferred_element_type=jnp.float32).astype(
        jnp.bfloat16
    )
    pairs = jnp.einsum(
        "trd,de->tre", attn_in[:, :ctx_rows], w_pair, preferred_element_type=jnp.float32
    ).astype(jnp.bfloat16)
    gathered = lax.all_gather(pairs, "row", axis=1, tiled=True)
    block_width = math.gcd(total_ctx, 512)
    block_total = total_ctx // block_width
    query_heads = query.reshape(table_count, local_rows, head_count, HEAD_DIM)

    def attend_step(carried, block_index):
        running_max, running_sum, summed = carried
        scores, _, value_block = block_scores(
            query_heads, gathered, block_index, block_width, ctx_count, score_scale
        )
        new_max = jnp.maximum(running_max, jnp.max(scores, axis=-1))
        factor = jnp.exp(running_max - new_max)
        weights = jnp.exp(scores - new_max[..., None])
        running_sum = running_sum * factor + jnp.sum(weights, axis=-1)
        summed = summed * jnp.transpose(factor, (0, 2, 1))[..., None] + jnp.einsum(
            "thrk,tkhe->trhe",
            weights.astype(jnp.bfloat16),
            value_block,
            preferred_element_type=jnp.float32,
        )
        return ((new_max, running_sum, summed), None)

    initial = jnp.full((table_count, head_count, local_rows), NEGATIVE, jnp.float32)
    start_sum = jnp.zeros((table_count, local_rows, head_count, HEAD_DIM), jnp.float32)
    (running_max, running_sum, summed), _ = lax.scan(
        attend_step, (initial, jnp.zeros_like(initial), start_sum), jnp.arange(block_total)
    )
    log_total = running_max + jnp.log(running_sum)
    attended = summed / jnp.transpose(running_sum, (0, 2, 1))[..., None]
    attn_low = attended.reshape(table_count, local_rows, dmodel).astype(jnp.bfloat16)
    branch = jnp.einsum("trd,de->tre", attn_low, w_out, preferred_element_type=jnp.float32)
    mixed = embed + branch
    normed2, inverse2 = standardize(mixed)
    mlp_in = (normed2 * ln2_gain + ln2_bias).astype(jnp.bfloat16)
    hidden = jnp.einsum("trd,de->tre", mlp_in, w_up, preferred_element_type=jnp.float32) + b_up
    activation, gelu_back = jax.vjp(gelu_exact, hidden)
    act_low = activation.astype(jnp.bfloat16)
    mlp = jnp.einsum("tre,ed->trd", act_low, w_down, preferred_element_type=jnp.float32)
    output = (mixed + mlp) * valid
    ctx_out = output[:, :ctx_rows].astype(jnp.bfloat16)
    qry_out = output[:, ctx_rows:].astype(jnp.bfloat16)
    squares = jnp.stack(
        [
            jnp.sum(valid * embed * embed),
            jnp.sum(valid * branch * branch),
            jnp.sum(valid * mlp * mlp),
            jnp.sum(valid * output * output),
        ]
    )
    live_rows = jnp.sum(valid)
    cotangent = jnp.concatenate([ctx_cot, qry_cot], axis=1)
    d_mlp = cotangent * valid.astype(jnp.bfloat16)
    grad_w_down = jnp.einsum("tre,trd->ed", act_low, d_mlp, preferred_element_type=jnp.float32)
    d_act = jnp.einsum("trd,ed->tre", d_mlp, w_down, preferred_element_type=jnp.float32)
    d_hidden = gelu_back(d_act)[0].astype(jnp.bfloat16)
    grad_b_up = jnp.sum(d_hidden.astype(jnp.float32), axis=(0, 1))
    grad_w_up = jnp.einsum("trd,tre->de", mlp_in, d_hidden, preferred_element_type=jnp.float32)
    d_mlp_in = jnp.einsum("tre,de->trd", d_hidden, w_up, preferred_element_type=jnp.float32)
    d_norm2, grad_ln2_gain, grad_ln2_bias = norm_back(d_mlp_in, normed2, inverse2, ln2_gain)
    d_mixed = d_mlp.astype(jnp.float32) + d_norm2
    d_branch = d_mixed.astype(jnp.bfloat16)
    grad_w_out = jnp.einsum("trd,tre->de", attn_low, d_branch, preferred_element_type=jnp.float32)
    d_attn = jnp.einsum("tre,de->trd", d_branch, w_out, preferred_element_type=jnp.float32).astype(
        jnp.bfloat16
    )
    d_attn_heads = d_attn.reshape(table_count, local_rows, head_count, HEAD_DIM)
    dots_rows = jnp.sum(d_attn_heads.astype(jnp.float32) * attended, axis=-1)
    row_dots = jnp.transpose(dots_rows, (0, 2, 1))

    def query_part(block_index):
        scores, key_block, value_block = block_scores(
            query_heads, gathered, block_index, block_width, ctx_count, score_scale
        )
        softened = jnp.exp(scores - log_total[..., None])
        d_soft = jnp.einsum(
            "trhe,tkhe->thrk", d_attn_heads, value_block, preferred_element_type=jnp.float32
        )
        d_scores = (softened * (d_soft - row_dots[..., None])).astype(jnp.bfloat16)
        d_part = (
            jnp.einsum("thrk,tkhe->trhe", d_scores, key_block, preferred_element_type=jnp.float32)
            * score_scale
        )
        return (softened, d_scores, d_part)

    start_query = jnp.zeros((table_count, local_rows, head_count, HEAD_DIM), jnp.float32)

    def grad_step(carried, block_index):
        d_query, d_pairs = carried
        softened, d_scores, d_part = query_part(block_index)
        d_values = jnp.einsum(
            "thrk,trhe->tkhe",
            softened.astype(jnp.bfloat16),
            d_attn_heads,
            preferred_element_type=jnp.float32,
        )
        d_keys = (
            jnp.einsum("thrk,trhe->tkhe", d_scores, query_heads, preferred_element_type=jnp.float32)
            * score_scale
        )
        grad_block = jnp.concatenate(
            [
                d_keys.reshape(table_count, block_width, dmodel),
                d_values.reshape(table_count, block_width, dmodel),
            ],
            axis=-1,
        )
        d_pairs = lax.dynamic_update_slice_in_dim(d_pairs, grad_block, block_index * block_width, 1)
        return ((d_query + d_part, d_pairs), None)

    start_pairs = jnp.zeros((table_count, total_ctx, 2 * dmodel), jnp.float32)
    (d_query, d_pairs), _ = lax.scan(grad_step, (start_query, start_pairs), jnp.arange(block_total))
    own_pairs = lax.psum_scatter(d_pairs, "row", scatter_dimension=1, tiled=True).astype(
        jnp.bfloat16
    )
    d_q = d_query.reshape(table_count, local_rows, dmodel).astype(jnp.bfloat16)
    grad_w_qkv = jnp.concatenate(
        [
            jnp.einsum("trd,tre->de", attn_in, d_q, preferred_element_type=jnp.float32),
            jnp.einsum(
                "trd,tre->de", attn_in[:, :ctx_rows], own_pairs, preferred_element_type=jnp.float32
            ),
        ],
        axis=1,
    )
    d_from_query = jnp.einsum("tre,de->trd", d_q, w_query, preferred_element_type=jnp.float32)
    d_from_pairs = jnp.einsum("tre,de->trd", own_pairs, w_pair, preferred_element_type=jnp.float32)
    d_attn_in = jnp.concatenate(
        [d_from_query[:, :ctx_rows] + d_from_pairs, d_from_query[:, ctx_rows:]], axis=1
    )
    d_norm1, grad_ln1_gain, grad_ln1_bias = norm_back(d_attn_in, normed1, inverse1, ln1_gain)
    d_embed = (d_mixed + d_norm1).astype(jnp.bfloat16)
    grad_w_emb = jnp.einsum("tfr,trd->fd", features, d_embed, preferred_element_type=jnp.float32)
    d_features = jnp.einsum("trd,fd->tfr", d_embed, w_emb, preferred_element_type=jnp.float32)
    d_features = (d_features * slot_live[:, :, None].astype(jnp.float32)).astype(jnp.bfloat16)
    ctx_feat_grad = d_features[:, :, :ctx_rows]
    qry_feat_grad = d_features[:, :, ctx_rows:]
    (
        qkv_part,
        out_part,
        up_part,
        down_part,
        gain1_part,
        bias1_part,
        gain2_part,
        bias2_part,
        upbias_part,
    ) = (
        lax.psum_scatter(grad_w_qkv, "row", scatter_dimension=0, tiled=True),
        lax.psum_scatter(grad_w_out, "row", scatter_dimension=0, tiled=True),
        lax.psum_scatter(grad_w_up, "row", scatter_dimension=0, tiled=True),
        lax.psum_scatter(grad_w_down, "row", scatter_dimension=0, tiled=True),
        lax.psum_scatter(grad_ln1_gain, "row", scatter_dimension=0, tiled=True),
        lax.psum_scatter(grad_ln1_bias, "row", scatter_dimension=0, tiled=True),
        lax.psum_scatter(grad_ln2_gain, "row", scatter_dimension=0, tiled=True),
        lax.psum_scatter(grad_ln2_bias, "row", scatter_dimension=0, tiled=True),
        lax.psum_scatter(grad_b_up, "row", scatter_dimension=0, tiled=True),
    )
    qkv_all, out_all, up_all, down_all, gain1_all, bias1_all, gain2_all, bias2_all, upbias_all = (
        lax.psum(qkv_part.astype(jnp.bfloat16), "tab").astype(jnp.float32),
        lax.psum(out_part.astype(jnp.bfloat16), "tab").astype(jnp.float32),
        lax.psum(up_part.astype(jnp.bfloat16), "tab").astype(jnp.float32),
        lax.psum(down_part.astype(jnp.bfloat16), "tab").astype(jnp.float32),
        lax.psum(gain1_part.astype(jnp.bfloat16), "tab").astype(jnp.float32),
        lax.psum(bias1_part.astype(jnp.bfloat16), "tab").astype(jnp.float32),
        lax.psum(gain2_part.astype(jnp.bfloat16), "tab").astype(jnp.float32),
        lax.psum(bias2_part.astype(jnp.bfloat16), "tab").astype(jnp.float32),
        lax.psum(upbias_part.astype(jnp.bfloat16), "tab").astype(jnp.float32),
    )
    embed_all, squares_all, count_all = lax.psum((grad_w_emb, squares, live_rows), ("tab", "row"))
    rms = jnp.sqrt(squares_all / (count_all * dmodel))
    return (
        ctx_out,
        qry_out,
        ctx_feat_grad,
        qry_feat_grad,
        embed_all,
        gain1_all,
        bias1_all,
        qkv_all,
        out_all,
        gain2_all,
        bias2_all,
        up_all,
        upbias_all,
        down_all,
        rms,
    )


MESH = pl.DeviceIdType.MESH
LANES = 128
NT = (((1,), (1,)), ((), ()))


def lane_of(shape):
    return lax.broadcasted_iota(jnp.int32, shape, len(shape) - 1)


def split_three(values):
    high = values.astype(jnp.bfloat16)
    rest = values - high.astype(jnp.float32)
    mid = rest.astype(jnp.bfloat16)
    tail = (rest - mid.astype(jnp.float32)).astype(jnp.bfloat16)
    return (high, mid, tail)


def set_lanes(values, first, columns):
    lane = lane_of(values.shape)
    values = values.astype(jnp.float32)
    for i, column in enumerate(columns):
        values = jnp.where(lane == first + i, column.astype(jnp.float32), values)
    return values.astype(jnp.bfloat16)


def greet(peers):
    barrier = pltpu.get_barrier_semaphore()
    for peer in peers:
        pl.semaphore_signal(barrier, inc=1, device_id=peer, device_id_type=MESH)
    pl.semaphore_wait(barrier, len(peers))


def front_kernel(
    dims, feat_counts, counts, ctx_feat, qry_feat, w_emb_in, gain_in, bias_in, w_qkv,
    out_in, queries_out, keys_out, values_out, outs_out, feat_out, w_out, own_feat, w_emb,
    by_slot, feat_in, window, w_lanes, w_mine, queries, keys, values, outs, packed, load_sem, store_sem, send_sem, recv_sem,
):
    row_size, x_size, chunk, ctx_rows, local_rows, heads, groups = dims
    z_size = row_size // x_size
    total = keys.shape[1]
    pair = x_size * local_rows
    dmodel = w_emb.shape[1]
    width = heads * HEAD_DIM
    tab, row = lax.axis_index("tab"), lax.axis_index("row")
    z = row // x_size
    table, group = row // groups, lax.rem(row, groups)
    tables = own_feat.shape[0]
    row_peers = [(tab, lax.rem(row + k, row_size)) for k in range(1, row_size)]
    numbers = {}

    def remote(name, src, dst, peer):
        i = numbers.setdefault(name, len(numbers))
        return pltpu.make_async_remote_copy(
            src_ref=src, dst_ref=dst, send_sem=send_sem.at[i], recv_sem=recv_sem.at[i],
            device_id=peer, device_id_type=MESH,
        )

    def feat_copy(dt, dg):
        t, g = lax.rem(table + dt, tables), lax.rem(group + dg, groups)
        if dt == 0:
            return remote(("near", dg), own_feat.at[table], feat_in.at[row], (tab, table * groups + g))
        if dg == 0:
            return remote(("far", dt), own_feat.at[t], feat_in.at[row], (tab, t * groups + group))
        came = t * groups + group
        return remote(("passed", dt, dg), feat_in.at[came], feat_in.at[came], (tab, table * groups + g))

    def out_copy(shift):
        p = lax.rem(row + shift, row_size)
        return remote(("out", shift), packed.at[p], out_in.at[row], (tab, p))

    span = window.shape[2]
    first = (group * width) // LANES * LANES

    def window_copy(n):
        at = pl.ds(pl.multiple_of(n * dmodel + first, LANES), span)
        return pltpu.make_async_copy(w_qkv.at[:, at], window.at[n], load_sem.at[n])

    for n in range(3):
        window_copy(n).start()
    by_slot[...] = jnp.zeros_like(by_slot)
    slots = ctx_feat.shape[0]
    slot = lax.broadcasted_iota(jnp.int32, (slots, 1), 0)
    for t in range(tables):
        live = jnp.where(slot < feat_counts[t], 1.0, 0.0)
        by_slot[:slots, :ctx_rows] = ctx_feat[:, t].astype(jnp.float32) * live
        wide = by_slot[...].T
        own_feat[t, :ctx_rows] = wide[:ctx_rows].astype(jnp.bfloat16)
        lane = lax.broadcasted_iota(jnp.int32, qry_feat.shape[1:], 1)
        narrow = jnp.where(lane < feat_counts[t], qry_feat[t].astype(jnp.float32), 0.0)
        nothing = jnp.zeros((narrow.shape[0], LANES - slots), jnp.float32)
        own_feat[t, ctx_rows:] = jnp.concatenate([narrow, nothing], axis=1).astype(jnp.bfloat16)
    w_emb[...] = jnp.zeros_like(w_emb)
    w_emb[:slots] = w_emb_in[...]
    gain, bias = gain_in[...][None], bias_in[...][None]
    greet(row_peers)
    for dt in range(1, tables):
        feat_copy(dt, 0).start()
    for dg in range(1, groups):
        feat_copy(0, dg).start()
    feat_in[row] = own_feat[table]
    offset = group * width - first
    for n in range(3):
        window_copy(n).wait()
        wide = window[n]
        mine = wide[:, :width]
        for shift in range(HEAD_DIM, span - width + 1, HEAD_DIM):
            mine = jnp.where(offset == shift, wide[:, shift : shift + width], mine)
        w_mine[:, n * width : (n + 1) * width] = mine
        for h in range(heads):
            one = mine[:, h * HEAD_DIM : (h + 1) * HEAD_DIM]
            at = (n * heads + h) * LANES
            w_lanes[:, at : at + LANES] = jnp.concatenate([one, jnp.zeros_like(one)], axis=1)
    w_store = pltpu.make_async_copy(w_mine, w_out, store_sem.at[0])
    w_store.start()
    count = counts[table]

    near = groups // x_size

    def project(step, _):
        @pl.when(step == 1)
        def _():
            for dt in range(1, tables):
                feat_copy(tables - dt, 0).wait_recv()
                for dg in range(1, groups):
                    feat_copy(dt, dg).start()

        there = lax.rem(z // near + step // near, tables) * near + lax.rem(z + step, near)
        embeds = []
        for other in range(x_size):
            p = there * x_size + other
            ahead = lax.rem(p // groups - table + tables, tables)
            across = lax.rem(group - lax.rem(p, groups) + groups, groups)
            for dt in range(tables):
                for dg in range(1, groups):

                    @pl.when((ahead == dt) & (across == dg))
                    def _():
                        feat_copy(dt, dg).wait_recv()

            embeds.append(feat_in[p])
        rows_feat = jnp.concatenate(embeds, axis=0)
        embed = jnp.dot(rows_feat, w_emb[...], preferred_element_type=jnp.float32)
        center = embed - jnp.mean(embed, axis=-1, keepdims=True)
        inverse = lax.rsqrt(jnp.mean(center * center, axis=-1, keepdims=True) + EPS)
        attn_in = (center * inverse * gain + bias).astype(jnp.bfloat16)
        projected = jnp.dot(attn_in, w_lanes[...], preferred_element_type=jnp.float32)
        rows = pl.ds(pl.multiple_of(there * pair, LANES), pair)
        lane = lane_of((pair, LANES))
        for h in range(heads):
            query = projected[:, h * LANES : (h + 1) * LANES] * HEAD_DIM ** (-0.5)
            queries[h, rows] = jnp.where(lane == HEAD_DIM, 1.0, query).astype(jnp.bfloat16)
        lane = lane_of((ctx_rows, LANES))
        for other in range(x_size):
            p = there * x_size + other
            key_rows = pl.ds(pl.multiple_of(p * ctx_rows, LANES), ctx_rows)
            position = p * ctx_rows + lax.broadcasted_iota(jnp.int32, (ctx_rows, LANES), 0)
            mask = jnp.where(position < count, 0.0, NEGATIVE)
            for h in range(heads):
                at = (heads + h) * LANES
                key = projected[other * local_rows : other * local_rows + ctx_rows, at : at + LANES]
                key = jnp.where(lane == HEAD_DIM, mask, key)
                key = jnp.where((lane > HEAD_DIM) & (lane < HEAD_DIM + 4), 1.0, key)
                keys[h, key_rows] = key.astype(jnp.bfloat16)
                at = (2 * heads + h) * LANES
                value = projected[other * local_rows : other * local_rows + ctx_rows, at : at + LANES]
                value = jnp.where((lane >= HEAD_DIM) & (lane < HEAD_DIM + 3), 1.0, value)
                values[h, key_rows] = value.astype(jnp.bfloat16)
        return 0

    lax.fori_loop(0, z_size, project, 0)
    stores = [
        pltpu.make_async_copy(src, dst, store_sem.at[i + 1])
        for i, (src, dst) in enumerate(((keys, keys_out), (values, values_out), (feat_in, feat_out)))
    ]
    for store in stores:
        store.start()
    whole = heads // 2

    def segment(step, _):
        k, h = step // heads, lax.rem(step, heads)
        there = lax.rem(z + k + 1, z_size)
        rows = pl.ds(pl.multiple_of(there * pair, LANES), pair)
        query = queries[h, rows]
        for i in range(total // chunk):
            at = pl.ds(i * chunk, chunk)
            scores = lax.dot_general(query, keys[h, at], NT, preferred_element_type=jnp.float32)
            top = jnp.max(scores, axis=-1, keepdims=True)
            if i:
                top = jnp.maximum(top, before)
            weights = jnp.exp(scores - top).astype(jnp.bfloat16)
            term = jnp.dot(weights, values[h, at], preferred_element_type=jnp.float32)
            summed = summed * jnp.exp(before - top) + term if i else term
            before = top
        sum_all = summed[:, HEAD_DIM : HEAD_DIM + 1]
        outs[h, rows] = (summed / sum_all).astype(jnp.bfloat16)
        queries[h, rows] = set_lanes(query, HEAD_DIM + 1, split_three(-(top + jnp.log(sum_all))))

        @pl.when(h == heads - 1)
        def _():
            for other in range(x_size):
                p = there * x_size + other
                at = pl.ds(pl.multiple_of(p * local_rows, 16), local_rows)
                parts = [outs[i, at, :HEAD_DIM] for i in range(heads)]
                for i in range(whole):
                    both = jnp.concatenate([parts[2 * i], parts[2 * i + 1]], axis=1)
                    packed[p, i * local_rows : (i + 1) * local_rows] = both
                if heads % 2:
                    last = parts[-1]
                    both = jnp.concatenate([last[: local_rows // 2], last[local_rows // 2 :]], axis=1)
                    packed[p, whole * local_rows :] = both
                ahead = lax.rem(p - row + row_size, row_size)
                for s in range(1, row_size):

                    @pl.when(ahead == s)
                    def _():
                        out_copy(s).start()

        return 0

    lax.fori_loop(0, z_size * heads, segment, 0)
    last = [
        pltpu.make_async_copy(queries, queries_out, store_sem.at[4]),
        pltpu.make_async_copy(outs, outs_out, store_sem.at[5]),
        pltpu.make_async_copy(packed.at[row], out_in.at[row], store_sem.at[6]),
    ]
    for store in last:
        store.start()
    for dt in range(tables):
        for dg in range(groups):
            if dt + dg:
                feat_copy(dt, dg).wait_send()
    for store in [w_store] + stores + last:
        store.wait()
    for s in range(1, row_size):
        out_copy(s).wait()


def front(feat_counts, counts, ctx_feat, qry_feat, w_emb, gain, bias, w_qkv, total_ctx, heads, groups, chunk, collective_id):
    row_size = lax.axis_size("row")
    tables, qry_rows, _ = qry_feat.shape
    dmodel = w_emb.shape[1]
    ctx_rows = total_ctx // row_size
    local_rows, slots = ctx_rows + qry_rows, LANES
    width = heads * HEAD_DIM
    x_size = 2
    span = -(-(width + (HEAD_DIM if width % LANES else 0)) // LANES) * LANES
    bf16 = lambda *shape: (shape, jnp.bfloat16)
    by_query, by_key = (heads, row_size * local_rows, LANES), (heads, total_ctx, LANES)
    block = (row_size, -(-heads * local_rows // 2), LANES)
    feat = (row_size, local_rows, slots)
    vmem = pl.BlockSpec(memory_space=pltpu.VMEM)
    anywhere = pl.BlockSpec(memory_space=pl.ANY)
    scratch = [
        feat, (3, dmodel, span), (dmodel, 3 * heads * LANES), (dmodel, 3 * width),
        by_query, by_key, by_key, by_query, block,
    ]
    return pl.pallas_call(
        functools.partial(front_kernel, (row_size, x_size, chunk, ctx_rows, local_rows, heads, groups)),
        out_shape=[
            jax.ShapeDtypeStruct(s, jnp.bfloat16)
            for s in (
                block, by_query, by_key, by_key, by_query, feat, (dmodel, 3 * width),
                (tables, local_rows, slots), (slots, dmodel),
            )
        ],
        in_specs=[pl.BlockSpec(memory_space=pltpu.SMEM)] * 2 + [vmem] * 5 + [anywhere],
        out_specs=[anywhere] * 7 + [vmem] * 2,
        scratch_shapes=[pltpu.VMEM((slots, ctx_rows), jnp.float32)] + [pltpu.VMEM(s, jnp.bfloat16) for s in scratch] + [
            pltpu.SemaphoreType.DMA((3,)),
            pltpu.SemaphoreType.DMA((7,)),
            pltpu.SemaphoreType.DMA((2 * (row_size - 1),)),
            pltpu.SemaphoreType.DMA((2 * (row_size - 1),)),
        ],
        compiler_params=pltpu.CompilerParams(
            collective_id=collective_id, has_side_effects=True, vmem_limit_bytes=60 * 2**20
        ),
        name="front",
    )(feat_counts, counts, ctx_feat, qry_feat, w_emb, gain, bias, w_qkv)


def gelu_parts(values):
    below = 0.5 + 0.5 * lax.erf(values * math.sqrt(0.5))
    return (below, values * jnp.exp(-0.5 * values * values) * (1.0 / math.sqrt(2.0 * math.pi)))


def middle_kernel(
    dims, ctx_count, qry_count, own_feat, w_emb, gain_in, bias_in, b_up, out_in, w_out_hbm, w_up_hbm, w_down_hbm, ctx_cot, qry_cot,
    ctx_out, qry_out, g_in, up_half, down_half, out_half, d_branch_out, vectors, sums,
    w_out, w_up, w_down, attn_in, cot, attn_low, mlp_in, mlp_in_t, mixed, normed, d_mlp_in, act, d_hidden, d_up_bias,
    packed, up, down, out, up_in0, down_in0, out_in0, load_sem, store_sem, send_sem, recv_sem,
):
    row_size, ctx_rows, local_rows, tables, groups, heads, tile = dims
    rows = tables * local_rows
    qry_rows = local_rows - ctx_rows
    dmodel, hidden_size = w_up.shape
    tiles = hidden_size // tile
    tab, row = lax.axis_index("tab"), lax.axis_index("row")
    core = lax.rem(tab, 2)
    core_peer = (tab ^ 1, row)
    row_peers = [(tab, lax.rem(row + k, row_size)) for k in range(1, row_size)]
    numbers = {}

    def remote(name, src, dst, peer):
        i = numbers.setdefault(name, len(numbers))
        return pltpu.make_async_remote_copy(
            src_ref=src, dst_ref=dst, send_sem=send_sem.at[i], recv_sem=recv_sem.at[i],
            device_id=peer, device_id_type=MESH,
        )

    gain, bias = gain_in[...][None], bias_in[...][None]
    loads = [
        pltpu.make_async_copy(src, dst, load_sem.at[i])
        for i, (src, dst) in enumerate(
            [(out_in, attn_in), (w_out_hbm, w_out), (w_up_hbm, w_up), (w_down_hbm, w_down)]
            + [(ctx_cot.at[t], cot.at[pl.ds(t * local_rows, ctx_rows)]) for t in range(tables)]
            + [(qry_cot.at[t], cot.at[pl.ds(t * local_rows + ctx_rows, qry_rows)]) for t in range(tables)]
        )
    ]
    for load in loads:
        load.start()
    greet([core_peer] + row_peers)

    at = lax.broadcasted_iota(jnp.int32, (local_rows, 1), 0)
    live = []
    for t in range(tables):
        place = jnp.where(at < ctx_rows, row * ctx_rows + at, row * qry_rows + at - ctx_rows)
        limit = jnp.where(at < ctx_rows, ctx_count[t], qry_count[t])
        live.append(jnp.where(place < limit, 1.0, 0.0))
    valid = jnp.concatenate(live, axis=0)
    own_rows = jnp.concatenate([own_feat[t] for t in range(tables)], axis=0)
    embed = jnp.dot(own_rows, w_emb[...], preferred_element_type=jnp.float32)

    whole = heads // 2
    loads[0].wait()
    for t in range(tables):
        parts = []
        for g in range(groups):
            block = attn_in[t * groups + g]
            for h in range(whole):
                parts.append(block[h * local_rows : (h + 1) * local_rows])
            if heads % 2:
                last = block[whole * local_rows :]
                parts.append(jnp.concatenate([last[:, :HEAD_DIM], last[:, HEAD_DIM:]], axis=0))
        attn_low[t * local_rows : (t + 1) * local_rows] = jnp.concatenate(parts, axis=1)
    loads[1].wait()
    branch = jnp.dot(attn_low[...], w_out[...], preferred_element_type=jnp.float32)
    summed = embed + branch
    mixed[...] = summed
    square_embed = jnp.sum(valid * embed * embed)
    square_branch = jnp.sum(valid * branch * branch)
    center = summed - jnp.mean(summed, axis=-1, keepdims=True)
    inverse = lax.rsqrt(jnp.mean(center * center, axis=-1, keepdims=True) + EPS)
    normed[...] = center * inverse
    mlp_in[...] = (normed[...] * gain + bias).astype(jnp.bfloat16)
    for load in loads[2:]:
        load.wait()
    cot[...] = (cot[...].astype(jnp.float32) * valid).astype(jnp.bfloat16)
    d_mlp_in[...] = jnp.zeros_like(d_mlp_in)

    def columns(i):
        return pl.ds(pl.multiple_of(i * tile, LANES), tile)

    def first(i, _):
        at = columns(i)
        hidden = jnp.dot(mlp_in[...], w_up[:, at], preferred_element_type=jnp.float32) + b_up[:, at]
        d_act = lax.dot_general(cot[...], w_down[at], NT, preferred_element_type=jnp.float32)
        below, slope = gelu_parts(hidden)
        act[:, at] = (hidden * below).astype(jnp.bfloat16)
        grad = (d_act * (below + slope)).astype(jnp.bfloat16)
        d_hidden[:, at] = grad
        d_up_bias[:, at] = jnp.sum(grad.astype(jnp.float32), axis=0, keepdims=True)
        d_mlp_in[...] += lax.dot_general(grad, w_up[:, at], NT, preferred_element_type=jnp.float32)
        return 0

    lax.fori_loop(0, tiles, first, 0)
    grad_in = d_mlp_in[...]
    scaled = grad_in * gain
    inner = (
        scaled
        - jnp.mean(scaled, axis=-1, keepdims=True)
        - normed[...] * jnp.mean(scaled * normed[...], axis=-1, keepdims=True)
    )
    vectors[...] = jnp.zeros_like(vectors)
    vectors[2:3] = jnp.sum(grad_in * normed[...], axis=0, keepdims=True)
    vectors[3:4] = jnp.sum(grad_in, axis=0, keepdims=True)
    for i in range(hidden_size // dmodel):
        vectors[4 + i : 5 + i] = d_up_bias[:, i * dmodel : (i + 1) * dmodel]
    d_branch = (cot[...].astype(jnp.float32) + inverse * inner).astype(jnp.bfloat16)
    for t in range(tables):
        d_branch_out[t] = d_branch[t * local_rows : (t + 1) * local_rows]
    d_attn = lax.dot_general(d_branch, w_out[...], NT, preferred_element_type=jnp.float32).astype(jnp.bfloat16)
    width = heads * HEAD_DIM
    for t in range(tables):
        for g in range(groups):
            block = d_attn[t * local_rows : (t + 1) * local_rows, g * width : (g + 1) * width]
            p = t * groups + g
            for h in range(whole):
                packed[p, h * local_rows : (h + 1) * local_rows] = block[:, h * LANES : (h + 1) * LANES]
            if heads % 2:
                last = block[:, whole * LANES :]
                both = jnp.concatenate([last[: local_rows // 2], last[local_rows // 2 :]], axis=1)
                packed[p, whole * local_rows :] = both
    own_g = pltpu.make_async_copy(packed.at[row], g_in.at[row], store_sem.at[0])
    own_g.start()
    g_copies = [remote(("g", k), packed.at[peer[1]], g_in.at[row], peer) for k, peer in enumerate(row_peers)]
    for copy in g_copies:
        copy.start()

    def half(ref, which):
        size = ref.shape[1] // 2
        return pl.ds(pl.multiple_of(which * size, 16), size)

    shard = dmodel // row_size
    d_out = jnp.dot(attn_low[...].T, d_branch, preferred_element_type=jnp.float32).astype(jnp.bfloat16)
    for p in range(row_size):
        out[p] = d_out[p * shard : (p + 1) * shard]
    out_copy = remote("out", out.at[:, half(out, 1 - core)], out_in0, core_peer)
    out_copy.start()
    mlp_in_t[...] = mlp_in[...].T
    d_mlp_in[...] = jnp.zeros_like(d_mlp_in)
    per = hidden_size // row_size

    def second(p, _):
        at = pl.ds(pl.multiple_of(p * per, LANES), per)
        piece = act[:, at]
        down[p] = jnp.dot(piece.T, cot[...], preferred_element_type=jnp.float32).astype(jnp.bfloat16)
        d_up = jnp.dot(mlp_in_t[...], d_hidden[:, at], preferred_element_type=jnp.float32).astype(jnp.bfloat16)
        for q in range(row_size):
            up[q, :, at] = d_up[q * shard : (q + 1) * shard]
        remote("down", down.at[p, half(down, 1 - core)], down_in0.at[p], core_peer).start()
        remote("up", up.at[:, half(up, 1 - core), at], up_in0.at[:, :, at], core_peer).start()
        d_mlp_in[...] += jnp.dot(piece, w_down[at], preferred_element_type=jnp.float32)
        return 0

    lax.fori_loop(0, row_size, second, 0)
    copies = [
        remote("up", up.at[:, half(up, 1 - core)], up_in0, core_peer),
        remote("down", down.at[:, half(down, 1 - core)], down_in0, core_peer),
    ]
    mlp = d_mlp_in[...]
    result = (mixed[...] + mlp) * valid
    square_mlp = jnp.sum(valid * mlp * mlp)
    square_result = jnp.sum(result * result)
    low = result.astype(jnp.bfloat16)
    for t in range(tables):
        ctx_out[t] = low[t * local_rows : t * local_rows + ctx_rows]
        qry_out[t] = low[t * local_rows + ctx_rows : (t + 1) * local_rows]
    lane = lane_of(sums.shape)
    parts = (square_embed, square_branch, square_mlp, square_result, jnp.sum(valid))
    total = jnp.zeros(sums.shape, jnp.float32)
    for i, part in enumerate(parts):
        total = jnp.where(lane == i, part, total)
    sums[...] = total
    stores = []
    for i, (copy, mine, taken, result_hbm) in enumerate(
        ((out_copy, out, out_in0, out_half), (copies[1], down, down_in0, down_half), (copies[0], up, up_in0, up_half))
    ):
        copy.wait()

        @pl.loop(0, row_size)
        def _(p):
            taken[p] = taken[p] + mine[p, half(mine, core)]

        store = pltpu.make_async_copy(taken, result_hbm, store_sem.at[i + 1])
        store.start()
        stores.append(store)
    for store in stores + [own_g]:
        store.wait()
    for copy in g_copies:
        copy.wait()


def middle(ctx_count, qry_count, own_feat, w_emb, gain, bias, b_up, out_in, w_out, w_up, w_down, ctx_cot, qry_cot,
           groups, heads, tile, collective_id):
    row_size = lax.axis_size("row")
    tables, local_rows, _ = own_feat.shape
    ctx_rows = ctx_cot.shape[1]
    rows = tables * local_rows
    dmodel, hidden_size = w_up.shape
    shard, per = dmodel // row_size, hidden_size // row_size
    halves = [(row_size, shard // 2, hidden_size), (row_size, per // 2, dmodel), (row_size, shard // 2, dmodel)]
    vmem = pl.BlockSpec(memory_space=pltpu.VMEM)
    smem = pl.BlockSpec(memory_space=pltpu.SMEM)
    anywhere = pl.BlockSpec(memory_space=pl.ANY)
    bf16 = lambda *shape: pltpu.VMEM(shape, jnp.bfloat16)
    f32 = lambda *shape: pltpu.VMEM(shape, jnp.float32)
    sends = row_size - 1 + 3
    return pl.pallas_call(
        functools.partial(middle_kernel, (row_size, ctx_rows, local_rows, tables, groups, heads, tile)),
        out_shape=[jax.ShapeDtypeStruct(s, jnp.bfloat16) for s in (ctx_cot.shape, qry_cot.shape, out_in.shape, *halves)]
        + [jax.ShapeDtypeStruct((tables, local_rows, dmodel), jnp.bfloat16)]
        + [jax.ShapeDtypeStruct((4 + hidden_size // dmodel, dmodel), jnp.float32)]
        + [jax.ShapeDtypeStruct((8, LANES), jnp.float32)],
        in_specs=[smem] * 2 + [vmem] * 5 + [anywhere] * 6,
        out_specs=[vmem] * 2 + [anywhere] * 4 + [vmem] * 3,
        scratch_shapes=[
            bf16(*w_out.shape), bf16(*w_up.shape), bf16(*w_down.shape), bf16(*out_in.shape), bf16(rows, dmodel),
            bf16(rows, dmodel), bf16(rows, dmodel), bf16(dmodel, rows),
            f32(rows, dmodel), f32(rows, dmodel), f32(rows, dmodel),
            bf16(rows, hidden_size), bf16(rows, hidden_size), f32(1, hidden_size),
            bf16(*out_in.shape),
            bf16(row_size, shard, hidden_size), bf16(row_size, per, dmodel), bf16(row_size, shard, dmodel),
            *[bf16(*s) for s in halves],
            pltpu.SemaphoreType.DMA((4 + 2 * tables,)),
            pltpu.SemaphoreType.DMA((4,)),
            pltpu.SemaphoreType.DMA((sends,)),
            pltpu.SemaphoreType.DMA((sends,)),
        ],
        compiler_params=pltpu.CompilerParams(
            collective_id=collective_id, has_side_effects=True, vmem_limit_bytes=62 * 2**20
        ),
        name="middle",
    )(ctx_count, qry_count, own_feat, w_emb, gain, bias, b_up, out_in, w_out, w_up, w_down, ctx_cot, qry_cot)


def tile_sum(parts):
    total = parts[0]
    for part in parts[1:]:
        total = total + part
    return total


ROW_AXES = ("x", "near", "far")
ATTEND_STEPS = ((5, 1, 0), (6, 2, 0), (6, 3, 0), (7, 0, 0), (7, 4, 0),
                (8, 1, 1), (9, 2, 1), (9, 3, 1), (10, 0, 1), (10, 4, 1), (11, 1, 2))
PROJECT_STEPS = ((0, 2, 2), (0, 3, 2), (0, 0, 2), (0, 4, 2))


def plan_streams(shapes):
    (up_rows, up_wide), (down_rows, down_wide), (out_rows, out_wide) = shapes
    cut = up_wide * 7 // 12 // (2 * LANES) * 2 * LANES
    deep = down_rows * 2 // 3 // 16 * 16
    return (
        ("up_y", "up", (0, up_rows), (0, cut), ("y", "x", "near", "far")),
        ("down_x", "down", (0, deep), (0, down_wide), ("x", "near", "y", "far")),
        ("up_z", "up", (0, up_rows), (cut, up_wide - cut), ("near", "y", "x", "far")),
        ("down_z", "down", (deep, down_rows - deep), (0, down_wide), ("near", "y", "x", "far")),
        ("out_y", "out", (0, out_rows), (0, out_wide), ("y", "x", "near", "far")),
    )


def back_kernel(
    dims, counts, up0, down0, out0, queries_hbm, keys_hbm, values_hbm, outs_hbm, g_in, feat, w_emb, w_mine, gain_in, bias_in,
    own_feat, d_branch, vectors, sums,
    ctx_grad, qry_grad, emb_all, own_all, qkv_all, out_all, up_all, down_all,
    queries, keys, values, outs, grads, d_q, d_kt, d_vt, d_k, d_v, terms, terms_in, d_qkv, d_emb, d_gain, d_bias,
    qkv_own, emb_own, qkv_in0, emb_in0, sums_in0, sums0, qkv_in1, emb_in1, sums_in1,
    qkv1, emb1, sums1, qkv_in2, emb_in2, sums_in2, qkv2, emb2, emb3, *rest,
):
    row_size, x_size, chunk, ctx_rows, local_rows, plan = dims
    gain, bias = gain_in[...][None], bias_in[...][None]
    buffers, (load_sem, send_sem, recv_sem) = rest[:-3], rest[-3:]
    z_size = row_size // x_size
    heads, total, _ = keys.shape
    pair = x_size * local_rows
    tab, row = lax.axis_index("tab"), lax.axis_index("row")
    core, y = lax.rem(tab, 2), tab // 2
    x, z = lax.rem(row, x_size), row // x_size
    core_peer, y_peer, x_peer = (tab ^ 1, row), (tab ^ 2, row), (tab, row ^ 1)
    row_peers = [(tab, lax.rem(row + k, row_size)) for k in range(1, row_size)]
    numbers = {}

    def remote(name, src, dst, peer):
        i = numbers.setdefault(name, len(numbers))
        return pltpu.make_async_remote_copy(
            src_ref=src, dst_ref=dst, send_sem=send_sem.at[i], recv_sem=recv_sem.at[i],
            device_id=peer, device_id_type=MESH,
        )

    def half(rows, which):
        return pl.ds(pl.multiple_of(which * (rows // 2), 16), rows // 2)

    def columns(ref, which):
        wide = ref.shape[-1] // 2
        return pl.ds(pl.multiple_of(which * wide, LANES), wide)

    axes = {"y": (y, y_peer)}
    for bit, axis in enumerate(ROW_AXES):
        axes[axis] = (lax.rem(row // 2**bit, 2), (tab, row ^ 2**bit))
    sources = {"up": up0, "down": down0, "out": out0}
    streams = []
    for number, (name, source, rows, cols, order) in enumerate(plan):
        ref = sources[source].reshape(2, 2, 2, *sources[source].shape[1:])
        ref = ref.at[:, :, :, pl.ds(*rows), pl.ds(*cols)]
        dims_left, steps = list(ROW_AXES[::-1]), []
        shape = [2, 2, 2, rows[1], cols[1]]
        landing = buffers[6 * number : 6 * number + 6]
        for k, axis in enumerate(order):
            mine, (here, peer) = [], axes[axis]
            if axis == "y":
                wide = shape[-1] // 2
                kept, sent = (
                    (slice(None),) * (len(shape) - 1) + (pl.ds(pl.multiple_of(which * wide, LANES), wide),)
                    for which in (here, 1 - here)
                )
                shape = shape[:-1] + [wide]
            else:
                at = dims_left.index(axis)
                kept, sent = ((slice(None),) * at + (which,) for which in (here, 1 - here))
                dims_left.pop(at)
                shape = shape[:at] + shape[at + 1 :]
            copy = remote((name, axis), ref.at[sent], landing[k], peer)
            own = pltpu.make_async_copy(ref.at[kept], landing[4], load_sem.at[4 + number]) if k == 0 else None
            steps.append((copy, own, ref.at[kept] if k else landing[4], landing[k]))
            ref = landing[k]
        streams.append((steps, landing[5]))
    loads = [
        pltpu.make_async_copy(src, dst, load_sem.at[i])
        for i, (src, dst) in enumerate(
            ((queries_hbm, queries), (keys_hbm, keys), (values_hbm, values), (outs_hbm, outs))
        )
    ]

    def advance(number, k):
        steps, last = streams[number]
        copy, own, mine, taken = steps[k]
        copy.wait()
        if own is not None:
            own.wait()
        if k + 1 < len(steps):
            lead = taken.shape[:-2]
            size = math.prod(lead)

            @pl.loop(0, size)
            def _(i):
                at = []
                for extent in lead[::-1]:
                    at.insert(0, lax.rem(i, extent))
                    i = i // extent
                taken[tuple(at)] = taken[tuple(at)] + mine[tuple(at)]

            steps[k + 1][0].start()
        else:
            last[core, y] = taken[...] + mine[...]

    lasts = [last for _, last in streams]

    def to_y():
        return [remote(("to_y", i), last.at[core, y], last.at[core, y], y_peer) for i, last in enumerate(lasts)]

    def to_core(which):
        at = y if which == 0 else 1 - y
        return [
            remote(("to_core", which, i), last.at[core, at], last.at[core, at], core_peer)
            for i, last in enumerate(lasts)
        ]

    def start(copies):
        for copy in copies:
            copy.start()

    def wait(copies):
        for copy in copies:
            copy.wait()

    start(loads)
    greet([core_peer, y_peer] + row_peers)
    for steps, _ in streams:
        steps[0][0].start()
        steps[0][1].start()
    d_kt[...] = jnp.zeros_like(d_kt)
    d_vt[...] = jnp.zeros_like(d_vt)
    whole = heads // 2

    def unpack(p):
        packed = g_in[p]
        parts = []
        for h in range(whole):
            tile = packed[h * local_rows : (h + 1) * local_rows]
            parts += [tile[:, :HEAD_DIM], tile[:, HEAD_DIM:]]
        if heads % 2:
            tile = packed[whole * local_rows :]
            parts.append(jnp.concatenate([tile[:, :HEAD_DIM], tile[:, HEAD_DIM:]], axis=0))
        rows = pl.ds(pl.multiple_of(p * local_rows, 16), local_rows)
        for h, part in enumerate(parts):
            part = part.astype(jnp.float32)
            result = outs[h, rows, :HEAD_DIM].astype(jnp.float32)
            inner = jnp.sum(part * result, axis=-1, keepdims=True)
            wide = jnp.concatenate([part, jnp.zeros_like(part)], axis=-1)
            grads[h, rows] = set_lanes(wide, HEAD_DIM, split_three(-inner))

    def segment(step, _):
        k, h = step // heads, lax.rem(step, heads)
        there = lax.rem(z + k, z_size)
        rows = pl.ds(pl.multiple_of(there * pair, LANES), pair)

        @pl.when(h == 0)
        def _():
            for other in range(x_size):
                p = there * x_size + other
                unpack(p)

        for at, number, k in ATTEND_STEPS:

            @pl.when(step == at)
            def _():
                advance(number, k)

        query, grad = queries[h, rows], grads[h, rows]
        query_t = query[:, :HEAD_DIM].T
        grad_t = grad[:, :HEAD_DIM].T
        d_query = jnp.zeros((pair, LANES), jnp.float32)
        for i in range(total // chunk):
            at = pl.ds(i * chunk, chunk)
            key, value = keys[h, at], values[h, at]
            probs = jnp.exp(lax.dot_general(query, key, NT, preferred_element_type=jnp.float32))
            d_probs = lax.dot_general(grad, value, NT, preferred_element_type=jnp.float32)
            d_scores = (probs * d_probs).astype(jnp.bfloat16)
            d_vt[h, :, at] += jnp.dot(grad_t, probs.astype(jnp.bfloat16), preferred_element_type=jnp.float32)
            d_kt[h, :, at] += jnp.dot(query_t, d_scores, preferred_element_type=jnp.float32)
            d_query += jnp.dot(d_scores, key, preferred_element_type=jnp.float32)
        d_q[h, rows] = (d_query[:, :HEAD_DIM] * HEAD_DIM ** (-0.5)).astype(jnp.bfloat16)
        return 0

    wait(loads)
    lax.fori_loop(0, z_size * heads, segment, 0)
    for h in range(heads):
        d_k[h] = d_kt[h].T.astype(jnp.bfloat16)
        d_v[h] = d_vt[h].T.astype(jnp.bfloat16)

    d_qkv[...] = jnp.zeros_like(d_qkv)
    d_emb[...] = jnp.zeros_like(d_emb)
    d_gain[...] = jnp.zeros_like(d_gain)
    d_bias[...] = jnp.zeros_like(d_bias)

    def term_copy(shift):
        p = lax.rem(row + shift, row_size)
        return remote(("term", shift), terms.at[p], terms_in.at[row], (tab, p))

    def project(step, _):
        shift = lax.rem(step + 1, z_size)
        there = lax.rem(z + shift, z_size)
        pieces, embeds = [], []
        for other in range(x_size):
            p = there * x_size + other
            rows = pl.ds(pl.multiple_of(p * local_rows, 16), local_rows)
            key_rows = pl.ds(pl.multiple_of(p * ctx_rows, 16), ctx_rows)
            parts = [d_q[h, rows] for h in range(heads)]
            nothing = jnp.zeros((local_rows - ctx_rows, HEAD_DIM), jnp.bfloat16)
            for ref in (d_k, d_v):
                parts += [jnp.concatenate([ref[h, key_rows], nothing], axis=0) for h in range(heads)]
            pieces.append(jnp.concatenate(parts, axis=1))
            embeds.append(feat[p])
        d_three = jnp.concatenate(pieces, axis=0)
        rows_feat = jnp.concatenate(embeds, axis=0)
        embed = jnp.dot(rows_feat, w_emb[...], preferred_element_type=jnp.float32)
        center = embed - jnp.mean(embed, axis=-1, keepdims=True)
        inverse = lax.rsqrt(jnp.mean(center * center, axis=-1, keepdims=True) + EPS)
        normed = center * inverse
        attn_in = (normed * gain + bias).astype(jnp.bfloat16)
        d_in = lax.dot_general(d_three, w_mine[...], NT, preferred_element_type=jnp.float32)
        d_gain[...] += jnp.sum(d_in * normed, axis=0, keepdims=True)
        d_bias[...] += jnp.sum(d_in, axis=0, keepdims=True)
        scaled = d_in * gain
        inner = (
            scaled
            - jnp.mean(scaled, axis=-1, keepdims=True)
            - normed * jnp.mean(scaled * normed, axis=-1, keepdims=True)
        )
        d_norm = (inverse * inner).astype(jnp.bfloat16)
        term = lax.dot_general(d_norm, w_emb[...], NT, preferred_element_type=jnp.float32).astype(jnp.bfloat16)
        d_emb[...] += jnp.dot(rows_feat.T, d_norm, preferred_element_type=jnp.float32)
        d_qkv[...] += jnp.dot(attn_in.T, d_three, preferred_element_type=jnp.float32)
        for other in range(x_size):
            p = there * x_size + other
            terms[p] = term[other * local_rows : (other + 1) * local_rows]
            ahead = lax.rem(p - row + row_size, row_size)
            for s in range(1, row_size):

                @pl.when(ahead == s)
                def _():
                    term_copy(s).start()

        for at, number, k in PROJECT_STEPS:

            @pl.when(step == at)
            def _():
                advance(number, k)

        return 0

    lax.fori_loop(0, z_size, project, 0)

    shard = qkv_own.shape[1]
    for p in range(row_size):
        qkv_own[p] = d_qkv[p * shard : (p + 1) * shard].astype(jnp.bfloat16)
    own_rows = jnp.concatenate([own_feat[t] for t in range(own_feat.shape[0])], axis=0)
    own_d = jnp.concatenate([d_branch[t] for t in range(own_feat.shape[0])], axis=0)
    d_own = d_emb[...] + jnp.dot(own_rows.T, own_d, preferred_element_type=jnp.float32)
    slots_all = d_own.shape[0]
    spare = lax.broadcasted_iota(jnp.int32, d_own.shape, 0) - (slots_all - vectors.shape[0])
    d_own = jnp.where(spare == 0, d_gain[...], d_own)
    d_own = jnp.where(spare == 1, d_bias[...], d_own)
    for i in range(2, vectors.shape[0]):
        d_own = jnp.where(spare == i, vectors[i : i + 1], d_own)
    emb_rows = emb_own.shape[1]
    for p in range(row_size):
        emb_own[p] = d_own[p * emb_rows : (p + 1) * emb_rows].astype(jnp.bfloat16)

    def tail_core():
        return [
            remote("qkv_core", qkv_own.at[:, half(shard, 1 - core)], qkv_in0, core_peer),
            remote("emb_core", emb_own.at[:, :, columns(emb_own, 1 - core)], emb_in0, core_peer),
            remote("sums_core", sums, sums_in0, core_peer),
        ]

    def tail_row():
        copies = []
        for k, peer in enumerate(row_peers):
            copies += [
                remote(("qkv_row", k), qkv_in0.at[peer[1]], qkv_in1.at[row], peer),
                remote(("emb_row", k), emb_in0.at[peer[1]], emb_in1.at[row], peer),
                remote(("sums_row", k), sums0, sums_in1.at[row], peer),
            ]
        return copies

    start(tail_core())
    wait(tail_core())
    qkv_in0[...] = qkv_in0[...] + qkv_own[:, half(shard, core)]
    emb_in0[...] = emb_in0[...] + emb_own[:, :, columns(emb_own, core)]
    sums0[...] = sums[...] + sums_in0[...]
    start(tail_row())
    qkv_in1[row] = qkv_in0[row]
    emb_in1[row] = emb_in0[row]
    sums_in1[row] = sums0[...]

    terms_in[row] = terms[row]
    for s in range(1, row_size):
        term_copy(s).wait()
    groups = qkv1.shape[0]
    for t in range(own_feat.shape[0]):
        term = lax.dot_general(d_branch[t], w_emb[...], NT, preferred_element_type=jnp.float32)
        for g in range(groups):
            term = term + terms_in[t * groups + g].astype(jnp.float32)
        slots = qry_grad.shape[2]
        lane = lane_of(term.shape)
        term = jnp.where(lane < counts[t], term, 0.0)
        ctx_grad[:, t] = term[:ctx_rows].T[:slots].astype(jnp.bfloat16)
        qry_grad[t] = term[ctx_rows:, :slots].astype(jnp.bfloat16)

    for number in range(len(streams)):
        advance(number, 3)
    start(to_y())
    start(to_core(0))

    wait(tail_row())
    for g in range(groups):
        qkv1[g] = tile_sum(
            [qkv_in1[g + t * groups].astype(jnp.float32) for t in range(row_size // groups)]
        ).astype(jnp.bfloat16)
    emb1[...] = tile_sum([emb_in1[p].astype(jnp.float32) for p in range(row_size)]).astype(jnp.bfloat16)
    sums1[...] = tile_sum([sums_in1[p] for p in range(row_size)])
    tail_y = [
        remote("qkv_y", qkv1, qkv_in2, y_peer),
        remote("emb_y", emb1, emb_in2, y_peer),
        remote("sums_y", sums1, sums_in2, y_peer),
    ]
    start(tail_y)
    wait(to_y())
    start(to_core(1))
    wait(tail_y)
    qkv2[core] = qkv1[...] + qkv_in2[...]
    emb2[:, columns(emb_own, core)] = emb1[...] + emb_in2[...]
    sums_all = sums1[...] + sums_in2[...]
    at_core = columns(emb_own, core)
    tail_last = [
        remote("qkv_last", qkv2.at[core], qkv2.at[core], core_peer),
        remote("emb_last", emb2.at[:, at_core], emb2.at[:, at_core], core_peer),
    ]
    start(tail_last)
    wait(to_core(0))
    wait(to_core(1))
    wait(tail_last)
    emb_row = [remote(("emb_all", k), emb2, emb3.at[row], peer) for k, peer in enumerate(row_peers)]
    start(emb_row)
    emb3[row] = emb2[...]
    results = {"up": up_all, "down": down_all, "out": out_all}
    for (_, source, rows, cols, _), last in zip(plan, lasts):
        deep, wide = last.shape[2:]
        half_rows = sources[source].shape[1]
        for i in range(2):
            for j in range(2):
                down_at, across = i * half_rows + rows[0], cols[0] + j * wide
                results[source][down_at : down_at + deep, across : across + wide] = last[i, j]
    width = heads * HEAD_DIM
    for i in range(2):
        parts = [
            qkv2[i, g][:, n * width : (n + 1) * width] for n in range(3) for g in range(groups)
        ]
        qkv_all[i * (shard // 2) : (i + 1) * (shard // 2)] = jnp.concatenate(parts, axis=1)
    wait(emb_row)
    slot_count = emb_all.shape[0]
    whole_emb = jnp.concatenate([emb3[p] for p in range(row_size)], axis=0).astype(jnp.float32)
    emb_all[...] = whole_emb[:slot_count]
    vec = whole_emb[slots_all - vectors.shape[0] :]
    dmodel = vec.shape[1]
    wide = (vectors.shape[0] - 4) * dmodel // row_size
    own_vec, own_up = vec[:4, :shard], vec[4:5, :wide]
    for p in range(1, row_size):
        at = p * wide
        own_vec = jnp.where(row == p, vec[:4, p * shard : (p + 1) * shard], own_vec)
        piece = vec[4 + at // dmodel : 5 + at // dmodel, at % dmodel : at % dmodel + wide]
        own_up = jnp.where(row == p, piece, own_up)
    own_all[...] = jnp.zeros_like(own_all)
    own_all[:4, :shard] = own_vec
    own_all[4:5] = own_up
    rms = jnp.sqrt(sums_all / (sums_all[:1, 4:5] * dmodel))
    own_all[5:6, :LANES] = rms[:1]


def back(counts, halves, queries, keys, values, outs, g_in, feat, w_emb, w_mine, gain, bias, own_feat, d_branch,
         vectors, sums, slot_count, ctx_rows, groups, chunk, collective_id):
    row_size, local_rows, slots = feat.shape
    heads, total, _ = keys.shape
    all_rows = queries.shape[1]
    dmodel = w_emb.shape[1]
    width = heads * HEAD_DIM
    x_size = 2
    z_size = row_size // x_size
    shapes = [(2 * h.shape[1], h.shape[2]) for h in halves]
    bf16 = lambda *shape: pltpu.VMEM(shape, jnp.bfloat16)
    f32 = lambda *shape: pltpu.VMEM(shape, jnp.float32)
    plan = plan_streams([h.shape[1:] for h in halves])
    landings = []
    for _, _, rows, cols, order in plan:
        lead, wide, first = 8, cols[1], None
        for axis in order:
            lead, wide = (lead, wide // 2) if axis == "y" else (lead // 2, wide)
            shape = (2,) * (lead.bit_length() - 1) + (rows[1], wide)
            first = first or shape
            landings.append(bf16(*shape))
        landings += [bf16(*first), bf16(2, 2, rows[1], wide)]
    by_head = bf16(heads, all_rows, LANES)
    shard, emb_rows = dmodel // row_size, slots // row_size
    inputs = [by_head, bf16(*keys.shape), bf16(*keys.shape), by_head]
    attention = [
        by_head, bf16(heads, all_rows, HEAD_DIM),
        f32(heads, HEAD_DIM, total), f32(heads, HEAD_DIM, total),
        bf16(heads, total, HEAD_DIM), bf16(heads, total, HEAD_DIM),
        bf16(*feat.shape), bf16(*feat.shape),
        f32(dmodel, 3 * width), f32(slots, dmodel), f32(1, dmodel), f32(1, dmodel),
    ]
    half_qkv, half_emb = (row_size, shard // 2, 3 * width), (row_size, emb_rows, dmodel // 2)
    tail = [
        bf16(row_size, shard, 3 * width), bf16(row_size, emb_rows, dmodel),
        bf16(*half_qkv), bf16(*half_emb), f32(*sums.shape), f32(*sums.shape),
        bf16(*half_qkv), bf16(*half_emb), f32(row_size, *sums.shape),
        bf16(groups, shard // 2, 3 * width), bf16(emb_rows, dmodel // 2), f32(*sums.shape),
        bf16(groups, shard // 2, 3 * width), bf16(emb_rows, dmodel // 2), f32(*sums.shape),
        bf16(2, groups, shard // 2, 3 * width), bf16(emb_rows, dmodel), bf16(row_size, emb_rows, dmodel),
    ]
    sends = 7 * len(plan) + 8 + 5 * (row_size - 1)
    vmem = pl.BlockSpec(memory_space=pltpu.VMEM)
    anywhere = pl.BlockSpec(memory_space=pl.ANY)
    f32_out = lambda *shape: jax.ShapeDtypeStruct(shape, jnp.float32)
    bf16_out = lambda *shape: jax.ShapeDtypeStruct(shape, jnp.bfloat16)
    return pl.pallas_call(
        functools.partial(back_kernel, (row_size, x_size, chunk, ctx_rows, local_rows, plan)),
        out_shape=[
            bf16_out(slot_count, own_feat.shape[0], ctx_rows),
            bf16_out(own_feat.shape[0], local_rows - ctx_rows, slot_count),
            f32_out(slot_count, dmodel),
            f32_out(8, (vectors.shape[0] - 4) * dmodel // row_size),
            bf16_out(shard, 3 * dmodel),
            bf16_out(*shapes[2]),
            bf16_out(*shapes[0]),
            bf16_out(*shapes[1]),
        ],
        in_specs=[pl.BlockSpec(memory_space=pltpu.SMEM)] + [anywhere] * 7 + [vmem] * 10,
        out_specs=[vmem] * 8,
        scratch_shapes=inputs + attention + tail + landings + [
            pltpu.SemaphoreType.DMA((4 + len(plan),)),
            pltpu.SemaphoreType.DMA((sends,)),
            pltpu.SemaphoreType.DMA((sends,)),
        ],
        compiler_params=pltpu.CompilerParams(
            collective_id=collective_id, has_side_effects=True, vmem_limit_bytes=62 * 2**20
        ),
        name="back",
    )(counts, *halves, queries, keys, values, outs, g_in, feat, w_emb, w_mine, gain, bias, own_feat, d_branch,
      vectors, sums)


def local_by_heads(
    ctx_feat,
    qry_feat,
    feat_count,
    ctx_count,
    qry_count,
    w_emb,
    ln1_gain,
    ln1_bias,
    w_qkv,
    w_out,
    ln2_gain,
    ln2_bias,
    w_up,
    b_up,
    w_down,
    ctx_cot,
    qry_cot,
):
    table_count, slot_count, ctx_rows = ctx_feat.shape
    qry_rows = qry_feat.shape[2]
    local_rows = ctx_rows + qry_rows
    dmodel = w_out.shape[0]
    head_count = dmodel // HEAD_DIM
    row_size = lax.axis_size("row")
    total_ctx = ctx_rows * row_size
    groups = row_size // table_count
    heads = head_count // groups
    packed, back_queries, keys, values, outs, table_feat, w_mine, by_row, w_emb_pad = front(
        feat_count,
        ctx_count,
        jnp.transpose(ctx_feat, (1, 0, 2)),
        jnp.transpose(qry_feat, (0, 2, 1)),
        w_emb,
        ln1_gain,
        ln1_bias,
        w_qkv,
        total_ctx,
        heads,
        groups,
        math.gcd(total_ctx, 1024),
        0,
    )
    ctx_out, qry_out, g_in, up_half, down_half, out_half, d_branch, vectors, sums = middle(
        ctx_count,
        qry_count,
        by_row,
        w_emb_pad,
        ln2_gain,
        ln2_bias,
        b_up[None],
        packed,
        w_out,
        w_up,
        w_down,
        ctx_cot,
        qry_cot,
        groups,
        heads,
        math.gcd(w_up.shape[1], 512),
        1,
    )
    ctx_feat_grad, qry_feat_grad, grad_w_emb, own, qkv_all, out_all, up_all, down_all = back(
        feat_count,
        (up_half, down_half, out_half),
        back_queries,
        keys,
        values,
        outs,
        g_in,
        table_feat,
        w_emb_pad,
        w_mine,
        ln1_gain,
        ln1_bias,
        by_row,
        d_branch,
        vectors,
        sums,
        slot_count,
        ctx_rows,
        groups,
        math.gcd(total_ctx, 512),
        2,
    )
    qkv_all, out_all, up_all, down_all = (g.astype(jnp.float32) for g in (qkv_all, out_all, up_all, down_all))
    ctx_feat_grad = jnp.transpose(ctx_feat_grad, (1, 0, 2))
    qry_feat_grad = jnp.transpose(qry_feat_grad, (0, 2, 1))
    gain1_all, bias1_all, gain2_all, bias2_all = (own[i, : dmodel // row_size] for i in range(4))
    upbias_all, rms = own[4], own[5, :4]
    return (
        ctx_out,
        qry_out,
        ctx_feat_grad,
        qry_feat_grad,
        grad_w_emb,
        gain1_all,
        bias1_all,
        qkv_all,
        out_all,
        gain2_all,
        bias2_all,
        up_all,
        upbias_all,
        down_all,
        rms,
    )


def local(ctx_feat, qry_feat, *rest):
    table_count, slot_count, ctx_rows = ctx_feat.shape
    qry_rows = qry_feat.shape[2]
    head_count = rest[6].shape[0] // HEAD_DIM
    row_size = lax.axis_size("row")
    even = row_size % table_count == 0 and head_count % (row_size // table_count) == 0
    whole = slot_count + 4 + rest[10].shape[1] // rest[6].shape[0] <= LANES and row_size == 8 and ctx_rows % LANES == 0 and qry_rows % 32 == 0
    inner = local_by_heads if even and whole else local_by_rows
    return inner(ctx_feat, qry_feat, *rest)


def solution(mesh):
    in_specs = (
        P("tab", None, "row"),
        P("tab", None, "row"),
        P("tab"),
        P("tab"),
        P("tab"),
        P(),
        P(),
        P(),
        P(),
        P(),
        P(),
        P(),
        P(),
        P(),
        P(),
        P("tab", "row", None),
        P("tab", "row", None),
    )
    out_specs = (
        P("tab", "row", None),
        P("tab", "row", None),
        P("tab", None, "row"),
        P("tab", None, "row"),
        P(),
        P("row"),
        P("row"),
        P("row", None),
        P("row", None),
        P("row"),
        P("row"),
        P("row", None),
        P("row"),
        P("row", None),
        P(),
    )
    return jax.shard_map(local, mesh=mesh, in_specs=in_specs, out_specs=out_specs, check_vma=False)
```

```python
import functools
import math

import jax
import jax.numpy as jnp
from jax import lax
from jax.experimental import pallas as pl
from jax.experimental.pallas import tpu as pltpu
from jax.sharding import PartitionSpec as P

HEAD_DIM = 64


EPS = 1e-05
NEGATIVE = -1e30


def standardize(values):
    center = values - jnp.mean(values, axis=-1, keepdims=True)
    inverse = lax.rsqrt(jnp.mean(center * center, axis=-1, keepdims=True) + EPS)
    return (center * inverse, inverse)


def norm_back(grad_out, normed, inverse, gain):
    scaled = grad_out * gain
    inner = (
        scaled
        - jnp.mean(scaled, axis=-1, keepdims=True)
        - normed * jnp.mean(scaled * normed, axis=-1, keepdims=True)
    )
    grad_gain = jnp.sum(grad_out * normed, axis=(0, 1))
    grad_bias = jnp.sum(grad_out, axis=(0, 1))
    return (inverse * inner, grad_gain, grad_bias)


def gelu_exact(values):
    return jax.nn.gelu(values, approximate=False)


def block_scores(query_heads, key_rows, block_index, block_width, key_count, score_scale):
    table_count, local_rows, head_count, head_size = query_heads.shape
    dmodel = head_count * head_size
    block = lax.dynamic_slice_in_dim(key_rows, block_index * block_width, block_width, 1)
    key_block = block[..., :dmodel].reshape(table_count, block_width, head_count, head_size)
    value_block = block[..., dmodel:].reshape(table_count, block_width, head_count, head_size)
    scores = (
        jnp.einsum("trhe,tkhe->thrk", query_heads, key_block, preferred_element_type=jnp.float32)
        * score_scale
    )
    position = block_index * block_width + jnp.arange(block_width)
    live_keys = position[None, :] < key_count[:, None]
    scores = jnp.where(live_keys[:, None, None, :], scores, NEGATIVE)
    return (scores, key_block, value_block)


def local_by_rows(
    ctx_feat,
    qry_feat,
    feat_count,
    ctx_count,
    qry_count,
    w_emb,
    ln1_gain,
    ln1_bias,
    w_qkv,
    w_out,
    ln2_gain,
    ln2_bias,
    w_up,
    b_up,
    w_down,
    ctx_cot,
    qry_cot,
):
    table_count, slot_count, ctx_rows = ctx_feat.shape
    qry_rows = qry_feat.shape[2]
    local_rows = ctx_rows + qry_rows
    dmodel = w_out.shape[0]
    head_count = dmodel // HEAD_DIM
    score_scale = HEAD_DIM ** (-0.5)
    total_ctx = ctx_rows * lax.axis_size("row")
    row_index = lax.axis_index("row")
    slot_live = (jnp.arange(slot_count)[None, :] < feat_count[:, None]).astype(jnp.bfloat16)
    features = jnp.concatenate([ctx_feat, qry_feat], axis=2) * slot_live[:, :, None]
    ctx_live = (row_index * ctx_rows + jnp.arange(ctx_rows))[None, :] < ctx_count[:, None]
    qry_live = (row_index * qry_rows + jnp.arange(qry_rows))[None, :] < qry_count[:, None]
    valid = jnp.concatenate([ctx_live, qry_live], axis=1).astype(jnp.float32)[..., None]
    embed = jnp.einsum("tfr,fd->trd", features, w_emb, preferred_element_type=jnp.float32)
    normed1, inverse1 = standardize(embed)
    attn_in = (normed1 * ln1_gain + ln1_bias).astype(jnp.bfloat16)
    w_query = w_qkv[:, :dmodel]
    w_pair = w_qkv[:, dmodel:]
    query = jnp.einsum("trd,de->tre", attn_in, w_query, preferred_element_type=jnp.float32).astype(
        jnp.bfloat16
    )
    pairs = jnp.einsum(
        "trd,de->tre", attn_in[:, :ctx_rows], w_pair, preferred_element_type=jnp.float32
    ).astype(jnp.bfloat16)
    gathered = lax.all_gather(pairs, "row", axis=1, tiled=True)
    block_width = math.gcd(total_ctx, 512)
    block_total = total_ctx // block_width
    query_heads = query.reshape(table_count, local_rows, head_count, HEAD_DIM)

    def attend_step(carried, block_index):
        running_max, running_sum, summed = carried
        scores, _, value_block = block_scores(
            query_heads, gathered, block_index, block_width, ctx_count, score_scale
        )
        new_max = jnp.maximum(running_max, jnp.max(scores, axis=-1))
        factor = jnp.exp(running_max - new_max)
        weights = jnp.exp(scores - new_max[..., None])
        running_sum = running_sum * factor + jnp.sum(weights, axis=-1)
        summed = summed * jnp.transpose(factor, (0, 2, 1))[..., None] + jnp.einsum(
            "thrk,tkhe->trhe",
            weights.astype(jnp.bfloat16),
            value_block,
            preferred_element_type=jnp.float32,
        )
        return ((new_max, running_sum, summed), None)

    initial = jnp.full((table_count, head_count, local_rows), NEGATIVE, jnp.float32)
    start_sum = jnp.zeros((table_count, local_rows, head_count, HEAD_DIM), jnp.float32)
    (running_max, running_sum, summed), _ = lax.scan(
        attend_step, (initial, jnp.zeros_like(initial), start_sum), jnp.arange(block_total)
    )
    log_total = running_max + jnp.log(running_sum)
    attended = summed / jnp.transpose(running_sum, (0, 2, 1))[..., None]
    attn_low = attended.reshape(table_count, local_rows, dmodel).astype(jnp.bfloat16)
    branch = jnp.einsum("trd,de->tre", attn_low, w_out, preferred_element_type=jnp.float32)
    mixed = embed + branch
    normed2, inverse2 = standardize(mixed)
    mlp_in = (normed2 * ln2_gain + ln2_bias).astype(jnp.bfloat16)
    hidden = jnp.einsum("trd,de->tre", mlp_in, w_up, preferred_element_type=jnp.float32) + b_up
    activation, gelu_back = jax.vjp(gelu_exact, hidden)
    act_low = activation.astype(jnp.bfloat16)
    mlp = jnp.einsum("tre,ed->trd", act_low, w_down, preferred_element_type=jnp.float32)
    output = (mixed + mlp) * valid
    ctx_out = output[:, :ctx_rows].astype(jnp.bfloat16)
    qry_out = output[:, ctx_rows:].astype(jnp.bfloat16)
    squares = jnp.stack(
        [
            jnp.sum(valid * embed * embed),
            jnp.sum(valid * branch * branch),
            jnp.sum(valid * mlp * mlp),
            jnp.sum(valid * output * output),
        ]
    )
    live_rows = jnp.sum(valid)
    cotangent = jnp.concatenate([ctx_cot, qry_cot], axis=1)
    d_mlp = cotangent * valid.astype(jnp.bfloat16)
    grad_w_down = jnp.einsum("tre,trd->ed", act_low, d_mlp, preferred_element_type=jnp.float32)
    d_act = jnp.einsum("trd,ed->tre", d_mlp, w_down, preferred_element_type=jnp.float32)
    d_hidden = gelu_back(d_act)[0].astype(jnp.bfloat16)
    grad_b_up = jnp.sum(d_hidden.astype(jnp.float32), axis=(0, 1))
    grad_w_up = jnp.einsum("trd,tre->de", mlp_in, d_hidden, preferred_element_type=jnp.float32)
    d_mlp_in = jnp.einsum("tre,de->trd", d_hidden, w_up, preferred_element_type=jnp.float32)
    d_norm2, grad_ln2_gain, grad_ln2_bias = norm_back(d_mlp_in, normed2, inverse2, ln2_gain)
    d_mixed = d_mlp.astype(jnp.float32) + d_norm2
    d_branch = d_mixed.astype(jnp.bfloat16)
    grad_w_out = jnp.einsum("trd,tre->de", attn_low, d_branch, preferred_element_type=jnp.float32)
    d_attn = jnp.einsum("tre,de->trd", d_branch, w_out, preferred_element_type=jnp.float32).astype(
        jnp.bfloat16
    )
    d_attn_heads = d_attn.reshape(table_count, local_rows, head_count, HEAD_DIM)
    dots_rows = jnp.sum(d_attn_heads.astype(jnp.float32) * attended, axis=-1)
    row_dots = jnp.transpose(dots_rows, (0, 2, 1))

    def query_part(block_index):
        scores, key_block, value_block = block_scores(
            query_heads, gathered, block_index, block_width, ctx_count, score_scale
        )
        softened = jnp.exp(scores - log_total[..., None])
        d_soft = jnp.einsum(
            "trhe,tkhe->thrk", d_attn_heads, value_block, preferred_element_type=jnp.float32
        )
        d_scores = (softened * (d_soft - row_dots[..., None])).astype(jnp.bfloat16)
        d_part = (
            jnp.einsum("thrk,tkhe->trhe", d_scores, key_block, preferred_element_type=jnp.float32)
            * score_scale
        )
        return (softened, d_scores, d_part)

    start_query = jnp.zeros((table_count, local_rows, head_count, HEAD_DIM), jnp.float32)

    def grad_step(carried, block_index):
        d_query, d_pairs = carried
        softened, d_scores, d_part = query_part(block_index)
        d_values = jnp.einsum(
            "thrk,trhe->tkhe",
            softened.astype(jnp.bfloat16),
            d_attn_heads,
            preferred_element_type=jnp.float32,
        )
        d_keys = (
            jnp.einsum("thrk,trhe->tkhe", d_scores, query_heads, preferred_element_type=jnp.float32)
            * score_scale
        )
        grad_block = jnp.concatenate(
            [
                d_keys.reshape(table_count, block_width, dmodel),
                d_values.reshape(table_count, block_width, dmodel),
            ],
            axis=-1,
        )
        d_pairs = lax.dynamic_update_slice_in_dim(d_pairs, grad_block, block_index * block_width, 1)
        return ((d_query + d_part, d_pairs), None)

    start_pairs = jnp.zeros((table_count, total_ctx, 2 * dmodel), jnp.float32)
    (d_query, d_pairs), _ = lax.scan(grad_step, (start_query, start_pairs), jnp.arange(block_total))
    own_pairs = lax.psum_scatter(d_pairs, "row", scatter_dimension=1, tiled=True).astype(
        jnp.bfloat16
    )
    d_q = d_query.reshape(table_count, local_rows, dmodel).astype(jnp.bfloat16)
    grad_w_qkv = jnp.concatenate(
        [
            jnp.einsum("trd,tre->de", attn_in, d_q, preferred_element_type=jnp.float32),
            jnp.einsum(
                "trd,tre->de", attn_in[:, :ctx_rows], own_pairs, preferred_element_type=jnp.float32
            ),
        ],
        axis=1,
    )
    d_from_query = jnp.einsum("tre,de->trd", d_q, w_query, preferred_element_type=jnp.float32)
    d_from_pairs = jnp.einsum("tre,de->trd", own_pairs, w_pair, preferred_element_type=jnp.float32)
    d_attn_in = jnp.concatenate(
        [d_from_query[:, :ctx_rows] + d_from_pairs, d_from_query[:, ctx_rows:]], axis=1
    )
    d_norm1, grad_ln1_gain, grad_ln1_bias = norm_back(d_attn_in, normed1, inverse1, ln1_gain)
    d_embed = (d_mixed + d_norm1).astype(jnp.bfloat16)
    grad_w_emb = jnp.einsum("tfr,trd->fd", features, d_embed, preferred_element_type=jnp.float32)
    d_features = jnp.einsum("trd,fd->tfr", d_embed, w_emb, preferred_element_type=jnp.float32)
    d_features = (d_features * slot_live[:, :, None].astype(jnp.float32)).astype(jnp.bfloat16)
    ctx_feat_grad = d_features[:, :, :ctx_rows]
    qry_feat_grad = d_features[:, :, ctx_rows:]
    (
        qkv_part,
        out_part,
        up_part,
        down_part,
        gain1_part,
        bias1_part,
        gain2_part,
        bias2_part,
        upbias_part,
    ) = (
        lax.psum_scatter(grad_w_qkv, "row", scatter_dimension=0, tiled=True),
        lax.psum_scatter(grad_w_out, "row", scatter_dimension=0, tiled=True),
        lax.psum_scatter(grad_w_up, "row", scatter_dimension=0, tiled=True),
        lax.psum_scatter(grad_w_down, "row", scatter_dimension=0, tiled=True),
        lax.psum_scatter(grad_ln1_gain, "row", scatter_dimension=0, tiled=True),
        lax.psum_scatter(grad_ln1_bias, "row", scatter_dimension=0, tiled=True),
        lax.psum_scatter(grad_ln2_gain, "row", scatter_dimension=0, tiled=True),
        lax.psum_scatter(grad_ln2_bias, "row", scatter_dimension=0, tiled=True),
        lax.psum_scatter(grad_b_up, "row", scatter_dimension=0, tiled=True),
    )
    qkv_all, out_all, up_all, down_all, gain1_all, bias1_all, gain2_all, bias2_all, upbias_all = (
        lax.psum(qkv_part.astype(jnp.bfloat16), "tab").astype(jnp.float32),
        lax.psum(out_part.astype(jnp.bfloat16), "tab").astype(jnp.float32),
        lax.psum(up_part.astype(jnp.bfloat16), "tab").astype(jnp.float32),
        lax.psum(down_part.astype(jnp.bfloat16), "tab").astype(jnp.float32),
        lax.psum(gain1_part.astype(jnp.bfloat16), "tab").astype(jnp.float32),
        lax.psum(bias1_part.astype(jnp.bfloat16), "tab").astype(jnp.float32),
        lax.psum(gain2_part.astype(jnp.bfloat16), "tab").astype(jnp.float32),
        lax.psum(bias2_part.astype(jnp.bfloat16), "tab").astype(jnp.float32),
        lax.psum(upbias_part.astype(jnp.bfloat16), "tab").astype(jnp.float32),
    )
    embed_all, squares_all, count_all = lax.psum((grad_w_emb, squares, live_rows), ("tab", "row"))
    rms = jnp.sqrt(squares_all / (count_all * dmodel))
    return (
        ctx_out,
        qry_out,
        ctx_feat_grad,
        qry_feat_grad,
        embed_all,
        gain1_all,
        bias1_all,
        qkv_all,
        out_all,
        gain2_all,
        bias2_all,
        up_all,
        upbias_all,
        down_all,
        rms,
    )


MESH = pl.DeviceIdType.MESH
LANES = 128
NT = (((1,), (1,)), ((), ()))


def lane_of(shape):
    return lax.broadcasted_iota(jnp.int32, shape, len(shape) - 1)


def split_three(values):
    high = values.astype(jnp.bfloat16)
    rest = values - high.astype(jnp.float32)
    mid = rest.astype(jnp.bfloat16)
    tail = (rest - mid.astype(jnp.float32)).astype(jnp.bfloat16)
    return (high, mid, tail)


def set_lanes(values, first, columns):
    lane = lane_of(values.shape)
    values = values.astype(jnp.float32)
    for i, column in enumerate(columns):
        values = jnp.where(lane == first + i, column.astype(jnp.float32), values)
    return values.astype(jnp.bfloat16)


def greet(peers):
    barrier = pltpu.get_barrier_semaphore()
    for peer in peers:
        pl.semaphore_signal(barrier, inc=1, device_id=peer, device_id_type=MESH)
    pl.semaphore_wait(barrier, len(peers))


def front_kernel(
    dims, feat_counts, counts, ctx_feat, qry_feat, w_emb_in, gain_in, bias_in, w_qkv,
    out_in, queries_out, keys_out, values_out, outs_out, feat_out, w_out, attn_out, own_feat, w_emb,
    by_slot, attn_all, feat_in, window, w_lanes, w_mine, queries, keys, values, outs, packed, load_sem, store_sem, send_sem, recv_sem,
):
    row_size, x_size, chunk, ctx_rows, local_rows, heads, groups = dims
    z_size = row_size // x_size
    total = keys.shape[1]
    pair = x_size * local_rows
    dmodel = w_emb.shape[1]
    width = heads * HEAD_DIM
    tab, row = lax.axis_index("tab"), lax.axis_index("row")
    z = row // x_size
    table, group = row // groups, lax.rem(row, groups)
    tables = own_feat.shape[0]
    row_peers = [(tab, lax.rem(row + k, row_size)) for k in range(1, row_size)]
    numbers = {}

    def remote(name, src, dst, peer):
        i = numbers.setdefault(name, len(numbers))
        return pltpu.make_async_remote_copy(
            src_ref=src, dst_ref=dst, send_sem=send_sem.at[i], recv_sem=recv_sem.at[i],
            device_id=peer, device_id_type=MESH,
        )

    def feat_copy(dt, dg):
        t, g = lax.rem(table + dt, tables), lax.rem(group + dg, groups)
        if dt == 0:
            return remote(("near", dg), own_feat.at[table], feat_in.at[row], (tab, table * groups + g))
        if dg == 0:
            return remote(("far", dt), own_feat.at[t], feat_in.at[row], (tab, t * groups + group))
        came = t * groups + group
        return remote(("passed", dt, dg), feat_in.at[came], feat_in.at[came], (tab, table * groups + g))

    def out_copy(shift):
        p = lax.rem(row + shift, row_size)
        return remote(("out", shift), packed.at[p], out_in.at[row], (tab, p))

    span = window.shape[2]
    first = (group * width) // LANES * LANES

    def window_copy(n):
        at = pl.ds(pl.multiple_of(n * dmodel + first, LANES), span)
        return pltpu.make_async_copy(w_qkv.at[:, at], window.at[n], load_sem.at[n])

    for n in range(3):
        window_copy(n).start()
    by_slot[...] = jnp.zeros_like(by_slot)
    slots = ctx_feat.shape[0]
    slot = lax.broadcasted_iota(jnp.int32, (slots, 1), 0)
    for t in range(tables):
        live = jnp.where(slot < feat_counts[t], 1.0, 0.0)
        by_slot[:slots, :ctx_rows] = ctx_feat[:, t].astype(jnp.float32) * live
        wide = by_slot[...].T
        own_feat[t, :ctx_rows] = wide[:ctx_rows].astype(jnp.bfloat16)
        lane = lax.broadcasted_iota(jnp.int32, qry_feat.shape[1:], 1)
        narrow = jnp.where(lane < feat_counts[t], qry_feat[t].astype(jnp.float32), 0.0)
        nothing = jnp.zeros((narrow.shape[0], LANES - slots), jnp.float32)
        own_feat[t, ctx_rows:] = jnp.concatenate([narrow, nothing], axis=1).astype(jnp.bfloat16)
    w_emb[...] = jnp.zeros_like(w_emb)
    w_emb[:slots] = w_emb_in[...]
    gain, bias = gain_in[...][None], bias_in[...][None]
    greet(row_peers)
    for dt in range(1, tables):
        feat_copy(dt, 0).start()
    for dg in range(1, groups):
        feat_copy(0, dg).start()
    feat_in[row] = own_feat[table]
    offset = group * width - first
    for n in range(3):
        window_copy(n).wait()
        wide = window[n]
        mine = wide[:, :width]
        for shift in range(HEAD_DIM, span - width + 1, HEAD_DIM):
            mine = jnp.where(offset == shift, wide[:, shift : shift + width], mine)
        w_mine[:, n * width : (n + 1) * width] = mine
        for h in range(heads):
            one = mine[:, h * HEAD_DIM : (h + 1) * HEAD_DIM]
            at = (n * heads + h) * LANES
            w_lanes[:, at : at + LANES] = jnp.concatenate([one, jnp.zeros_like(one)], axis=1)
    w_store = pltpu.make_async_copy(w_mine, w_out, store_sem.at[0])
    w_store.start()
    count = counts[table]

    near = groups // x_size

    def project(step, _):
        @pl.when(step == 1)
        def _():
            for dt in range(1, tables):
                feat_copy(tables - dt, 0).wait_recv()
                for dg in range(1, groups):
                    feat_copy(dt, dg).start()

        there = lax.rem(z // near + step // near, tables) * near + lax.rem(z + step, near)
        embeds = []
        for other in range(x_size):
            p = there * x_size + other
            ahead = lax.rem(p // groups - table + tables, tables)
            across = lax.rem(group - lax.rem(p, groups) + groups, groups)
            for dt in range(tables):
                for dg in range(1, groups):

                    @pl.when((ahead == dt) & (across == dg))
                    def _():
                        feat_copy(dt, dg).wait_recv()

            embeds.append(feat_in[p])
        rows_feat = jnp.concatenate(embeds, axis=0)
        embed = jnp.dot(rows_feat, w_emb[...], preferred_element_type=jnp.float32)
        center = embed - jnp.mean(embed, axis=-1, keepdims=True)
        inverse = lax.rsqrt(jnp.mean(center * center, axis=-1, keepdims=True) + EPS)
        attn_in = (center * inverse * gain + bias).astype(jnp.bfloat16)
        projected = jnp.dot(attn_in, w_lanes[...], preferred_element_type=jnp.float32)
        rows = pl.ds(pl.multiple_of(there * pair, LANES), pair)
        attn_all[rows] = attn_in
        lane = lane_of((pair, LANES))
        for h in range(heads):
            query = projected[:, h * LANES : (h + 1) * LANES] * HEAD_DIM ** (-0.5)
            queries[h, rows] = jnp.where(lane == HEAD_DIM, 1.0, query).astype(jnp.bfloat16)
        lane = lane_of((ctx_rows, LANES))
        for other in range(x_size):
            p = there * x_size + other
            key_rows = pl.ds(pl.multiple_of(p * ctx_rows, LANES), ctx_rows)
            position = p * ctx_rows + lax.broadcasted_iota(jnp.int32, (ctx_rows, LANES), 0)
            mask = jnp.where(position < count, 0.0, NEGATIVE)
            for h in range(heads):
                at = (heads + h) * LANES
                key = projected[other * local_rows : other * local_rows + ctx_rows, at : at + LANES]
                key = jnp.where(lane == HEAD_DIM, mask, key)
                key = jnp.where((lane > HEAD_DIM) & (lane < HEAD_DIM + 4), 1.0, key)
                keys[h, key_rows] = key.astype(jnp.bfloat16)
                at = (2 * heads + h) * LANES
                value = projected[other * local_rows : other * local_rows + ctx_rows, at : at + LANES]
                value = jnp.where((lane >= HEAD_DIM) & (lane < HEAD_DIM + 3), 1.0, value)
                values[h, key_rows] = value.astype(jnp.bfloat16)
        return 0

    lax.fori_loop(0, z_size, project, 0)
    stores = [
        pltpu.make_async_copy(src, dst, store_sem.at[i + 1])
        for i, (src, dst) in enumerate(
            ((keys, keys_out), (values, values_out), (feat_in, feat_out), (attn_all, attn_out))
        )
    ]
    for store in stores:
        store.start()
    whole = heads // 2

    def segment(step, _):
        k, h = step // heads, lax.rem(step, heads)
        there = lax.rem(z + k + 1, z_size)
        rows = pl.ds(pl.multiple_of(there * pair, LANES), pair)
        query = queries[h, rows]
        for i in range(total // chunk):
            at = pl.ds(i * chunk, chunk)
            scores = lax.dot_general(query, keys[h, at], NT, preferred_element_type=jnp.float32)
            top = jnp.max(scores, axis=-1, keepdims=True)
            if i:
                top = jnp.maximum(top, before)
            weights = jnp.exp(scores - top).astype(jnp.bfloat16)
            term = jnp.dot(weights, values[h, at], preferred_element_type=jnp.float32)
            summed = summed * jnp.exp(before - top) + term if i else term
            before = top
        sum_all = summed[:, HEAD_DIM : HEAD_DIM + 1]
        outs[h, rows] = (summed / sum_all).astype(jnp.bfloat16)
        queries[h, rows] = set_lanes(query, HEAD_DIM + 1, split_three(-(top + jnp.log(sum_all))))

        @pl.when(h == heads - 1)
        def _():
            for other in range(x_size):
                p = there * x_size + other
                at = pl.ds(pl.multiple_of(p * local_rows, 16), local_rows)
                parts = [outs[i, at, :HEAD_DIM] for i in range(heads)]
                for i in range(whole):
                    both = jnp.concatenate([parts[2 * i], parts[2 * i + 1]], axis=1)
                    packed[p, i * local_rows : (i + 1) * local_rows] = both
                if heads % 2:
                    last = parts[-1]
                    both = jnp.concatenate([last[: local_rows // 2], last[local_rows // 2 :]], axis=1)
                    packed[p, whole * local_rows :] = both
                ahead = lax.rem(p - row + row_size, row_size)
                for s in range(1, row_size):

                    @pl.when(ahead == s)
                    def _():
                        out_copy(s).start()

        return 0

    lax.fori_loop(0, z_size * heads, segment, 0)
    last = [
        pltpu.make_async_copy(queries, queries_out, store_sem.at[5]),
        pltpu.make_async_copy(outs, outs_out, store_sem.at[6]),
        pltpu.make_async_copy(packed.at[row], out_in.at[row], store_sem.at[7]),
    ]
    for store in last:
        store.start()
    for dt in range(tables):
        for dg in range(groups):
            if dt + dg:
                feat_copy(dt, dg).wait_send()
    for store in [w_store] + stores + last:
        store.wait()
    for s in range(1, row_size):
        out_copy(s).wait()


def front(feat_counts, counts, ctx_feat, qry_feat, w_emb, gain, bias, w_qkv, total_ctx, heads, groups, chunk, collective_id):
    row_size = lax.axis_size("row")
    tables, qry_rows, _ = qry_feat.shape
    dmodel = w_emb.shape[1]
    ctx_rows = total_ctx // row_size
    local_rows, slots = ctx_rows + qry_rows, LANES
    width = heads * HEAD_DIM
    x_size = 2
    span = -(-(width + (HEAD_DIM if width % LANES else 0)) // LANES) * LANES
    bf16 = lambda *shape: (shape, jnp.bfloat16)
    by_query, by_key = (heads, row_size * local_rows, LANES), (heads, total_ctx, LANES)
    block = (row_size, -(-heads * local_rows // 2), LANES)
    feat = (row_size, local_rows, slots)
    vmem = pl.BlockSpec(memory_space=pltpu.VMEM)
    anywhere = pl.BlockSpec(memory_space=pl.ANY)
    scratch = [
        feat, (3, dmodel, span), (dmodel, 3 * heads * LANES), (dmodel, 3 * width),
        by_query, by_key, by_key, by_query, block,
    ]
    return pl.pallas_call(
        functools.partial(front_kernel, (row_size, x_size, chunk, ctx_rows, local_rows, heads, groups)),
        out_shape=[
            jax.ShapeDtypeStruct(s, jnp.bfloat16)
            for s in (
                block, by_query, by_key, by_key, by_query, feat, (dmodel, 3 * width),
                (row_size * local_rows, dmodel),
                (tables, local_rows, slots), (slots, dmodel),
            )
        ],
        in_specs=[pl.BlockSpec(memory_space=pltpu.SMEM)] * 2 + [vmem] * 5 + [anywhere],
        out_specs=[anywhere] * 8 + [vmem] * 2,
        scratch_shapes=[
            pltpu.VMEM((slots, ctx_rows), jnp.float32),
            pltpu.VMEM((row_size * local_rows, dmodel), jnp.bfloat16),
        ] + [pltpu.VMEM(s, jnp.bfloat16) for s in scratch] + [
            pltpu.SemaphoreType.DMA((3,)),
            pltpu.SemaphoreType.DMA((8,)),
            pltpu.SemaphoreType.DMA((2 * (row_size - 1),)),
            pltpu.SemaphoreType.DMA((2 * (row_size - 1),)),
        ],
        compiler_params=pltpu.CompilerParams(
            collective_id=collective_id, has_side_effects=True, vmem_limit_bytes=60 * 2**20
        ),
        name="front",
    )(feat_counts, counts, ctx_feat, qry_feat, w_emb, gain, bias, w_qkv)


def gelu_parts(values):
    below = 0.5 + 0.5 * lax.erf(values * math.sqrt(0.5))
    return (below, values * jnp.exp(-0.5 * values * values) * (1.0 / math.sqrt(2.0 * math.pi)))


def middle_kernel(
    dims, ctx_count, qry_count, own_feat, w_emb, gain_in, bias_in, b_up, out_in, w_out_hbm, w_up_hbm, w_down_hbm, ctx_cot, qry_cot,
    ctx_out, qry_out, g_in, up_half, down_half, out_half, d_branch_out, vectors, sums,
    w_out, w_up, w_down, attn_in, cot, attn_low, mlp_in, mlp_in_t, mixed, normed, d_mlp_in, act, d_hidden, d_up_bias,
    packed, up, down, out, up_in0, down_in0, out_in0, load_sem, store_sem, send_sem, recv_sem,
):
    row_size, ctx_rows, local_rows, tables, groups, heads, tile = dims
    rows = tables * local_rows
    qry_rows = local_rows - ctx_rows
    dmodel, hidden_size = w_up.shape
    tiles = hidden_size // tile
    tab, row = lax.axis_index("tab"), lax.axis_index("row")
    core = lax.rem(tab, 2)
    core_peer = (tab ^ 1, row)
    row_peers = [(tab, lax.rem(row + k, row_size)) for k in range(1, row_size)]
    numbers = {}

    def remote(name, src, dst, peer):
        i = numbers.setdefault(name, len(numbers))
        return pltpu.make_async_remote_copy(
            src_ref=src, dst_ref=dst, send_sem=send_sem.at[i], recv_sem=recv_sem.at[i],
            device_id=peer, device_id_type=MESH,
        )

    gain, bias = gain_in[...][None], bias_in[...][None]
    loads = [
        pltpu.make_async_copy(src, dst, load_sem.at[i])
        for i, (src, dst) in enumerate(
            [(out_in, attn_in), (w_out_hbm, w_out), (w_up_hbm, w_up), (w_down_hbm, w_down)]
            + [(ctx_cot.at[t], cot.at[pl.ds(t * local_rows, ctx_rows)]) for t in range(tables)]
            + [(qry_cot.at[t], cot.at[pl.ds(t * local_rows + ctx_rows, qry_rows)]) for t in range(tables)]
        )
    ]
    for load in loads:
        load.start()
    greet([core_peer] + row_peers)

    at = lax.broadcasted_iota(jnp.int32, (local_rows, 1), 0)
    live = []
    for t in range(tables):
        place = jnp.where(at < ctx_rows, row * ctx_rows + at, row * qry_rows + at - ctx_rows)
        limit = jnp.where(at < ctx_rows, ctx_count[t], qry_count[t])
        live.append(jnp.where(place < limit, 1.0, 0.0))
    valid = jnp.concatenate(live, axis=0)
    own_rows = jnp.concatenate([own_feat[t] for t in range(tables)], axis=0)
    embed = jnp.dot(own_rows, w_emb[...], preferred_element_type=jnp.float32)

    whole = heads // 2
    loads[0].wait()
    for t in range(tables):
        parts = []
        for g in range(groups):
            block = attn_in[t * groups + g]
            for h in range(whole):
                parts.append(block[h * local_rows : (h + 1) * local_rows])
            if heads % 2:
                last = block[whole * local_rows :]
                parts.append(jnp.concatenate([last[:, :HEAD_DIM], last[:, HEAD_DIM:]], axis=0))
        attn_low[t * local_rows : (t + 1) * local_rows] = jnp.concatenate(parts, axis=1)
    loads[1].wait()
    branch = jnp.dot(attn_low[...], w_out[...], preferred_element_type=jnp.float32)
    summed = embed + branch
    mixed[...] = summed
    square_embed = jnp.sum(valid * embed * embed)
    square_branch = jnp.sum(valid * branch * branch)
    center = summed - jnp.mean(summed, axis=-1, keepdims=True)
    inverse = lax.rsqrt(jnp.mean(center * center, axis=-1, keepdims=True) + EPS)
    normed[...] = center * inverse
    mlp_in[...] = (normed[...] * gain + bias).astype(jnp.bfloat16)
    for load in loads[2:]:
        load.wait()
    cot[...] = (cot[...].astype(jnp.float32) * valid).astype(jnp.bfloat16)
    d_mlp_in[...] = jnp.zeros_like(d_mlp_in)

    def columns(i):
        return pl.ds(pl.multiple_of(i * tile, LANES), tile)

    def first(i, _):
        at = columns(i)
        hidden = jnp.dot(mlp_in[...], w_up[:, at], preferred_element_type=jnp.float32) + b_up[:, at]
        d_act = lax.dot_general(cot[...], w_down[at], NT, preferred_element_type=jnp.float32)
        below, slope = gelu_parts(hidden)
        act[:, at] = (hidden * below).astype(jnp.bfloat16)
        grad = (d_act * (below + slope)).astype(jnp.bfloat16)
        d_hidden[:, at] = grad
        d_up_bias[:, at] = jnp.sum(grad.astype(jnp.float32), axis=0, keepdims=True)
        d_mlp_in[...] += lax.dot_general(grad, w_up[:, at], NT, preferred_element_type=jnp.float32)
        return 0

    lax.fori_loop(0, tiles, first, 0)
    grad_in = d_mlp_in[...]
    scaled = grad_in * gain
    inner = (
        scaled
        - jnp.mean(scaled, axis=-1, keepdims=True)
        - normed[...] * jnp.mean(scaled * normed[...], axis=-1, keepdims=True)
    )
    vectors[...] = jnp.zeros_like(vectors)
    vectors[2:3] = jnp.sum(grad_in * normed[...], axis=0, keepdims=True)
    vectors[3:4] = jnp.sum(grad_in, axis=0, keepdims=True)
    for i in range(hidden_size // dmodel):
        vectors[4 + i : 5 + i] = d_up_bias[:, i * dmodel : (i + 1) * dmodel]
    d_branch = (cot[...].astype(jnp.float32) + inverse * inner).astype(jnp.bfloat16)
    for t in range(tables):
        d_branch_out[t] = d_branch[t * local_rows : (t + 1) * local_rows]
    d_attn = lax.dot_general(d_branch, w_out[...], NT, preferred_element_type=jnp.float32).astype(jnp.bfloat16)
    width = heads * HEAD_DIM
    for t in range(tables):
        for g in range(groups):
            block = d_attn[t * local_rows : (t + 1) * local_rows, g * width : (g + 1) * width]
            p = t * groups + g
            for h in range(whole):
                packed[p, h * local_rows : (h + 1) * local_rows] = block[:, h * LANES : (h + 1) * LANES]
            if heads % 2:
                last = block[:, whole * LANES :]
                both = jnp.concatenate([last[: local_rows // 2], last[local_rows // 2 :]], axis=1)
                packed[p, whole * local_rows :] = both
    own_g = pltpu.make_async_copy(packed.at[row], g_in.at[row], store_sem.at[0])
    own_g.start()
    g_copies = [remote(("g", k), packed.at[peer[1]], g_in.at[row], peer) for k, peer in enumerate(row_peers)]
    for copy in g_copies:
        copy.start()

    def half(ref, which):
        size = ref.shape[1] // 2
        return pl.ds(pl.multiple_of(which * size, 16), size)

    shard = dmodel // row_size
    d_out = jnp.dot(attn_low[...].T, d_branch, preferred_element_type=jnp.float32).astype(jnp.bfloat16)
    for p in range(row_size):
        out[p] = d_out[p * shard : (p + 1) * shard]
    out_copy = remote("out", out.at[:, half(out, 1 - core)], out_in0, core_peer)
    out_copy.start()
    mlp_in_t[...] = mlp_in[...].T
    d_mlp_in[...] = jnp.zeros_like(d_mlp_in)
    per = hidden_size // row_size

    def span_of(p):
        return pl.ds(pl.multiple_of(p * per, LANES), per)

    def pieces(p):
        at = span_of(p)
        return [
            pltpu.make_async_remote_copy(
                src_ref=src, dst_ref=dst, send_sem=send_sem.at[first + p], recv_sem=recv_sem.at[first + p],
                device_id=core_peer, device_id_type=MESH,
            )
            for src, dst, first in (
                (down.at[p, half(down, 1 - core)], down_in0.at[p], row_size),
                (up.at[:, half(up, 1 - core), at], up_in0.at[:, :, at], 2 * row_size),
            )
        ]

    def stored(p):
        at = span_of(p)
        return [
            pltpu.make_async_copy(down_in0.at[p], down_half.at[p], store_sem.at[2 + p]),
            pltpu.make_async_copy(up_in0.at[:, :, at], up_half.at[:, :, at], store_sem.at[2 + row_size + p]),
        ]

    def add_piece(p):
        at = span_of(p)
        for copy in pieces(p):
            copy.wait()
        down_in0[p] = down_in0[p] + down[p, half(down, core)]
        for q in range(row_size):
            up_in0[q, :, at] = up_in0[q, :, at] + up[q, half(up, core), at]
        for store in stored(p):
            store.start()

    def second(p, _):
        at = span_of(p)
        piece = act[:, at]
        down[p] = jnp.dot(piece.T, cot[...], preferred_element_type=jnp.float32).astype(jnp.bfloat16)
        d_up = jnp.dot(mlp_in_t[...], d_hidden[:, at], preferred_element_type=jnp.float32).astype(jnp.bfloat16)
        for q in range(row_size):
            up[q, :, at] = d_up[q * shard : (q + 1) * shard]
        for copy in pieces(p):
            copy.start()
        d_mlp_in[...] += jnp.dot(piece, w_down[at], preferred_element_type=jnp.float32)

        @pl.when(p > 0)
        def _():
            add_piece(p - 1)

        return 0

    lax.fori_loop(0, row_size, second, 0)
    add_piece(row_size - 1)
    out_copy.wait()

    @pl.loop(0, row_size)
    def _(p):
        out_in0[p] = out_in0[p] + out[p, half(out, core)]

    out_store = pltpu.make_async_copy(out_in0, out_half, store_sem.at[1])
    out_store.start()
    mlp = d_mlp_in[...]
    result = (mixed[...] + mlp) * valid
    square_mlp = jnp.sum(valid * mlp * mlp)
    square_result = jnp.sum(result * result)
    low = result.astype(jnp.bfloat16)
    for t in range(tables):
        ctx_out[t] = low[t * local_rows : t * local_rows + ctx_rows]
        qry_out[t] = low[t * local_rows + ctx_rows : (t + 1) * local_rows]
    lane = lane_of(sums.shape)
    parts = (square_embed, square_branch, square_mlp, square_result, jnp.sum(valid))
    total = jnp.zeros(sums.shape, jnp.float32)
    for i, part in enumerate(parts):
        total = jnp.where(lane == i, part, total)
    sums[...] = total
    for p in range(row_size):
        for store in stored(p):
            store.wait()
    out_store.wait()
    own_g.wait()
    for copy in g_copies:
        copy.wait()


def middle(ctx_count, qry_count, own_feat, w_emb, gain, bias, b_up, out_in, w_out, w_up, w_down, ctx_cot, qry_cot,
           groups, heads, tile, collective_id):
    row_size = lax.axis_size("row")
    tables, local_rows, _ = own_feat.shape
    ctx_rows = ctx_cot.shape[1]
    rows = tables * local_rows
    dmodel, hidden_size = w_up.shape
    shard, per = dmodel // row_size, hidden_size // row_size
    halves = [(row_size, shard // 2, hidden_size), (row_size, per // 2, dmodel), (row_size, shard // 2, dmodel)]
    vmem = pl.BlockSpec(memory_space=pltpu.VMEM)
    smem = pl.BlockSpec(memory_space=pltpu.SMEM)
    anywhere = pl.BlockSpec(memory_space=pl.ANY)
    bf16 = lambda *shape: pltpu.VMEM(shape, jnp.bfloat16)
    f32 = lambda *shape: pltpu.VMEM(shape, jnp.float32)
    sends = 3 * row_size
    return pl.pallas_call(
        functools.partial(middle_kernel, (row_size, ctx_rows, local_rows, tables, groups, heads, tile)),
        out_shape=[jax.ShapeDtypeStruct(s, jnp.bfloat16) for s in (ctx_cot.shape, qry_cot.shape, out_in.shape, *halves)]
        + [jax.ShapeDtypeStruct((tables, local_rows, dmodel), jnp.bfloat16)]
        + [jax.ShapeDtypeStruct((4 + hidden_size // dmodel, dmodel), jnp.float32)]
        + [jax.ShapeDtypeStruct((8, LANES), jnp.float32)],
        in_specs=[smem] * 2 + [vmem] * 5 + [anywhere] * 6,
        out_specs=[vmem] * 2 + [anywhere] * 4 + [vmem] * 3,
        scratch_shapes=[
            bf16(*w_out.shape), bf16(*w_up.shape), bf16(*w_down.shape), bf16(*out_in.shape), bf16(rows, dmodel),
            bf16(rows, dmodel), bf16(rows, dmodel), bf16(dmodel, rows),
            f32(rows, dmodel), f32(rows, dmodel), f32(rows, dmodel),
            bf16(rows, hidden_size), bf16(rows, hidden_size), f32(1, hidden_size),
            bf16(*out_in.shape),
            bf16(row_size, shard, hidden_size), bf16(row_size, per, dmodel), bf16(row_size, shard, dmodel),
            *[bf16(*s) for s in halves],
            pltpu.SemaphoreType.DMA((4 + 2 * tables,)),
            pltpu.SemaphoreType.DMA((2 + 2 * row_size,)),
            pltpu.SemaphoreType.DMA((sends,)),
            pltpu.SemaphoreType.DMA((sends,)),
        ],
        compiler_params=pltpu.CompilerParams(
            collective_id=collective_id, has_side_effects=True, vmem_limit_bytes=62 * 2**20
        ),
        name="middle",
    )(ctx_count, qry_count, own_feat, w_emb, gain, bias, b_up, out_in, w_out, w_up, w_down, ctx_cot, qry_cot)


def tile_sum(parts):
    total = parts[0]
    for part in parts[1:]:
        total = total + part
    return total


ROW_AXES = ("x", "near", "far")
ATTEND_STEPS = ((5, 1, 0), (5, 2, 0), (5, 3, 0), (5, 0, 0), (5, 4, 0), (7, 1, 1), (7, 2, 1), (7, 3, 1), (8, 0, 1), (8, 4, 1), (9, 1, 2), (9, 2, 2), (9, 3, 2), (10, 0, 2), (10, 4, 2))
CHAIN_STEPS = ((9, 0, 1), (11, 0, 2))
LAST_STEPS = ((0, 0, 3), (0, 1, 1))
GATHER_STEP = 0


def plan_streams(shapes):
    (up_rows, up_wide), (down_rows, down_wide), (out_rows, out_wide) = shapes
    cut = up_wide * 7 // 12 // (2 * LANES) * 2 * LANES
    deep = down_rows * 2 // 3 // 16 * 16
    return (
        ("up_y", "up", (0, up_rows), (0, cut), ("y", "x", "near", "far")),
        ("down_x", "down", (0, deep), (0, down_wide), ("x", "near", "y", "far")),
        ("up_z", "up", (0, up_rows), (cut, up_wide - cut), ("near", "y", "x", "far")),
        ("down_z", "down", (deep, down_rows - deep), (0, down_wide), ("near", "y", "x", "far")),
        ("out_y", "out", (0, out_rows), (0, out_wide), ("y", "x", "near", "far")),
    )


def back_kernel(
    dims, counts, up0, down0, out0, queries_hbm, keys_hbm, values_hbm, outs_hbm, attn_hbm, g_hbm, feat_hbm, w_mine_hbm, branch_hbm,
    w_emb, gain_in, bias_in, own_feat, vectors, sums,
    ctx_grad, qry_grad, emb_all, own_all, qkv_all, out_all, up_all, down_all,
    queries, keys, values, outs, attn_in, g_in, feat, w_mine, d_branch, grads, d_q, d_qt, d_kt, d_vt, d_k, d_v, terms, terms_x, terms_z, terms_far, d_emb, d_gain, d_bias,
    emb_own, emb_in0, sums_in0, sums0, emb_in1, sums_in1, emb1, sums1, emb_in2, sums_in2, emb2, emb3, *rest,
):
    row_size, x_size, chunk, ctx_rows, local_rows, plan = dims
    gain, bias = gain_in[...][None], bias_in[...][None]
    buffers, (load_sem, send_sem, recv_sem) = rest[:-3], rest[-3:]
    chains, buffers = (buffers[:6], buffers[6:12]), buffers[12:]
    z_size = row_size // x_size
    heads, total, _ = keys.shape
    pair = x_size * local_rows
    tab, row = lax.axis_index("tab"), lax.axis_index("row")
    core, y = lax.rem(tab, 2), tab // 2
    x, z = lax.rem(row, x_size), row // x_size
    core_peer, y_peer, x_peer = (tab ^ 1, row), (tab ^ 2, row), (tab, row ^ 1)
    row_peers = [(tab, lax.rem(row + k, row_size)) for k in range(1, row_size)]
    cross_peers = [(tab ^ 1, peer[1]) for peer in row_peers]
    numbers = {}

    def remote(name, src, dst, peer):
        i = numbers.setdefault(name, len(numbers))
        return pltpu.make_async_remote_copy(
            src_ref=src, dst_ref=dst, send_sem=send_sem.at[i], recv_sem=recv_sem.at[i],
            device_id=peer, device_id_type=MESH,
        )

    def half(rows, which):
        return pl.ds(pl.multiple_of(which * (rows // 2), 16), rows // 2)

    def columns(ref, which):
        wide = ref.shape[-1] // 2
        return pl.ds(pl.multiple_of(which * wide, LANES), wide)

    axes = {"y": (y, y_peer)}
    for bit, axis in enumerate(ROW_AXES):
        axes[axis] = (lax.rem(row // 2**bit, 2), (tab, row ^ 2**bit))
    sources = {"up": up0, "down": down0, "out": out0}
    streams = []
    for number, (name, source, rows, cols, order) in enumerate(plan):
        ref = sources[source].reshape(2, 2, 2, *sources[source].shape[1:])
        ref = ref.at[:, :, :, pl.ds(*rows), pl.ds(*cols)]
        dims_left, steps = list(ROW_AXES[::-1]), []
        shape = [2, 2, 2, rows[1], cols[1]]
        landing = buffers[6 * number : 6 * number + 6]
        for k, axis in enumerate(order):
            mine, (here, peer) = [], axes[axis]
            if axis == "y":
                wide = shape[-1] // 2
                kept, sent = (
                    (slice(None),) * (len(shape) - 1) + (pl.ds(pl.multiple_of(which * wide, LANES), wide),)
                    for which in (here, 1 - here)
                )
                shape = shape[:-1] + [wide]
            else:
                at = dims_left.index(axis)
                kept, sent = ((slice(None),) * at + (which,) for which in (here, 1 - here))
                dims_left.pop(at)
                shape = shape[:at] + shape[at + 1 :]
            copy = remote((name, axis), ref.at[sent], landing[k], peer)
            own = pltpu.make_async_copy(ref.at[kept], landing[4], load_sem.at[9 + number]) if k == 0 else None
            steps.append((copy, own, ref.at[kept] if k else landing[4], landing[k]))
            ref = landing[k]
        streams.append((steps, landing[5]))
    loads = [
        pltpu.make_async_copy(src, dst, load_sem.at[i])
        for i, (src, dst) in enumerate(
            (
                (g_hbm, g_in), (outs_hbm, outs), (queries_hbm, queries), (keys_hbm, keys), (values_hbm, values),
                (attn_hbm, attn_in), (feat_hbm, feat), (w_mine_hbm, w_mine), (branch_hbm, d_branch),
            )
        )
    ]

    def advance(number, k):
        steps, last = streams[number]
        copy, own, mine, taken = steps[k]
        copy.wait()
        if own is not None:
            own.wait()
        if k + 1 < len(steps):
            lead = taken.shape[:-2]
            size = math.prod(lead)

            @pl.loop(0, size)
            def _(i):
                at = []
                for extent in lead[::-1]:
                    at.insert(0, lax.rem(i, extent))
                    i = i // extent
                taken[tuple(at)] = taken[tuple(at)] + mine[tuple(at)]

            steps[k + 1][0].start()
        else:
            last[core, y] = taken[...] + mine[...]

    lasts = [last for _, last in streams]

    def to_y():
        return [remote(("to_y", i), last.at[core, y], last.at[core, y], y_peer) for i, last in enumerate(lasts)]

    def to_core(which):
        at = y if which == 0 else 1 - y
        return [
            remote(("to_core", which, i), last.at[core, at], last.at[core, at], core_peer)
            for i, last in enumerate(lasts)
        ]

    def start(copies):
        for copy in copies:
            copy.start()

    def wait(copies):
        for copy in copies:
            copy.wait()

    start(loads)
    greet([core_peer, y_peer] + row_peers + cross_peers)
    for steps, _ in streams:
        steps[0][0].start()
        steps[0][1].start()
    chains[1][0][...] = jnp.zeros_like(chains[1][0])

    shard = chains[0][0].shape[1]
    groups = chains[0][3].shape[0]

    def chain_core(i):
        pay, taken = chains[i][:2]
        return [remote(("core", i), pay.at[:, half(shard, 1 - core)], taken, core_peer)]

    def chain_row(i):
        _, ours, taken = chains[i][:3]
        return [remote(("row", i, k), ours.at[peer[1]], taken.at[row], peer) for k, peer in enumerate(row_peers)]

    def chain_y(i):
        return [remote(("y", i), chains[i][3], chains[i][4], y_peer)]

    def chain_last(i):
        last = chains[i][5]
        return [remote(("last", i), last.at[core], last.at[core], core_peer)]

    def link(i, k):
        pay, ours, came, total_own, came_y, last = chains[i]
        if k == 1:
            wait(chain_core(i))
            ours[...] = ours[...] + pay[:, half(shard, core)]
            start(chain_row(i))
            came[row] = ours[row]
        elif k == 2:
            wait(chain_row(i))
            for g in range(groups):
                total_own[g] = tile_sum(
                    [came[g + t * groups].astype(jnp.float32) for t in range(row_size // groups)]
                ).astype(jnp.bfloat16)
            start(chain_y(i))
        elif k == 3:
            wait(chain_y(i))
            last[core] = total_own[...] + came_y[...]
            start(chain_last(i))
        else:
            wait(chain_last(i))

    def finish_head(h):
        d_k[h] = d_kt[h].T.astype(jnp.bfloat16)
        d_v[h] = d_vt[h].T.astype(jnp.bfloat16)
        both = jnp.concatenate([d_kt[h], d_vt[h]], axis=0).astype(jnp.bfloat16)
        from_keys = tile_sum([
            jnp.dot(
                both[:, p * ctx_rows : (p + 1) * ctx_rows],
                attn_in[p * local_rows : p * local_rows + ctx_rows],
                preferred_element_type=jnp.float32,
            )
            for p in range(row_size)
        ])
        from_queries = jnp.dot(d_qt[...], attn_in[...], preferred_element_type=jnp.float32)
        grad = jnp.concatenate([from_queries, from_keys], axis=0).T.astype(jnp.bfloat16)
        for one in range(heads):
            i = one // (heads - 1)
            pay = chains[i][0]
            each = HEAD_DIM if i else (heads - 1) * HEAD_DIM
            first = 0 if i else one * HEAD_DIM

            @pl.when(h == one)
            def _():
                for n in range(3):
                    piece = grad[:, n * HEAD_DIM : (n + 1) * HEAD_DIM]
                    for p in range(row_size):
                        pay[p, :, n * each + first : n * each + first + HEAD_DIM] = piece[p * shard : (p + 1) * shard]
                if one >= heads - 2:
                    start(chain_core(i))

    d_kt[...] = jnp.zeros_like(d_kt)
    d_vt[...] = jnp.zeros_like(d_vt)
    whole = heads // 2

    def unpack(p):
        packed = g_in[p]
        parts = []
        for h in range(whole):
            tile = packed[h * local_rows : (h + 1) * local_rows]
            parts += [tile[:, :HEAD_DIM], tile[:, HEAD_DIM:]]
        if heads % 2:
            tile = packed[whole * local_rows :]
            parts.append(jnp.concatenate([tile[:, :HEAD_DIM], tile[:, HEAD_DIM:]], axis=0))
        rows = pl.ds(pl.multiple_of(p * local_rows, 16), local_rows)
        for h, part in enumerate(parts):
            part = part.astype(jnp.float32)
            result = outs[h, rows, :HEAD_DIM].astype(jnp.float32)
            inner = jnp.sum(part * result, axis=-1, keepdims=True)
            wide = jnp.concatenate([part, jnp.zeros_like(part)], axis=-1)
            grads[h, rows] = set_lanes(wide, HEAD_DIM, split_three(-inner))

    def segment(step, _):
        h, k = step // z_size, lax.rem(step, z_size)
        there = k
        rows = pl.ds(pl.multiple_of(there * pair, LANES), pair)

        for at, i, n in CHAIN_STEPS:

            @pl.when(step == at)
            def _():
                link(i, n)

        for at, number, n in ATTEND_STEPS:

            @pl.when(step == at)
            def _():
                advance(number, n)

        query, grad = queries[h, rows], grads[h, rows]
        query_t = query[:, :HEAD_DIM].T
        grad_t = grad[:, :HEAD_DIM].T
        d_query = jnp.zeros((pair, LANES), jnp.float32)
        for i in range(total // chunk):
            at = pl.ds(i * chunk, chunk)
            key, value = keys[h, at], values[h, at]
            probs = jnp.exp(lax.dot_general(query, key, NT, preferred_element_type=jnp.float32))
            d_probs = lax.dot_general(grad, value, NT, preferred_element_type=jnp.float32)
            d_scores = (probs * d_probs).astype(jnp.bfloat16)
            d_vt[h, :, at] += jnp.dot(grad_t, probs.astype(jnp.bfloat16), preferred_element_type=jnp.float32)
            d_kt[h, :, at] += jnp.dot(query_t, d_scores, preferred_element_type=jnp.float32)
            d_query += jnp.dot(d_scores, key, preferred_element_type=jnp.float32)
        d_query = (d_query[:, :HEAD_DIM] * HEAD_DIM ** (-0.5)).astype(jnp.bfloat16)
        d_q[h, rows] = d_query
        d_qt[:, rows] = d_query.T

        @pl.when(step == z_size - 1)
        def _():
            wait(loads[5:])

        @pl.when(k == z_size - 1)
        def _():
            finish_head(h)

        return 0

    wait(loads[:2])
    for p in range(row_size):
        unpack(p)
    wait(loads[2:5])
    lax.fori_loop(0, z_size * heads, segment, 0)

    d_emb[...] = jnp.zeros_like(d_emb)
    d_gain[...] = jnp.zeros_like(d_gain)
    d_bias[...] = jnp.zeros_like(d_bias)

    near_bit, far_bit = lax.rem(z, 2), z // 2
    near_peer, far_peer = (tab, row ^ 2), (tab, row ^ 4)

    def term_x(k):
        return remote(("term_x", k), terms.at[k, 1 - x], terms_x.at[k], x_peer)

    def term_near(k):
        return remote(("term_near", k), terms.at[k, x], terms_z.at[k], near_peer)

    def term_far():
        return remote("term_far", terms.at[2, x], terms_far, far_peer)

    def term_sum(k):
        term_x(k).wait()
        total = terms[k, x].astype(jnp.float32) + terms_x[k].astype(jnp.float32)
        if k >= 2:
            term_near(k - 2).wait()
            total = total + terms_z[k - 2].astype(jnp.float32)
        terms[k, x] = total.astype(jnp.bfloat16)
        if k < 2:
            term_near(k).start()
        elif k == 2:
            term_far().start()

    def project(step, _):
        there = lax.rem(far_bit + step + 1, 2) * 2 + lax.rem(near_bit + step // 2 + 1, 2)
        pieces, embeds = [], []
        for other in range(x_size):
            p = there * x_size + other
            rows = pl.ds(pl.multiple_of(p * local_rows, 16), local_rows)
            key_rows = pl.ds(pl.multiple_of(p * ctx_rows, 16), ctx_rows)
            parts = [d_q[h, rows] for h in range(heads)]
            nothing = jnp.zeros((local_rows - ctx_rows, HEAD_DIM), jnp.bfloat16)
            for ref in (d_k, d_v):
                parts += [jnp.concatenate([ref[h, key_rows], nothing], axis=0) for h in range(heads)]
            pieces.append(jnp.concatenate(parts, axis=1))
            embeds.append(feat[p])
        d_three = jnp.concatenate(pieces, axis=0)
        rows_feat = jnp.concatenate(embeds, axis=0)
        embed = jnp.dot(rows_feat, w_emb[...], preferred_element_type=jnp.float32)
        center = embed - jnp.mean(embed, axis=-1, keepdims=True)
        inverse = lax.rsqrt(jnp.mean(center * center, axis=-1, keepdims=True) + EPS)
        normed = center * inverse
        d_in = lax.dot_general(d_three, w_mine[...], NT, preferred_element_type=jnp.float32)
        d_gain[...] += jnp.sum(d_in * normed, axis=0, keepdims=True)
        d_bias[...] += jnp.sum(d_in, axis=0, keepdims=True)
        scaled = d_in * gain
        inner = (
            scaled
            - jnp.mean(scaled, axis=-1, keepdims=True)
            - normed * jnp.mean(scaled * normed, axis=-1, keepdims=True)
        )
        d_norm = (inverse * inner).astype(jnp.bfloat16)
        term = lax.dot_general(d_norm, w_emb[...], NT, preferred_element_type=jnp.float32).astype(jnp.bfloat16)
        d_emb[...] += jnp.dot(rows_feat.T, d_norm, preferred_element_type=jnp.float32)
        for other in range(x_size):
            terms[step, other] = term[other * local_rows : (other + 1) * local_rows]
        for k in range(z_size):

            @pl.when(step == k)
            def _():
                term_x(k).start()
                if k:
                    term_sum(k - 1)

        @pl.when(step == GATHER_STEP)
        def _():
            for number in range(len(streams)):
                advance(number, 3)
            start(to_y())
            start(to_core(0))

        for at, i, n in LAST_STEPS:

            @pl.when(step == at)
            def _():
                link(i, n)

        return 0

    lax.fori_loop(0, z_size, project, 0)

    own_rows = jnp.concatenate([own_feat[t] for t in range(own_feat.shape[0])], axis=0)
    own_d = jnp.concatenate([d_branch[t] for t in range(own_feat.shape[0])], axis=0)
    d_own = d_emb[...] + jnp.dot(own_rows.T, own_d, preferred_element_type=jnp.float32)
    slots_all = d_own.shape[0]
    spare = lax.broadcasted_iota(jnp.int32, d_own.shape, 0) - (slots_all - vectors.shape[0])
    d_own = jnp.where(spare == 0, d_gain[...], d_own)
    d_own = jnp.where(spare == 1, d_bias[...], d_own)
    for i in range(2, vectors.shape[0]):
        d_own = jnp.where(spare == i, vectors[i : i + 1], d_own)
    emb_rows = emb_own.shape[1]
    for p in range(row_size):
        emb_own[p] = d_own[p * emb_rows : (p + 1) * emb_rows].astype(jnp.bfloat16)

    def tail_core():
        return [
            remote("emb_core", emb_own.at[:, :, columns(emb_own, 1 - core)], emb_in0, core_peer),
            remote("sums_core", sums, sums_in0, core_peer),
        ]

    def tail_row():
        copies = []
        for k, peer in enumerate(row_peers):
            copies += [
                remote(("emb_row", k), emb_in0.at[peer[1]], emb_in1.at[row], peer),
                remote(("sums_row", k), sums0, sums_in1.at[row], peer),
            ]
        return copies

    def tail_y():
        return [remote("emb_y", emb1, emb_in2, y_peer), remote("sums_y", sums1, sums_in2, y_peer)]

    at_core = columns(emb_own, core)

    def tail_all():
        peers = row_peers + [core_peer] + cross_peers
        return [
            remote(("emb_all", k), emb2, emb3.at[row, :, at_core], peer) for k, peer in enumerate(peers)
        ]

    start(tail_core())
    link(1, 2)
    wait(tail_core())
    emb_in0[...] = emb_in0[...] + emb_own[:, :, at_core]
    sums0[...] = sums[...] + sums_in0[...]
    start(tail_row())
    emb_in1[row] = emb_in0[row]
    sums_in1[row] = sums0[...]
    wait(to_y())
    start(to_core(1))

    term_sum(z_size - 1)
    term_far().wait()
    for t in range(own_feat.shape[0]):
        term = lax.dot_general(d_branch[t], w_emb[...], NT, preferred_element_type=jnp.float32)
        from_heads = jnp.where(far_bit == t, terms[z_size - 1, x].astype(jnp.float32), terms_far[...].astype(jnp.float32))
        term = term + from_heads
        slots = qry_grad.shape[2]
        lane = lane_of(term.shape)
        term = jnp.where(lane < counts[t], term, 0.0)
        ctx_grad[:, t] = term[:ctx_rows].T[:slots].astype(jnp.bfloat16)
        qry_grad[t] = term[ctx_rows:, :slots].astype(jnp.bfloat16)

    wait(tail_row())
    emb1[...] = tile_sum([emb_in1[p].astype(jnp.float32) for p in range(row_size)]).astype(jnp.bfloat16)
    sums1[...] = tile_sum([sums_in1[p] for p in range(row_size)])
    start(tail_y())
    link(1, 3)
    wait(tail_y())
    emb2[...] = emb1[...] + emb_in2[...]
    sums_all = sums1[...] + sums_in2[...]
    start(tail_all())
    emb3[row, :, at_core] = emb2[...]
    link(0, 4)
    link(1, 4)
    for i in range(2):
        parts = []
        for n in range(3):
            for g in range(groups):
                for h in range(heads):
                    which = h // (heads - 1)
                    each = HEAD_DIM if which else (heads - 1) * HEAD_DIM
                    first = n * each + (0 if which else h * HEAD_DIM)
                    parts.append(chains[which][5][i, g][:, first : first + HEAD_DIM])
        qkv_all[i * (shard // 2) : (i + 1) * (shard // 2)] = jnp.concatenate(parts, axis=1)
    wait(to_core(0))
    wait(to_core(1))
    results = {"up": up_all, "down": down_all, "out": out_all}
    for (_, source, rows, cols, _), last in zip(plan, lasts):
        deep, wide = last.shape[2:]
        half_rows = sources[source].shape[1]
        for i in range(2):
            for j in range(2):
                down_at, across = i * half_rows + rows[0], cols[0] + j * wide
                results[source][down_at : down_at + deep, across : across + wide] = last[i, j]
    wait(tail_all())
    slot_count = emb_all.shape[0]
    whole_emb = jnp.concatenate([emb3[p] for p in range(row_size)], axis=0).astype(jnp.float32)
    emb_all[...] = whole_emb[:slot_count]
    vec = whole_emb[slots_all - vectors.shape[0] :]
    dmodel = vec.shape[1]
    wide = (vectors.shape[0] - 4) * dmodel // row_size
    own_vec, own_up = vec[:4, :shard], vec[4:5, :wide]
    for p in range(1, row_size):
        at = p * wide
        own_vec = jnp.where(row == p, vec[:4, p * shard : (p + 1) * shard], own_vec)
        piece = vec[4 + at // dmodel : 5 + at // dmodel, at % dmodel : at % dmodel + wide]
        own_up = jnp.where(row == p, piece, own_up)
    own_all[...] = jnp.zeros_like(own_all)
    own_all[:4, :shard] = own_vec
    own_all[4:5] = own_up
    rms = jnp.sqrt(sums_all / (sums_all[:1, 4:5] * dmodel))
    own_all[5:6, :LANES] = rms[:1]


def back(counts, halves, queries, keys, values, outs, attn_in, g_in, feat, w_emb, w_mine, gain, bias, own_feat, d_branch,
         vectors, sums, slot_count, ctx_rows, groups, chunk, collective_id):
    row_size, local_rows, slots = feat.shape
    heads, total, _ = keys.shape
    all_rows = queries.shape[1]
    dmodel = w_emb.shape[1]
    width = heads * HEAD_DIM
    x_size = 2
    z_size = row_size // x_size
    shapes = [(2 * h.shape[1], h.shape[2]) for h in halves]
    bf16 = lambda *shape: pltpu.VMEM(shape, jnp.bfloat16)
    f32 = lambda *shape: pltpu.VMEM(shape, jnp.float32)
    plan = plan_streams([h.shape[1:] for h in halves])
    landings = []
    for _, _, rows, cols, order in plan:
        lead, wide, first = 8, cols[1], None
        for axis in order:
            lead, wide = (lead, wide // 2) if axis == "y" else (lead // 2, wide)
            shape = (2,) * (lead.bit_length() - 1) + (rows[1], wide)
            first = first or shape
            landings.append(bf16(*shape))
        landings += [bf16(*first), bf16(2, 2, rows[1], wide)]
    by_head = bf16(heads, all_rows, LANES)
    shard, emb_rows = dmodel // row_size, slots // row_size
    inputs = [by_head, bf16(*keys.shape), bf16(*keys.shape), by_head]
    inputs += [bf16(*a.shape) for a in (attn_in, g_in, feat, w_mine, d_branch)]
    attention = [
        by_head, bf16(heads, all_rows, HEAD_DIM), bf16(HEAD_DIM, all_rows),
        f32(heads, HEAD_DIM, total), f32(heads, HEAD_DIM, total),
        bf16(heads, total, HEAD_DIM), bf16(heads, total, HEAD_DIM),
        bf16(z_size, x_size, local_rows, slots), bf16(z_size, local_rows, slots), bf16(2, local_rows, slots),
        bf16(local_rows, slots),
        f32(slots, dmodel), f32(1, dmodel), f32(1, dmodel),
    ]
    half_emb = (row_size, emb_rows, dmodel // 2)
    tail = [
        bf16(row_size, emb_rows, dmodel), bf16(*half_emb), f32(*sums.shape), f32(*sums.shape),
        bf16(*half_emb), f32(row_size, *sums.shape), bf16(emb_rows, dmodel // 2), f32(*sums.shape),
        bf16(emb_rows, dmodel // 2), f32(*sums.shape), bf16(emb_rows, dmodel // 2), bf16(row_size, emb_rows, dmodel),
    ]
    for each in (heads - 1, 1):
        wide = -(-3 * each * HEAD_DIM // LANES) * LANES
        mine, ours = (row_size, shard // 2, wide), (groups, shard // 2, wide)
        tail += [bf16(row_size, shard, wide), bf16(*mine), bf16(*mine), bf16(*ours), bf16(*ours), bf16(2, *ours)]
    sends = 7 * len(plan) + 18 + 6 * (row_size - 1)
    vmem = pl.BlockSpec(memory_space=pltpu.VMEM)
    anywhere = pl.BlockSpec(memory_space=pl.ANY)
    f32_out = lambda *shape: jax.ShapeDtypeStruct(shape, jnp.float32)
    bf16_out = lambda *shape: jax.ShapeDtypeStruct(shape, jnp.bfloat16)
    return pl.pallas_call(
        functools.partial(back_kernel, (row_size, x_size, chunk, ctx_rows, local_rows, plan)),
        out_shape=[
            bf16_out(slot_count, own_feat.shape[0], ctx_rows),
            bf16_out(own_feat.shape[0], local_rows - ctx_rows, slot_count),
            f32_out(slot_count, dmodel),
            f32_out(8, (vectors.shape[0] - 4) * dmodel // row_size),
            bf16_out(shard, 3 * dmodel),
            bf16_out(*shapes[2]),
            bf16_out(*shapes[0]),
            bf16_out(*shapes[1]),
        ],
        in_specs=[pl.BlockSpec(memory_space=pltpu.SMEM)] + [anywhere] * 12 + [vmem] * 6,
        out_specs=[vmem] * 8,
        scratch_shapes=inputs + attention + tail + landings + [
            pltpu.SemaphoreType.DMA((9 + len(plan),)),
            pltpu.SemaphoreType.DMA((sends,)),
            pltpu.SemaphoreType.DMA((sends,)),
        ],
        compiler_params=pltpu.CompilerParams(
            collective_id=collective_id, has_side_effects=True, vmem_limit_bytes=62 * 2**20
        ),
        name="back",
    )(counts, *halves, queries, keys, values, outs, attn_in, g_in, feat, w_mine, d_branch, w_emb, gain, bias, own_feat,
      vectors, sums)


def finish(own, lengths, kept, widened):
    sources = [*kept, *widened]
    count = len(sources)

    def kernel(own_ref, *refs):
        vectors, refs = refs[count : count + len(lengths)], refs[:count] + refs[count + len(lengths) :]
        ins, outs, held = refs[:count], refs[count : 2 * count], refs[2 * count : 3 * count]
        wide, (in_sem, out_sem) = refs[3 * count : -2], refs[-2:]
        loads = [pltpu.make_async_copy(ins[i], held[i], in_sem.at[i]) for i in range(count)]
        for load in loads:
            load.start()
        for i, size in enumerate(lengths):
            vectors[i][...] = own_ref[i, :size]
        stores = []
        for i, load in enumerate(loads):
            load.wait()
            ready = held[i]
            if i >= len(kept):
                ready = wide[i - len(kept)]
                ready[...] = held[i][...].astype(jnp.float32)
            stores.append(pltpu.make_async_copy(ready, outs[i], out_sem.at[i]))
            stores[-1].start()
        for store in stores:
            store.wait()

    return pl.pallas_call(
        kernel,
        out_shape=[jax.ShapeDtypeStruct((size,), jnp.float32) for size in lengths]
        + [jax.ShapeDtypeStruct(a.shape, a.dtype) for a in kept]
        + [jax.ShapeDtypeStruct(a.shape, jnp.float32) for a in widened],
        in_specs=[pl.BlockSpec(memory_space=pltpu.VMEM)] + [pl.BlockSpec(memory_space=pl.ANY)] * count,
        out_specs=[pl.BlockSpec(memory_space=pltpu.VMEM)] * len(lengths) + [pl.BlockSpec(memory_space=pl.ANY)] * count,
        scratch_shapes=[pltpu.VMEM(a.shape, a.dtype) for a in sources]
        + [pltpu.VMEM(a.shape, jnp.float32) for a in widened]
        + [pltpu.SemaphoreType.DMA((count,))] * 2,
        compiler_params=pltpu.CompilerParams(vmem_limit_bytes=62 * 2**20),
        name="finish",
    )(own, *sources)


def local_by_heads(
    ctx_feat,
    qry_feat,
    feat_count,
    ctx_count,
    qry_count,
    w_emb,
    ln1_gain,
    ln1_bias,
    w_qkv,
    w_out,
    ln2_gain,
    ln2_bias,
    w_up,
    b_up,
    w_down,
    ctx_cot,
    qry_cot,
):
    table_count, slot_count, ctx_rows = ctx_feat.shape
    qry_rows = qry_feat.shape[2]
    local_rows = ctx_rows + qry_rows
    dmodel = w_out.shape[0]
    head_count = dmodel // HEAD_DIM
    row_size = lax.axis_size("row")
    total_ctx = ctx_rows * row_size
    groups = row_size // table_count
    heads = head_count // groups
    packed, back_queries, keys, values, outs, table_feat, w_mine, attn_in, by_row, w_emb_pad = front(
        feat_count,
        ctx_count,
        jnp.transpose(ctx_feat, (1, 0, 2)),
        jnp.transpose(qry_feat, (0, 2, 1)),
        w_emb,
        ln1_gain,
        ln1_bias,
        w_qkv,
        total_ctx,
        heads,
        groups,
        math.gcd(total_ctx, 1024),
        0,
    )
    ctx_out, qry_out, g_in, up_half, down_half, out_half, d_branch, vectors, sums = middle(
        ctx_count,
        qry_count,
        by_row,
        w_emb_pad,
        ln2_gain,
        ln2_bias,
        b_up[None],
        packed,
        w_out,
        w_up,
        w_down,
        ctx_cot,
        qry_cot,
        groups,
        heads,
        math.gcd(w_up.shape[1], 512),
        1,
    )
    ctx_feat_grad, qry_feat_grad, grad_w_emb, own, qkv_all, out_all, up_all, down_all = back(
        feat_count,
        (up_half, down_half, out_half),
        back_queries,
        keys,
        values,
        outs,
        attn_in,
        g_in,
        table_feat,
        w_emb_pad,
        w_mine,
        ln1_gain,
        ln1_bias,
        by_row,
        d_branch,
        vectors,
        sums,
        slot_count,
        ctx_rows,
        groups,
        math.gcd(total_ctx, 512),
        2,
    )
    shard = dmodel // row_size
    (
        gain1_all, bias1_all, gain2_all, bias2_all, upbias_all, rms,
        ctx_out, qry_out, ctx_feat_grad, qry_feat_grad, grad_w_emb, up_all, down_all, qkv_all, out_all,
    ) = finish(
        own, (shard,) * 4 + (w_up.shape[1] // row_size, 4),
        (ctx_out, qry_out, ctx_feat_grad, qry_feat_grad, grad_w_emb), (up_all, down_all, qkv_all, out_all)
    )
    ctx_feat_grad = jnp.transpose(ctx_feat_grad, (1, 0, 2))
    qry_feat_grad = jnp.transpose(qry_feat_grad, (0, 2, 1))
    return (
        ctx_out,
        qry_out,
        ctx_feat_grad,
        qry_feat_grad,
        grad_w_emb,
        gain1_all,
        bias1_all,
        qkv_all,
        out_all,
        gain2_all,
        bias2_all,
        up_all,
        upbias_all,
        down_all,
        rms,
    )


def local(ctx_feat, qry_feat, *rest):
    table_count, slot_count, ctx_rows = ctx_feat.shape
    qry_rows = qry_feat.shape[2]
    head_count = rest[6].shape[0] // HEAD_DIM
    row_size = lax.axis_size("row")
    even = row_size % table_count == 0 and head_count % (row_size // table_count) == 0 and head_count // (row_size // table_count) > 1
    whole = slot_count + 4 + rest[10].shape[1] // rest[6].shape[0] <= LANES and row_size == 8 and table_count == 2 and ctx_rows % LANES == 0 and qry_rows % 32 == 0
    inner = local_by_heads if even and whole else local_by_rows
    return inner(ctx_feat, qry_feat, *rest)


def solution(mesh):
    in_specs = (
        P("tab", None, "row"),
        P("tab", None, "row"),
        P("tab"),
        P("tab"),
        P("tab"),
        P(),
        P(),
        P(),
        P(),
        P(),
        P(),
        P(),
        P(),
        P(),
        P(),
        P("tab", "row", None),
        P("tab", "row", None),
    )
    out_specs = (
        P("tab", "row", None),
        P("tab", "row", None),
        P("tab", None, "row"),
        P("tab", None, "row"),
        P(),
        P("row"),
        P("row"),
        P("row", None),
        P("row", None),
        P("row"),
        P("row"),
        P("row", None),
        P("row"),
        P("row", None),
        P(),
    )
    return jax.shard_map(local, mesh=mesh, in_specs=in_specs, out_specs=out_specs, check_vma=False)
```

```python
import functools
import math

import jax
import jax.numpy as jnp
from jax import lax
from jax.experimental import pallas as pl
from jax.experimental.pallas import tpu as pltpu
from jax.sharding import PartitionSpec as P

HEAD_DIM = 64


EPS = 1e-05
NEGATIVE = -1e30


def standardize(values):
    center = values - jnp.mean(values, axis=-1, keepdims=True)
    inverse = lax.rsqrt(jnp.mean(center * center, axis=-1, keepdims=True) + EPS)
    return (center * inverse, inverse)


def norm_back(grad_out, normed, inverse, gain):
    scaled = grad_out * gain
    inner = (
        scaled
        - jnp.mean(scaled, axis=-1, keepdims=True)
        - normed * jnp.mean(scaled * normed, axis=-1, keepdims=True)
    )
    grad_gain = jnp.sum(grad_out * normed, axis=(0, 1))
    grad_bias = jnp.sum(grad_out, axis=(0, 1))
    return (inverse * inner, grad_gain, grad_bias)


def gelu_exact(values):
    return jax.nn.gelu(values, approximate=False)


def block_scores(query_heads, key_rows, block_index, block_width, key_count, score_scale):
    table_count, local_rows, head_count, head_size = query_heads.shape
    dmodel = head_count * head_size
    block = lax.dynamic_slice_in_dim(key_rows, block_index * block_width, block_width, 1)
    key_block = block[..., :dmodel].reshape(table_count, block_width, head_count, head_size)
    value_block = block[..., dmodel:].reshape(table_count, block_width, head_count, head_size)
    scores = (
        jnp.einsum("trhe,tkhe->thrk", query_heads, key_block, preferred_element_type=jnp.float32)
        * score_scale
    )
    position = block_index * block_width + jnp.arange(block_width)
    live_keys = position[None, :] < key_count[:, None]
    scores = jnp.where(live_keys[:, None, None, :], scores, NEGATIVE)
    return (scores, key_block, value_block)


def local_by_rows(
    ctx_feat,
    qry_feat,
    feat_count,
    ctx_count,
    qry_count,
    w_emb,
    ln1_gain,
    ln1_bias,
    w_qkv,
    w_out,
    ln2_gain,
    ln2_bias,
    w_up,
    b_up,
    w_down,
    ctx_cot,
    qry_cot,
):
    table_count, slot_count, ctx_rows = ctx_feat.shape
    qry_rows = qry_feat.shape[2]
    local_rows = ctx_rows + qry_rows
    dmodel = w_out.shape[0]
    head_count = dmodel // HEAD_DIM
    score_scale = HEAD_DIM ** (-0.5)
    total_ctx = ctx_rows * lax.axis_size("row")
    row_index = lax.axis_index("row")
    slot_live = (jnp.arange(slot_count)[None, :] < feat_count[:, None]).astype(jnp.bfloat16)
    features = jnp.concatenate([ctx_feat, qry_feat], axis=2) * slot_live[:, :, None]
    ctx_live = (row_index * ctx_rows + jnp.arange(ctx_rows))[None, :] < ctx_count[:, None]
    qry_live = (row_index * qry_rows + jnp.arange(qry_rows))[None, :] < qry_count[:, None]
    valid = jnp.concatenate([ctx_live, qry_live], axis=1).astype(jnp.float32)[..., None]
    embed = jnp.einsum("tfr,fd->trd", features, w_emb, preferred_element_type=jnp.float32)
    normed1, inverse1 = standardize(embed)
    attn_in = (normed1 * ln1_gain + ln1_bias).astype(jnp.bfloat16)
    w_query = w_qkv[:, :dmodel]
    w_pair = w_qkv[:, dmodel:]
    query = jnp.einsum("trd,de->tre", attn_in, w_query, preferred_element_type=jnp.float32).astype(
        jnp.bfloat16
    )
    pairs = jnp.einsum(
        "trd,de->tre", attn_in[:, :ctx_rows], w_pair, preferred_element_type=jnp.float32
    ).astype(jnp.bfloat16)
    gathered = lax.all_gather(pairs, "row", axis=1, tiled=True)
    block_width = math.gcd(total_ctx, 512)
    block_total = total_ctx // block_width
    query_heads = query.reshape(table_count, local_rows, head_count, HEAD_DIM)

    def attend_step(carried, block_index):
        running_max, running_sum, summed = carried
        scores, _, value_block = block_scores(
            query_heads, gathered, block_index, block_width, ctx_count, score_scale
        )
        new_max = jnp.maximum(running_max, jnp.max(scores, axis=-1))
        factor = jnp.exp(running_max - new_max)
        weights = jnp.exp(scores - new_max[..., None])
        running_sum = running_sum * factor + jnp.sum(weights, axis=-1)
        summed = summed * jnp.transpose(factor, (0, 2, 1))[..., None] + jnp.einsum(
            "thrk,tkhe->trhe",
            weights.astype(jnp.bfloat16),
            value_block,
            preferred_element_type=jnp.float32,
        )
        return ((new_max, running_sum, summed), None)

    initial = jnp.full((table_count, head_count, local_rows), NEGATIVE, jnp.float32)
    start_sum = jnp.zeros((table_count, local_rows, head_count, HEAD_DIM), jnp.float32)
    (running_max, running_sum, summed), _ = lax.scan(
        attend_step, (initial, jnp.zeros_like(initial), start_sum), jnp.arange(block_total)
    )
    log_total = running_max + jnp.log(running_sum)
    attended = summed / jnp.transpose(running_sum, (0, 2, 1))[..., None]
    attn_low = attended.reshape(table_count, local_rows, dmodel).astype(jnp.bfloat16)
    branch = jnp.einsum("trd,de->tre", attn_low, w_out, preferred_element_type=jnp.float32)
    mixed = embed + branch
    normed2, inverse2 = standardize(mixed)
    mlp_in = (normed2 * ln2_gain + ln2_bias).astype(jnp.bfloat16)
    hidden = jnp.einsum("trd,de->tre", mlp_in, w_up, preferred_element_type=jnp.float32) + b_up
    activation, gelu_back = jax.vjp(gelu_exact, hidden)
    act_low = activation.astype(jnp.bfloat16)
    mlp = jnp.einsum("tre,ed->trd", act_low, w_down, preferred_element_type=jnp.float32)
    output = (mixed + mlp) * valid
    ctx_out = output[:, :ctx_rows].astype(jnp.bfloat16)
    qry_out = output[:, ctx_rows:].astype(jnp.bfloat16)
    squares = jnp.stack(
        [
            jnp.sum(valid * embed * embed),
            jnp.sum(valid * branch * branch),
            jnp.sum(valid * mlp * mlp),
            jnp.sum(valid * output * output),
        ]
    )
    live_rows = jnp.sum(valid)
    cotangent = jnp.concatenate([ctx_cot, qry_cot], axis=1)
    d_mlp = cotangent * valid.astype(jnp.bfloat16)
    grad_w_down = jnp.einsum("tre,trd->ed", act_low, d_mlp, preferred_element_type=jnp.float32)
    d_act = jnp.einsum("trd,ed->tre", d_mlp, w_down, preferred_element_type=jnp.float32)
    d_hidden = gelu_back(d_act)[0].astype(jnp.bfloat16)
    grad_b_up = jnp.sum(d_hidden.astype(jnp.float32), axis=(0, 1))
    grad_w_up = jnp.einsum("trd,tre->de", mlp_in, d_hidden, preferred_element_type=jnp.float32)
    d_mlp_in = jnp.einsum("tre,de->trd", d_hidden, w_up, preferred_element_type=jnp.float32)
    d_norm2, grad_ln2_gain, grad_ln2_bias = norm_back(d_mlp_in, normed2, inverse2, ln2_gain)
    d_mixed = d_mlp.astype(jnp.float32) + d_norm2
    d_branch = d_mixed.astype(jnp.bfloat16)
    grad_w_out = jnp.einsum("trd,tre->de", attn_low, d_branch, preferred_element_type=jnp.float32)
    d_attn = jnp.einsum("tre,de->trd", d_branch, w_out, preferred_element_type=jnp.float32).astype(
        jnp.bfloat16
    )
    d_attn_heads = d_attn.reshape(table_count, local_rows, head_count, HEAD_DIM)
    dots_rows = jnp.sum(d_attn_heads.astype(jnp.float32) * attended, axis=-1)
    row_dots = jnp.transpose(dots_rows, (0, 2, 1))

    def query_part(block_index):
        scores, key_block, value_block = block_scores(
            query_heads, gathered, block_index, block_width, ctx_count, score_scale
        )
        softened = jnp.exp(scores - log_total[..., None])
        d_soft = jnp.einsum(
            "trhe,tkhe->thrk", d_attn_heads, value_block, preferred_element_type=jnp.float32
        )
        d_scores = (softened * (d_soft - row_dots[..., None])).astype(jnp.bfloat16)
        d_part = (
            jnp.einsum("thrk,tkhe->trhe", d_scores, key_block, preferred_element_type=jnp.float32)
            * score_scale
        )
        return (softened, d_scores, d_part)

    start_query = jnp.zeros((table_count, local_rows, head_count, HEAD_DIM), jnp.float32)

    def grad_step(carried, block_index):
        d_query, d_pairs = carried
        softened, d_scores, d_part = query_part(block_index)
        d_values = jnp.einsum(
            "thrk,trhe->tkhe",
            softened.astype(jnp.bfloat16),
            d_attn_heads,
            preferred_element_type=jnp.float32,
        )
        d_keys = (
            jnp.einsum("thrk,trhe->tkhe", d_scores, query_heads, preferred_element_type=jnp.float32)
            * score_scale
        )
        grad_block = jnp.concatenate(
            [
                d_keys.reshape(table_count, block_width, dmodel),
                d_values.reshape(table_count, block_width, dmodel),
            ],
            axis=-1,
        )
        d_pairs = lax.dynamic_update_slice_in_dim(d_pairs, grad_block, block_index * block_width, 1)
        return ((d_query + d_part, d_pairs), None)

    start_pairs = jnp.zeros((table_count, total_ctx, 2 * dmodel), jnp.float32)
    (d_query, d_pairs), _ = lax.scan(grad_step, (start_query, start_pairs), jnp.arange(block_total))
    own_pairs = lax.psum_scatter(d_pairs, "row", scatter_dimension=1, tiled=True).astype(
        jnp.bfloat16
    )
    d_q = d_query.reshape(table_count, local_rows, dmodel).astype(jnp.bfloat16)
    grad_w_qkv = jnp.concatenate(
        [
            jnp.einsum("trd,tre->de", attn_in, d_q, preferred_element_type=jnp.float32),
            jnp.einsum(
                "trd,tre->de", attn_in[:, :ctx_rows], own_pairs, preferred_element_type=jnp.float32
            ),
        ],
        axis=1,
    )
    d_from_query = jnp.einsum("tre,de->trd", d_q, w_query, preferred_element_type=jnp.float32)
    d_from_pairs = jnp.einsum("tre,de->trd", own_pairs, w_pair, preferred_element_type=jnp.float32)
    d_attn_in = jnp.concatenate(
        [d_from_query[:, :ctx_rows] + d_from_pairs, d_from_query[:, ctx_rows:]], axis=1
    )
    d_norm1, grad_ln1_gain, grad_ln1_bias = norm_back(d_attn_in, normed1, inverse1, ln1_gain)
    d_embed = (d_mixed + d_norm1).astype(jnp.bfloat16)
    grad_w_emb = jnp.einsum("tfr,trd->fd", features, d_embed, preferred_element_type=jnp.float32)
    d_features = jnp.einsum("trd,fd->tfr", d_embed, w_emb, preferred_element_type=jnp.float32)
    d_features = (d_features * slot_live[:, :, None].astype(jnp.float32)).astype(jnp.bfloat16)
    ctx_feat_grad = d_features[:, :, :ctx_rows]
    qry_feat_grad = d_features[:, :, ctx_rows:]
    (
        qkv_part,
        out_part,
        up_part,
        down_part,
        gain1_part,
        bias1_part,
        gain2_part,
        bias2_part,
        upbias_part,
    ) = (
        lax.psum_scatter(grad_w_qkv, "row", scatter_dimension=0, tiled=True),
        lax.psum_scatter(grad_w_out, "row", scatter_dimension=0, tiled=True),
        lax.psum_scatter(grad_w_up, "row", scatter_dimension=0, tiled=True),
        lax.psum_scatter(grad_w_down, "row", scatter_dimension=0, tiled=True),
        lax.psum_scatter(grad_ln1_gain, "row", scatter_dimension=0, tiled=True),
        lax.psum_scatter(grad_ln1_bias, "row", scatter_dimension=0, tiled=True),
        lax.psum_scatter(grad_ln2_gain, "row", scatter_dimension=0, tiled=True),
        lax.psum_scatter(grad_ln2_bias, "row", scatter_dimension=0, tiled=True),
        lax.psum_scatter(grad_b_up, "row", scatter_dimension=0, tiled=True),
    )
    qkv_all, out_all, up_all, down_all, gain1_all, bias1_all, gain2_all, bias2_all, upbias_all = (
        lax.psum(qkv_part.astype(jnp.bfloat16), "tab").astype(jnp.float32),
        lax.psum(out_part.astype(jnp.bfloat16), "tab").astype(jnp.float32),
        lax.psum(up_part.astype(jnp.bfloat16), "tab").astype(jnp.float32),
        lax.psum(down_part.astype(jnp.bfloat16), "tab").astype(jnp.float32),
        lax.psum(gain1_part.astype(jnp.bfloat16), "tab").astype(jnp.float32),
        lax.psum(bias1_part.astype(jnp.bfloat16), "tab").astype(jnp.float32),
        lax.psum(gain2_part.astype(jnp.bfloat16), "tab").astype(jnp.float32),
        lax.psum(bias2_part.astype(jnp.bfloat16), "tab").astype(jnp.float32),
        lax.psum(upbias_part.astype(jnp.bfloat16), "tab").astype(jnp.float32),
    )
    embed_all, squares_all, count_all = lax.psum((grad_w_emb, squares, live_rows), ("tab", "row"))
    rms = jnp.sqrt(squares_all / (count_all * dmodel))
    return (
        ctx_out,
        qry_out,
        ctx_feat_grad,
        qry_feat_grad,
        embed_all,
        gain1_all,
        bias1_all,
        qkv_all,
        out_all,
        gain2_all,
        bias2_all,
        up_all,
        upbias_all,
        down_all,
        rms,
    )


MESH = pl.DeviceIdType.MESH
LANES = 128
NT = (((1,), (1,)), ((), ()))


def lane_of(shape):
    return lax.broadcasted_iota(jnp.int32, shape, len(shape) - 1)


def split_three(values):
    high = values.astype(jnp.bfloat16)
    rest = values - high.astype(jnp.float32)
    mid = rest.astype(jnp.bfloat16)
    tail = (rest - mid.astype(jnp.float32)).astype(jnp.bfloat16)
    return (high, mid, tail)


def set_lanes(values, first, columns):
    lane = lane_of(values.shape)
    values = values.astype(jnp.float32)
    for i, column in enumerate(columns):
        values = jnp.where(lane == first + i, column.astype(jnp.float32), values)
    return values.astype(jnp.bfloat16)


def greet(peers):
    barrier = pltpu.get_barrier_semaphore()
    for peer in peers:
        pl.semaphore_signal(barrier, inc=1, device_id=peer, device_id_type=MESH)
    pl.semaphore_wait(barrier, len(peers))


def front_kernel(
    dims, feat_counts, counts, ctx_feat, qry_feat, w_emb_in, gain_in, bias_in, w_qkv,
    out_in, queries_out, keys_out, values_out, outs_out, feat_out, w_out, attn_out, own_feat, w_emb,
    by_slot, attn_all, feat_in, window, w_lanes, w_mine, queries, keys, values, outs, packed, load_sem, store_sem, send_sem, recv_sem,
):
    row_size, x_size, chunk, ctx_rows, local_rows, heads, groups = dims
    z_size = row_size // x_size
    total = keys.shape[1]
    pair = x_size * local_rows
    dmodel = w_emb.shape[1]
    width = heads * HEAD_DIM
    tab, row = lax.axis_index("tab"), lax.axis_index("row")
    z = row // x_size
    table, group = row // groups, lax.rem(row, groups)
    tables = own_feat.shape[0]
    row_peers = [(tab, lax.rem(row + k, row_size)) for k in range(1, row_size)]
    numbers = {}

    def remote(name, src, dst, peer):
        i = numbers.setdefault(name, len(numbers))
        return pltpu.make_async_remote_copy(
            src_ref=src, dst_ref=dst, send_sem=send_sem.at[i], recv_sem=recv_sem.at[i],
            device_id=peer, device_id_type=MESH,
        )

    def feat_copy(dt, dg):
        t, g = lax.rem(table + dt, tables), lax.rem(group + dg, groups)
        if dt == 0:
            return remote(("near", dg), own_feat.at[table], feat_in.at[row], (tab, table * groups + g))
        if dg == 0:
            return remote(("far", dt), own_feat.at[t], feat_in.at[row], (tab, t * groups + group))
        came = t * groups + group
        return remote(("passed", dt, dg), feat_in.at[came], feat_in.at[came], (tab, table * groups + g))

    def out_copy(shift):
        p = lax.rem(row + shift, row_size)
        return remote(("out", shift), packed.at[p], out_in.at[row], (tab, p))

    span = window.shape[2]
    first = (group * width) // LANES * LANES

    def window_copy(n):
        at = pl.ds(pl.multiple_of(n * dmodel + first, LANES), span)
        return pltpu.make_async_copy(w_qkv.at[:, at], window.at[n], load_sem.at[n])

    for n in range(3):
        window_copy(n).start()
    by_slot[...] = jnp.zeros_like(by_slot)
    slots = ctx_feat.shape[0]
    slot = lax.broadcasted_iota(jnp.int32, (slots, 1), 0)
    for t in range(tables):
        live = jnp.where(slot < feat_counts[t], 1.0, 0.0)
        by_slot[:slots, :ctx_rows] = ctx_feat[:, t].astype(jnp.float32) * live
        wide = by_slot[...].T
        own_feat[t, :ctx_rows] = wide[:ctx_rows].astype(jnp.bfloat16)
        lane = lax.broadcasted_iota(jnp.int32, qry_feat.shape[1:], 1)
        narrow = jnp.where(lane < feat_counts[t], qry_feat[t].astype(jnp.float32), 0.0)
        nothing = jnp.zeros((narrow.shape[0], LANES - slots), jnp.float32)
        own_feat[t, ctx_rows:] = jnp.concatenate([narrow, nothing], axis=1).astype(jnp.bfloat16)
    w_emb[...] = jnp.zeros_like(w_emb)
    w_emb[:slots] = w_emb_in[...]
    gain, bias = gain_in[...][None], bias_in[...][None]
    greet(row_peers)
    for dt in range(1, tables):
        feat_copy(dt, 0).start()
    for dg in range(1, groups):
        feat_copy(0, dg).start()
    feat_in[row] = own_feat[table]
    offset = group * width - first
    for n in range(3):
        window_copy(n).wait()
        wide = window[n]
        mine = wide[:, :width]
        for shift in range(HEAD_DIM, span - width + 1, HEAD_DIM):
            mine = jnp.where(offset == shift, wide[:, shift : shift + width], mine)
        w_mine[:, n * width : (n + 1) * width] = mine
        for h in range(heads):
            one = mine[:, h * HEAD_DIM : (h + 1) * HEAD_DIM]
            at = (n * heads + h) * LANES
            w_lanes[:, at : at + LANES] = jnp.concatenate([one, jnp.zeros_like(one)], axis=1)
    w_store = pltpu.make_async_copy(w_mine, w_out, store_sem.at[0])
    w_store.start()
    count = counts[table]

    near = groups // x_size

    def project(step, _):
        @pl.when(step == 1)
        def _():
            for dt in range(1, tables):
                feat_copy(tables - dt, 0).wait_recv()
                for dg in range(1, groups):
                    feat_copy(dt, dg).start()

        there = lax.rem(z // near + step // near, tables) * near + lax.rem(z + step, near)
        embeds = []
        for other in range(x_size):
            p = there * x_size + other
            ahead = lax.rem(p // groups - table + tables, tables)
            across = lax.rem(group - lax.rem(p, groups) + groups, groups)
            for dt in range(tables):
                for dg in range(1, groups):

                    @pl.when((ahead == dt) & (across == dg))
                    def _():
                        feat_copy(dt, dg).wait_recv()

            embeds.append(feat_in[p])
        rows_feat = jnp.concatenate(embeds, axis=0)
        embed = jnp.dot(rows_feat, w_emb[...], preferred_element_type=jnp.float32)
        center = embed - jnp.mean(embed, axis=-1, keepdims=True)
        inverse = lax.rsqrt(jnp.mean(center * center, axis=-1, keepdims=True) + EPS)
        attn_in = (center * inverse * gain + bias).astype(jnp.bfloat16)
        projected = jnp.dot(attn_in, w_lanes[...], preferred_element_type=jnp.float32)
        rows = pl.ds(pl.multiple_of(there * pair, LANES), pair)
        attn_all[rows] = attn_in
        lane = lane_of((pair, LANES))
        for h in range(heads):
            query = projected[:, h * LANES : (h + 1) * LANES] * HEAD_DIM ** (-0.5)
            queries[h, rows] = jnp.where(lane == HEAD_DIM, 1.0, query).astype(jnp.bfloat16)
        lane = lane_of((ctx_rows, LANES))
        for other in range(x_size):
            p = there * x_size + other
            key_rows = pl.ds(pl.multiple_of(p * ctx_rows, LANES), ctx_rows)
            position = p * ctx_rows + lax.broadcasted_iota(jnp.int32, (ctx_rows, LANES), 0)
            mask = jnp.where(position < count, 0.0, NEGATIVE)
            for h in range(heads):
                at = (heads + h) * LANES
                key = projected[other * local_rows : other * local_rows + ctx_rows, at : at + LANES]
                key = jnp.where(lane == HEAD_DIM, mask, key)
                key = jnp.where((lane > HEAD_DIM) & (lane < HEAD_DIM + 4), 1.0, key)
                keys[h, key_rows] = key.astype(jnp.bfloat16)
                at = (2 * heads + h) * LANES
                value = projected[other * local_rows : other * local_rows + ctx_rows, at : at + LANES]
                value = jnp.where((lane >= HEAD_DIM) & (lane < HEAD_DIM + 3), 1.0, value)
                values[h, key_rows] = value.astype(jnp.bfloat16)
        return 0

    lax.fori_loop(0, z_size, project, 0)
    stores = [
        pltpu.make_async_copy(src, dst, store_sem.at[i + 1])
        for i, (src, dst) in enumerate(
            ((keys, keys_out), (values, values_out), (feat_in, feat_out), (attn_all, attn_out))
        )
    ]
    for store in stores:
        store.start()
    whole = heads // 2

    def segment(step, _):
        k, h = step // heads, lax.rem(step, heads)
        there = lax.rem(z + k + 1, z_size)
        rows = pl.ds(pl.multiple_of(there * pair, LANES), pair)
        query = queries[h, rows]
        for i in range(total // chunk):
            at = pl.ds(i * chunk, chunk)
            scores = lax.dot_general(query, keys[h, at], NT, preferred_element_type=jnp.float32)
            top = jnp.max(scores, axis=-1, keepdims=True)
            if i:
                top = jnp.maximum(top, before)
            weights = jnp.exp(scores - top).astype(jnp.bfloat16)
            term = jnp.dot(weights, values[h, at], preferred_element_type=jnp.float32)
            summed = summed * jnp.exp(before - top) + term if i else term
            before = top
        sum_all = summed[:, HEAD_DIM : HEAD_DIM + 1]
        outs[h, rows] = (summed / sum_all).astype(jnp.bfloat16)
        queries[h, rows] = set_lanes(query, HEAD_DIM + 1, split_three(-(top + jnp.log(sum_all))))

        @pl.when(h == heads - 1)
        def _():
            for other in range(x_size):
                p = there * x_size + other
                at = pl.ds(pl.multiple_of(p * local_rows, 16), local_rows)
                parts = [outs[i, at, :HEAD_DIM] for i in range(heads)]
                for i in range(whole):
                    both = jnp.concatenate([parts[2 * i], parts[2 * i + 1]], axis=1)
                    packed[p, i * local_rows : (i + 1) * local_rows] = both
                if heads % 2:
                    last = parts[-1]
                    both = jnp.concatenate([last[: local_rows // 2], last[local_rows // 2 :]], axis=1)
                    packed[p, whole * local_rows :] = both
                ahead = lax.rem(p - row + row_size, row_size)
                for s in range(1, row_size):

                    @pl.when(ahead == s)
                    def _():
                        out_copy(s).start()

        return 0

    lax.fori_loop(0, z_size * heads, segment, 0)
    last = [
        pltpu.make_async_copy(queries, queries_out, store_sem.at[5]),
        pltpu.make_async_copy(outs, outs_out, store_sem.at[6]),
        pltpu.make_async_copy(packed.at[row], out_in.at[row], store_sem.at[7]),
    ]
    for store in last:
        store.start()
    for dt in range(tables):
        for dg in range(groups):
            if dt + dg:
                feat_copy(dt, dg).wait_send()
    for store in [w_store] + stores + last:
        store.wait()
    for s in range(1, row_size):
        out_copy(s).wait()


def front(feat_counts, counts, ctx_feat, qry_feat, w_emb, gain, bias, w_qkv, total_ctx, heads, groups, chunk, collective_id):
    row_size = lax.axis_size("row")
    tables, qry_rows, _ = qry_feat.shape
    dmodel = w_emb.shape[1]
    ctx_rows = total_ctx // row_size
    local_rows, slots = ctx_rows + qry_rows, LANES
    width = heads * HEAD_DIM
    x_size = 2
    span = -(-(width + (HEAD_DIM if width % LANES else 0)) // LANES) * LANES
    bf16 = lambda *shape: (shape, jnp.bfloat16)
    by_query, by_key = (heads, row_size * local_rows, LANES), (heads, total_ctx, LANES)
    block = (row_size, -(-heads * local_rows // 2), LANES)
    feat = (row_size, local_rows, slots)
    vmem = pl.BlockSpec(memory_space=pltpu.VMEM)
    anywhere = pl.BlockSpec(memory_space=pl.ANY)
    scratch = [
        feat, (3, dmodel, span), (dmodel, 3 * heads * LANES), (dmodel, 3 * width),
        by_query, by_key, by_key, by_query, block,
    ]
    return pl.pallas_call(
        functools.partial(front_kernel, (row_size, x_size, chunk, ctx_rows, local_rows, heads, groups)),
        out_shape=[
            jax.ShapeDtypeStruct(s, jnp.bfloat16)
            for s in (
                block, by_query, by_key, by_key, by_query, feat, (dmodel, 3 * width),
                (row_size * local_rows, dmodel),
                (tables, local_rows, slots), (slots, dmodel),
            )
        ],
        in_specs=[pl.BlockSpec(memory_space=pltpu.SMEM)] * 2 + [vmem] * 5 + [anywhere],
        out_specs=[anywhere] * 8 + [vmem] * 2,
        scratch_shapes=[
            pltpu.VMEM((slots, ctx_rows), jnp.float32),
            pltpu.VMEM((row_size * local_rows, dmodel), jnp.bfloat16),
        ] + [pltpu.VMEM(s, jnp.bfloat16) for s in scratch] + [
            pltpu.SemaphoreType.DMA((3,)),
            pltpu.SemaphoreType.DMA((8,)),
            pltpu.SemaphoreType.DMA((2 * (row_size - 1),)),
            pltpu.SemaphoreType.DMA((2 * (row_size - 1),)),
        ],
        compiler_params=pltpu.CompilerParams(
            collective_id=collective_id, has_side_effects=True, vmem_limit_bytes=60 * 2**20
        ),
        name="front",
    )(feat_counts, counts, ctx_feat, qry_feat, w_emb, gain, bias, w_qkv)


def gelu_parts(values):
    below = 0.5 + 0.5 * lax.erf(values * math.sqrt(0.5))
    return (below, values * jnp.exp(-0.5 * values * values) * (1.0 / math.sqrt(2.0 * math.pi)))


def middle_kernel(
    dims, ctx_count, qry_count, own_feat, w_emb, gain_in, bias_in, b_up, out_in, w_out_hbm, w_up_hbm, w_down_hbm, ctx_cot, qry_cot,
    ctx_out, qry_out, g_in, up_half, down_half, out_half, d_branch_out, vectors, sums,
    w_out, w_up, w_down, attn_in, cot, attn_low, mlp_in, mlp_in_t, mixed, normed, inverses, d_mlp_in, act, d_hidden, d_up_bias,
    packed, up, down, out, up_in0, down_in0, out_in0, load_sem, store_sem, send_sem, recv_sem,
):
    row_size, ctx_rows, local_rows, tables, groups, heads, tile = dims
    rows = tables * local_rows
    qry_rows = local_rows - ctx_rows
    dmodel, hidden_size = w_up.shape
    tiles = hidden_size // tile
    tab, row = lax.axis_index("tab"), lax.axis_index("row")
    core = lax.rem(tab, 2)
    core_peer = (tab ^ 1, row)
    row_peers = [(tab, lax.rem(row + k, row_size)) for k in range(1, row_size)]
    numbers = {}

    def remote(name, src, dst, peer):
        i = numbers.setdefault(name, len(numbers))
        return pltpu.make_async_remote_copy(
            src_ref=src, dst_ref=dst, send_sem=send_sem.at[i], recv_sem=recv_sem.at[i],
            device_id=peer, device_id_type=MESH,
        )

    gain, bias = gain_in[...][None], bias_in[...][None]
    loads = [
        pltpu.make_async_copy(src, dst, load_sem.at[i])
        for i, (src, dst) in enumerate(
            [(out_in, attn_in), (w_out_hbm, w_out), (w_up_hbm, w_up), (w_down_hbm, w_down)]
            + [(ctx_cot.at[t], cot.at[pl.ds(t * local_rows, ctx_rows)]) for t in range(tables)]
            + [(qry_cot.at[t], cot.at[pl.ds(t * local_rows + ctx_rows, qry_rows)]) for t in range(tables)]
        )
    ]
    for load in loads:
        load.start()
    greet([core_peer] + row_peers)

    at = lax.broadcasted_iota(jnp.int32, (local_rows, 1), 0)
    live = []
    for t in range(tables):
        place = jnp.where(at < ctx_rows, row * ctx_rows + at, row * qry_rows + at - ctx_rows)
        limit = jnp.where(at < ctx_rows, ctx_count[t], qry_count[t])
        live.append(jnp.where(place < limit, 1.0, 0.0))
    valid = jnp.concatenate(live, axis=0)
    own_rows = jnp.concatenate([own_feat[t] for t in range(tables)], axis=0)
    embed = jnp.dot(own_rows, w_emb[...], preferred_element_type=jnp.float32)

    whole = heads // 2
    loads[0].wait()
    for t in range(tables):
        parts = []
        for g in range(groups):
            block = attn_in[t * groups + g]
            for h in range(whole):
                parts.append(block[h * local_rows : (h + 1) * local_rows])
            if heads % 2:
                last = block[whole * local_rows :]
                parts.append(jnp.concatenate([last[:, :HEAD_DIM], last[:, HEAD_DIM:]], axis=0))
        attn_low[t * local_rows : (t + 1) * local_rows] = jnp.concatenate(parts, axis=1)
    loads[1].wait()
    branch = jnp.dot(attn_low[...], w_out[...], preferred_element_type=jnp.float32)
    summed = embed + branch
    mixed[...] = summed
    square_embed = jnp.sum(valid * embed * embed)
    square_branch = jnp.sum(valid * branch * branch)
    center = summed - jnp.mean(summed, axis=-1, keepdims=True)
    inverse = lax.rsqrt(jnp.mean(center * center, axis=-1, keepdims=True) + EPS)
    normed[...] = center * inverse
    inverses[...] = inverse
    mlp_in[...] = (normed[...] * gain + bias).astype(jnp.bfloat16)
    for load in loads[2:]:
        load.wait()
    cot[...] = (cot[...].astype(jnp.float32) * valid).astype(jnp.bfloat16)
    d_mlp_in[...] = jnp.zeros_like(d_mlp_in)

    def columns(i):
        return pl.ds(pl.multiple_of(i * tile, LANES), tile)

    d_up_bias[...] = jnp.zeros_like(d_up_bias)
    vectors[...] = jnp.zeros_like(vectors)
    width = heads * HEAD_DIM
    far_bit, group = row // groups, lax.rem(row, groups)
    g_copies = []
    for turn in range(tables):
        t = lax.rem(far_bit + 1 + turn, tables)
        mine = pl.ds(pl.multiple_of(t * local_rows, 16), local_rows)

        def first(i, _):
            at = columns(i)
            hidden = jnp.dot(mlp_in[mine], w_up[:, at], preferred_element_type=jnp.float32) + b_up[:, at]
            d_act = lax.dot_general(cot[mine], w_down[at], NT, preferred_element_type=jnp.float32)
            below, slope = gelu_parts(hidden)
            act[mine, at] = (hidden * below).astype(jnp.bfloat16)
            grad = (d_act * (below + slope)).astype(jnp.bfloat16)
            d_hidden[mine, at] = grad
            d_up_bias[:, at] += jnp.sum(grad.astype(jnp.float32), axis=0, keepdims=True)
            d_mlp_in[mine] += lax.dot_general(grad, w_up[:, at], NT, preferred_element_type=jnp.float32)
            return 0

        lax.fori_loop(0, tiles, first, 0)
        grad_in, norm = d_mlp_in[mine], normed[mine]
        scaled = grad_in * gain
        inner = (
            scaled
            - jnp.mean(scaled, axis=-1, keepdims=True)
            - norm * jnp.mean(scaled * norm, axis=-1, keepdims=True)
        )
        vectors[2:3] += jnp.sum(grad_in * norm, axis=0, keepdims=True)
        vectors[3:4] += jnp.sum(grad_in, axis=0, keepdims=True)
        d_branch = (cot[mine].astype(jnp.float32) + inverses[mine] * inner).astype(jnp.bfloat16)
        d_branch_out[t] = d_branch
        d_attn = lax.dot_general(d_branch, w_out[...], NT, preferred_element_type=jnp.float32).astype(jnp.bfloat16)
        for g in range(groups):
            block = d_attn[:, g * width : (g + 1) * width]
            p = t * groups + g
            for h in range(whole):
                packed[p, h * local_rows : (h + 1) * local_rows] = block[:, h * LANES : (h + 1) * LANES]
            if heads % 2:
                last = block[:, whole * LANES :]
                both = jnp.concatenate([last[: local_rows // 2], last[local_rows // 2 :]], axis=1)
                packed[p, whole * local_rows :] = both
        for k in range(groups):
            p = t * groups + lax.rem(group + k, groups)
            if turn == tables - 1 and k == 0:
                own_g = pltpu.make_async_copy(packed.at[row], g_in.at[row], store_sem.at[0])
                own_g.start()
            else:
                g_copies.append(remote(("g", turn, k), packed.at[p], g_in.at[row], (tab, p)))
                g_copies[-1].start()
    for i in range(hidden_size // dmodel):
        vectors[4 + i : 5 + i] = d_up_bias[:, i * dmodel : (i + 1) * dmodel]
    d_branch = jnp.concatenate([d_branch_out[t] for t in range(tables)], axis=0)

    def half(ref, which):
        size = ref.shape[1] // 2
        return pl.ds(pl.multiple_of(which * size, 16), size)

    shard = dmodel // row_size
    d_out = jnp.dot(attn_low[...].T, d_branch, preferred_element_type=jnp.float32).astype(jnp.bfloat16)
    for p in range(row_size):
        out[p] = d_out[p * shard : (p + 1) * shard]
    out_copy = remote("out", out.at[:, half(out, 1 - core)], out_in0, core_peer)
    out_copy.start()
    mlp_in_t[...] = mlp_in[...].T
    d_mlp_in[...] = jnp.zeros_like(d_mlp_in)
    per = hidden_size // row_size

    steps = row_size // 2

    def span_of(p):
        return pl.ds(pl.multiple_of(p * 2 * per, LANES), 2 * per)

    def owners(p):
        return pl.ds(2 * p, 2)

    def pieces(p):
        at = span_of(p)
        return [
            pltpu.make_async_remote_copy(
                src_ref=src, dst_ref=dst, send_sem=send_sem.at[first + p], recv_sem=recv_sem.at[first + p],
                device_id=core_peer, device_id_type=MESH,
            )
            for src, dst, first in (
                (down.at[owners(p), half(down, 1 - core)], down_in0.at[owners(p)], row_size),
                (up.at[:, half(up, 1 - core), at], up_in0.at[:, :, at], 2 * row_size),
            )
        ]

    def stored(p):
        at = span_of(p)
        return [
            pltpu.make_async_copy(down_in0.at[owners(p)], down_half.at[owners(p)], store_sem.at[2 + p]),
            pltpu.make_async_copy(up_in0.at[:, :, at], up_half.at[:, :, at], store_sem.at[2 + row_size + p]),
        ]

    def add_piece(p):
        at = span_of(p)
        for copy in pieces(p):
            copy.wait()
        for q in range(2):
            down_in0[2 * p + q] = down_in0[2 * p + q] + down[2 * p + q, half(down, core)]
        for q in range(row_size):
            up_in0[q, :, at] = up_in0[q, :, at] + up[q, half(up, core), at]
        for store in stored(p):
            store.start()

    def second(p, _):
        at = span_of(p)
        piece = act[:, at]
        d_down = jnp.dot(piece.T, cot[...], preferred_element_type=jnp.float32).astype(jnp.bfloat16)
        for q in range(2):
            down[2 * p + q] = d_down[q * per : (q + 1) * per]
        d_up = jnp.dot(mlp_in_t[...], d_hidden[:, at], preferred_element_type=jnp.float32).astype(jnp.bfloat16)
        for q in range(row_size):
            up[q, :, at] = d_up[q * shard : (q + 1) * shard]
        for copy in pieces(p):
            copy.start()
        d_mlp_in[...] += jnp.dot(piece, w_down[at], preferred_element_type=jnp.float32)

        @pl.when(p > 0)
        def _():
            add_piece(p - 1)

        return 0

    lax.fori_loop(0, steps, second, 0)
    add_piece(steps - 1)
    out_copy.wait()

    @pl.loop(0, row_size)
    def _(p):
        out_in0[p] = out_in0[p] + out[p, half(out, core)]

    out_store = pltpu.make_async_copy(out_in0, out_half, store_sem.at[1])
    out_store.start()
    mlp = d_mlp_in[...]
    result = (mixed[...] + mlp) * valid
    square_mlp = jnp.sum(valid * mlp * mlp)
    square_result = jnp.sum(result * result)
    low = result.astype(jnp.bfloat16)
    for t in range(tables):
        ctx_out[t] = low[t * local_rows : t * local_rows + ctx_rows]
        qry_out[t] = low[t * local_rows + ctx_rows : (t + 1) * local_rows]
    lane = lane_of(sums.shape)
    parts = (square_embed, square_branch, square_mlp, square_result, jnp.sum(valid))
    total = jnp.zeros(sums.shape, jnp.float32)
    for i, part in enumerate(parts):
        total = jnp.where(lane == i, part, total)
    sums[...] = total
    for p in range(steps):
        for store in stored(p):
            store.wait()
    out_store.wait()
    own_g.wait()
    for copy in g_copies:
        copy.wait()


def middle(ctx_count, qry_count, own_feat, w_emb, gain, bias, b_up, out_in, w_out, w_up, w_down, ctx_cot, qry_cot,
           groups, heads, tile, collective_id):
    row_size = lax.axis_size("row")
    tables, local_rows, _ = own_feat.shape
    ctx_rows = ctx_cot.shape[1]
    rows = tables * local_rows
    dmodel, hidden_size = w_up.shape
    shard, per = dmodel // row_size, hidden_size // row_size
    halves = [(row_size, shard // 2, hidden_size), (row_size, per // 2, dmodel), (row_size, shard // 2, dmodel)]
    vmem = pl.BlockSpec(memory_space=pltpu.VMEM)
    smem = pl.BlockSpec(memory_space=pltpu.SMEM)
    anywhere = pl.BlockSpec(memory_space=pl.ANY)
    bf16 = lambda *shape: pltpu.VMEM(shape, jnp.bfloat16)
    f32 = lambda *shape: pltpu.VMEM(shape, jnp.float32)
    sends = 3 * row_size
    return pl.pallas_call(
        functools.partial(middle_kernel, (row_size, ctx_rows, local_rows, tables, groups, heads, tile)),
        out_shape=[jax.ShapeDtypeStruct(s, jnp.bfloat16) for s in (ctx_cot.shape, qry_cot.shape, out_in.shape, *halves)]
        + [jax.ShapeDtypeStruct((tables, local_rows, dmodel), jnp.bfloat16)]
        + [jax.ShapeDtypeStruct((4 + hidden_size // dmodel, dmodel), jnp.float32)]
        + [jax.ShapeDtypeStruct((8, LANES), jnp.float32)],
        in_specs=[smem] * 2 + [vmem] * 5 + [anywhere] * 6,
        out_specs=[vmem] * 2 + [anywhere] * 4 + [vmem] * 3,
        scratch_shapes=[
            bf16(*w_out.shape), bf16(*w_up.shape), bf16(*w_down.shape), bf16(*out_in.shape), bf16(rows, dmodel),
            bf16(rows, dmodel), bf16(rows, dmodel), bf16(dmodel, rows),
            f32(rows, dmodel), f32(rows, dmodel), f32(rows, 1), f32(rows, dmodel),
            bf16(rows, hidden_size), bf16(rows, hidden_size), f32(1, hidden_size),
            bf16(*out_in.shape),
            bf16(row_size, shard, hidden_size), bf16(row_size, per, dmodel), bf16(row_size, shard, dmodel),
            *[bf16(*s) for s in halves],
            pltpu.SemaphoreType.DMA((4 + 2 * tables,)),
            pltpu.SemaphoreType.DMA((2 + 2 * row_size,)),
            pltpu.SemaphoreType.DMA((sends,)),
            pltpu.SemaphoreType.DMA((sends,)),
        ],
        compiler_params=pltpu.CompilerParams(
            collective_id=collective_id, has_side_effects=True, vmem_limit_bytes=62 * 2**20
        ),
        name="middle",
    )(ctx_count, qry_count, own_feat, w_emb, gain, bias, b_up, out_in, w_out, w_up, w_down, ctx_cot, qry_cot)


def tile_sum(parts):
    total = parts[0]
    for part in parts[1:]:
        total = total + part
    return total


ROW_AXES = ("x", "near", "far")
ATTEND_STEPS = ((5, 1, 0), (5, 2, 0), (5, 3, 0), (5, 0, 0), (5, 4, 0), (7, 1, 1), (7, 2, 1), (7, 3, 1), (8, 0, 1), (8, 4, 1), (9, 1, 2), (9, 2, 2), (9, 3, 2), (10, 0, 2), (10, 4, 2))
CHAIN_STEPS = ((9, 0, 1), (11, 0, 2))
LAST_STEPS = ((0, 0, 3), (0, 1, 1))
GATHER_STEP = 0


def plan_streams(shapes):
    (up_rows, up_wide), (down_rows, down_wide), (out_rows, out_wide) = shapes
    cut = up_wide * 7 // 12 // (2 * LANES) * 2 * LANES
    deep = down_rows * 2 // 3 // 16 * 16
    return (
        ("up_y", "up", (0, up_rows), (0, cut), ("y", "x", "near", "far")),
        ("down_x", "down", (0, deep), (0, down_wide), ("x", "near", "y", "far")),
        ("up_z", "up", (0, up_rows), (cut, up_wide - cut), ("near", "y", "x", "far")),
        ("down_z", "down", (deep, down_rows - deep), (0, down_wide), ("near", "y", "x", "far")),
        ("out_y", "out", (0, out_rows), (0, out_wide), ("y", "x", "near", "far")),
    )


def back_kernel(
    dims, counts, up0, down0, out0, queries_hbm, keys_hbm, values_hbm, outs_hbm, attn_hbm, g_hbm, feat_hbm, w_mine_hbm, branch_hbm,
    w_emb, gain_in, bias_in, own_feat, vectors, sums,
    ctx_grad, qry_grad, emb_all, own_all, qkv_all, out_all, up_all, down_all,
    queries, keys, values, outs, attn_in, g_in, feat, w_mine, d_branch, grads, d_q, d_qt, d_kt, d_vt, d_k, d_v, terms, terms_x, terms_z, terms_far, d_emb, d_gain, d_bias,
    emb_own, emb_in0, sums_in0, sums0, emb_in1, sums_in1, emb1, sums1, emb_in2, sums_in2, emb2, emb3, *rest,
):
    row_size, x_size, chunk, ctx_rows, local_rows, plan = dims
    gain, bias = gain_in[...][None], bias_in[...][None]
    buffers, (load_sem, send_sem, recv_sem) = rest[:-3], rest[-3:]
    chains, buffers = (buffers[:6], buffers[6:12]), buffers[12:]
    z_size = row_size // x_size
    heads, total, _ = keys.shape
    pair = x_size * local_rows
    tab, row = lax.axis_index("tab"), lax.axis_index("row")
    core, y = lax.rem(tab, 2), tab // 2
    x, z = lax.rem(row, x_size), row // x_size
    core_peer, y_peer, x_peer = (tab ^ 1, row), (tab ^ 2, row), (tab, row ^ 1)
    row_peers = [(tab, lax.rem(row + k, row_size)) for k in range(1, row_size)]
    cross_peers = [(tab ^ 1, peer[1]) for peer in row_peers]
    numbers = {}

    def remote(name, src, dst, peer):
        i = numbers.setdefault(name, len(numbers))
        return pltpu.make_async_remote_copy(
            src_ref=src, dst_ref=dst, send_sem=send_sem.at[i], recv_sem=recv_sem.at[i],
            device_id=peer, device_id_type=MESH,
        )

    def half(rows, which):
        return pl.ds(pl.multiple_of(which * (rows // 2), 16), rows // 2)

    def columns(ref, which):
        wide = ref.shape[-1] // 2
        return pl.ds(pl.multiple_of(which * wide, LANES), wide)

    axes = {"y": (y, y_peer)}
    for bit, axis in enumerate(ROW_AXES):
        axes[axis] = (lax.rem(row // 2**bit, 2), (tab, row ^ 2**bit))
    sources = {"up": up0, "down": down0, "out": out0}
    streams = []
    for number, (name, source, rows, cols, order) in enumerate(plan):
        ref = sources[source].reshape(2, 2, 2, *sources[source].shape[1:])
        ref = ref.at[:, :, :, pl.ds(*rows), pl.ds(*cols)]
        dims_left, steps = list(ROW_AXES[::-1]), []
        shape = [2, 2, 2, rows[1], cols[1]]
        landing = buffers[6 * number : 6 * number + 6]
        for k, axis in enumerate(order):
            mine, (here, peer) = [], axes[axis]
            if axis == "y":
                wide = shape[-1] // 2
                kept, sent = (
                    (slice(None),) * (len(shape) - 1) + (pl.ds(pl.multiple_of(which * wide, LANES), wide),)
                    for which in (here, 1 - here)
                )
                shape = shape[:-1] + [wide]
            else:
                at = dims_left.index(axis)
                kept, sent = ((slice(None),) * at + (which,) for which in (here, 1 - here))
                dims_left.pop(at)
                shape = shape[:at] + shape[at + 1 :]
            copy = remote((name, axis), ref.at[sent], landing[k], peer)
            own = pltpu.make_async_copy(ref.at[kept], landing[4], load_sem.at[9 + number]) if k == 0 else None
            steps.append((copy, own, ref.at[kept] if k else landing[4], landing[k]))
            ref = landing[k]
        streams.append((steps, landing[5]))
    loads = [
        pltpu.make_async_copy(src, dst, load_sem.at[i])
        for i, (src, dst) in enumerate(
            (
                (g_hbm, g_in), (outs_hbm, outs), (queries_hbm, queries), (keys_hbm, keys), (values_hbm, values),
                (attn_hbm, attn_in), (feat_hbm, feat), (w_mine_hbm, w_mine), (branch_hbm, d_branch),
            )
        )
    ]

    def advance(number, k):
        steps, last = streams[number]
        copy, own, mine, taken = steps[k]
        copy.wait()
        if own is not None:
            own.wait()
        if k + 1 < len(steps):
            lead = taken.shape[:-2]
            size = math.prod(lead)

            @pl.loop(0, size)
            def _(i):
                at = []
                for extent in lead[::-1]:
                    at.insert(0, lax.rem(i, extent))
                    i = i // extent
                taken[tuple(at)] = taken[tuple(at)] + mine[tuple(at)]

            steps[k + 1][0].start()
        else:
            last[core, y] = taken[...] + mine[...]

    lasts = [last for _, last in streams]

    def to_y():
        return [remote(("to_y", i), last.at[core, y], last.at[core, y], y_peer) for i, last in enumerate(lasts)]

    def to_core(which):
        at = y if which == 0 else 1 - y
        return [
            remote(("to_core", which, i), last.at[core, at], last.at[core, at], core_peer)
            for i, last in enumerate(lasts)
        ]

    def start(copies):
        for copy in copies:
            copy.start()

    def wait(copies):
        for copy in copies:
            copy.wait()

    start(loads)
    greet([core_peer, y_peer] + row_peers + cross_peers)
    for steps, _ in streams:
        steps[0][0].start()
        steps[0][1].start()
    chains[1][0][...] = jnp.zeros_like(chains[1][0])

    shard = chains[0][0].shape[1]
    groups = chains[0][3].shape[0]

    def chain_core(i):
        pay, taken = chains[i][:2]
        return [remote(("core", i), pay.at[:, half(shard, 1 - core)], taken, core_peer)]

    def chain_row(i):
        _, ours, taken = chains[i][:3]
        return [remote(("row", i, k), ours.at[peer[1]], taken.at[row], peer) for k, peer in enumerate(row_peers)]

    def chain_y(i):
        return [remote(("y", i), chains[i][3], chains[i][4], y_peer)]

    def chain_last(i):
        last = chains[i][5]
        return [remote(("last", i), last.at[core], last.at[core], core_peer)]

    def link(i, k):
        pay, ours, came, total_own, came_y, last = chains[i]
        if k == 1:
            wait(chain_core(i))
            ours[...] = ours[...] + pay[:, half(shard, core)]
            start(chain_row(i))
            came[row] = ours[row]
        elif k == 2:
            wait(chain_row(i))
            for g in range(groups):
                total_own[g] = tile_sum(
                    [came[g + t * groups].astype(jnp.float32) for t in range(row_size // groups)]
                ).astype(jnp.bfloat16)
            start(chain_y(i))
        elif k == 3:
            wait(chain_y(i))
            last[core] = total_own[...] + came_y[...]
            start(chain_last(i))
        else:
            wait(chain_last(i))

    def finish_head(h):
        d_k[h] = d_kt[h].T.astype(jnp.bfloat16)
        d_v[h] = d_vt[h].T.astype(jnp.bfloat16)
        both = jnp.concatenate([d_kt[h], d_vt[h]], axis=0).astype(jnp.bfloat16)
        from_keys = tile_sum([
            jnp.dot(
                both[:, p * ctx_rows : (p + 1) * ctx_rows],
                attn_in[p * local_rows : p * local_rows + ctx_rows],
                preferred_element_type=jnp.float32,
            )
            for p in range(row_size)
        ])
        from_queries = jnp.dot(d_qt[...], attn_in[...], preferred_element_type=jnp.float32)
        grad = jnp.concatenate([from_queries, from_keys], axis=0).T.astype(jnp.bfloat16)
        for one in range(heads):
            i = one // (heads - 1)
            pay = chains[i][0]
            each = HEAD_DIM if i else (heads - 1) * HEAD_DIM
            first = 0 if i else one * HEAD_DIM

            @pl.when(h == one)
            def _():
                for n in range(3):
                    piece = grad[:, n * HEAD_DIM : (n + 1) * HEAD_DIM]
                    for p in range(row_size):
                        pay[p, :, n * each + first : n * each + first + HEAD_DIM] = piece[p * shard : (p + 1) * shard]
                if one >= heads - 2:
                    start(chain_core(i))

    d_kt[...] = jnp.zeros_like(d_kt)
    d_vt[...] = jnp.zeros_like(d_vt)
    whole = heads // 2

    def unpack(p):
        packed = g_in[p]
        parts = []
        for h in range(whole):
            tile = packed[h * local_rows : (h + 1) * local_rows]
            parts += [tile[:, :HEAD_DIM], tile[:, HEAD_DIM:]]
        if heads % 2:
            tile = packed[whole * local_rows :]
            parts.append(jnp.concatenate([tile[:, :HEAD_DIM], tile[:, HEAD_DIM:]], axis=0))
        rows = pl.ds(pl.multiple_of(p * local_rows, 16), local_rows)
        for h, part in enumerate(parts):
            part = part.astype(jnp.float32)
            result = outs[h, rows, :HEAD_DIM].astype(jnp.float32)
            inner = jnp.sum(part * result, axis=-1, keepdims=True)
            wide = jnp.concatenate([part, jnp.zeros_like(part)], axis=-1)
            grads[h, rows] = set_lanes(wide, HEAD_DIM, split_three(-inner))

    def segment(step, _):
        h, k = step // z_size, lax.rem(step, z_size)
        there = k
        rows = pl.ds(pl.multiple_of(there * pair, LANES), pair)

        for at, i, n in CHAIN_STEPS:

            @pl.when(step == at)
            def _():
                link(i, n)

        for at, number, n in ATTEND_STEPS:

            @pl.when(step == at)
            def _():
                advance(number, n)

        query, grad = queries[h, rows], grads[h, rows]
        query_t = query[:, :HEAD_DIM].T
        grad_t = grad[:, :HEAD_DIM].T
        d_query = jnp.zeros((pair, LANES), jnp.float32)
        for i in range(total // chunk):
            at = pl.ds(i * chunk, chunk)
            key, value = keys[h, at], values[h, at]
            probs = jnp.exp(lax.dot_general(query, key, NT, preferred_element_type=jnp.float32))
            d_probs = lax.dot_general(grad, value, NT, preferred_element_type=jnp.float32)
            d_scores = (probs * d_probs).astype(jnp.bfloat16)
            d_vt[h, :, at] += jnp.dot(grad_t, probs.astype(jnp.bfloat16), preferred_element_type=jnp.float32)
            d_kt[h, :, at] += jnp.dot(query_t, d_scores, preferred_element_type=jnp.float32)
            d_query += jnp.dot(d_scores, key, preferred_element_type=jnp.float32)
        d_query = (d_query[:, :HEAD_DIM] * HEAD_DIM ** (-0.5)).astype(jnp.bfloat16)
        d_q[h, rows] = d_query
        d_qt[:, rows] = d_query.T

        @pl.when(step == z_size - 1)
        def _():
            wait(loads[5:])

        @pl.when(k == z_size - 1)
        def _():
            finish_head(h)

        return 0

    wait(loads[:2])
    for p in range(row_size):
        unpack(p)
    wait(loads[2:5])
    lax.fori_loop(0, z_size * heads, segment, 0)

    d_emb[...] = jnp.zeros_like(d_emb)
    d_gain[...] = jnp.zeros_like(d_gain)
    d_bias[...] = jnp.zeros_like(d_bias)

    near_bit, far_bit = lax.rem(z, 2), z // 2
    near_peer, far_peer = (tab, row ^ 2), (tab, row ^ 4)

    def term_x(k):
        return remote(("term_x", k), terms.at[k, 1 - x], terms_x.at[k], x_peer)

    def term_near(k):
        return remote(("term_near", k), terms.at[k, x], terms_z.at[k], near_peer)

    def term_far():
        return remote("term_far", terms.at[2, x], terms_far, far_peer)

    def term_sum(k):
        term_x(k).wait()
        total = terms[k, x].astype(jnp.float32) + terms_x[k].astype(jnp.float32)
        if k >= 2:
            term_near(k - 2).wait()
            total = total + terms_z[k - 2].astype(jnp.float32)
        terms[k, x] = total.astype(jnp.bfloat16)
        if k < 2:
            term_near(k).start()
        elif k == 2:
            term_far().start()

    def project(step, _):
        there = lax.rem(far_bit + step + 1, 2) * 2 + lax.rem(near_bit + step // 2 + 1, 2)
        pieces, embeds = [], []
        for other in range(x_size):
            p = there * x_size + other
            rows = pl.ds(pl.multiple_of(p * local_rows, 16), local_rows)
            key_rows = pl.ds(pl.multiple_of(p * ctx_rows, 16), ctx_rows)
            parts = [d_q[h, rows] for h in range(heads)]
            nothing = jnp.zeros((local_rows - ctx_rows, HEAD_DIM), jnp.bfloat16)
            for ref in (d_k, d_v):
                parts += [jnp.concatenate([ref[h, key_rows], nothing], axis=0) for h in range(heads)]
            pieces.append(jnp.concatenate(parts, axis=1))
            embeds.append(feat[p])
        d_three = jnp.concatenate(pieces, axis=0)
        rows_feat = jnp.concatenate(embeds, axis=0)
        embed = jnp.dot(rows_feat, w_emb[...], preferred_element_type=jnp.float32)
        center = embed - jnp.mean(embed, axis=-1, keepdims=True)
        inverse = lax.rsqrt(jnp.mean(center * center, axis=-1, keepdims=True) + EPS)
        normed = center * inverse
        d_in = lax.dot_general(d_three, w_mine[...], NT, preferred_element_type=jnp.float32)
        d_gain[...] += jnp.sum(d_in * normed, axis=0, keepdims=True)
        d_bias[...] += jnp.sum(d_in, axis=0, keepdims=True)
        scaled = d_in * gain
        inner = (
            scaled
            - jnp.mean(scaled, axis=-1, keepdims=True)
            - normed * jnp.mean(scaled * normed, axis=-1, keepdims=True)
        )
        d_norm = (inverse * inner).astype(jnp.bfloat16)
        term = lax.dot_general(d_norm, w_emb[...], NT, preferred_element_type=jnp.float32).astype(jnp.bfloat16)
        d_emb[...] += jnp.dot(rows_feat.T, d_norm, preferred_element_type=jnp.float32)
        for other in range(x_size):
            terms[step, other] = term[other * local_rows : (other + 1) * local_rows]
        for k in range(z_size):

            @pl.when(step == k)
            def _():
                term_x(k).start()
                if k:
                    term_sum(k - 1)

        @pl.when(step == GATHER_STEP)
        def _():
            for number in range(len(streams)):
                advance(number, 3)
            start(to_y())
            start(to_core(0))

        for at, i, n in LAST_STEPS:

            @pl.when(step == at)
            def _():
                link(i, n)

        return 0

    lax.fori_loop(0, z_size, project, 0)

    own_rows = jnp.concatenate([own_feat[t] for t in range(own_feat.shape[0])], axis=0)
    own_d = jnp.concatenate([d_branch[t] for t in range(own_feat.shape[0])], axis=0)
    d_own = d_emb[...] + jnp.dot(own_rows.T, own_d, preferred_element_type=jnp.float32)
    slots_all = d_own.shape[0]
    spare = lax.broadcasted_iota(jnp.int32, d_own.shape, 0) - (slots_all - vectors.shape[0])
    d_own = jnp.where(spare == 0, d_gain[...], d_own)
    d_own = jnp.where(spare == 1, d_bias[...], d_own)
    for i in range(2, vectors.shape[0]):
        d_own = jnp.where(spare == i, vectors[i : i + 1], d_own)
    emb_rows = emb_own.shape[1]
    for p in range(row_size):
        emb_own[p] = d_own[p * emb_rows : (p + 1) * emb_rows].astype(jnp.bfloat16)

    def tail_core():
        return [
            remote("emb_core", emb_own.at[:, :, columns(emb_own, 1 - core)], emb_in0, core_peer),
            remote("sums_core", sums, sums_in0, core_peer),
        ]

    def tail_row():
        copies = []
        for k, peer in enumerate(row_peers):
            copies += [
                remote(("emb_row", k), emb_in0.at[peer[1]], emb_in1.at[row], peer),
                remote(("sums_row", k), sums0, sums_in1.at[row], peer),
            ]
        return copies

    def tail_y():
        return [remote("emb_y", emb1, emb_in2, y_peer), remote("sums_y", sums1, sums_in2, y_peer)]

    at_core = columns(emb_own, core)

    def tail_all():
        peers = row_peers + [core_peer] + cross_peers
        return [
            remote(("emb_all", k), emb2, emb3.at[row, :, at_core], peer) for k, peer in enumerate(peers)
        ]

    start(tail_core())
    link(1, 2)
    wait(tail_core())
    emb_in0[...] = emb_in0[...] + emb_own[:, :, at_core]
    sums0[...] = sums[...] + sums_in0[...]
    start(tail_row())
    emb_in1[row] = emb_in0[row]
    sums_in1[row] = sums0[...]
    wait(to_y())
    start(to_core(1))

    term_sum(z_size - 1)
    term_far().wait()
    for t in range(own_feat.shape[0]):
        term = lax.dot_general(d_branch[t], w_emb[...], NT, preferred_element_type=jnp.float32)
        from_heads = jnp.where(far_bit == t, terms[z_size - 1, x].astype(jnp.float32), terms_far[...].astype(jnp.float32))
        term = term + from_heads
        slots = qry_grad.shape[2]
        lane = lane_of(term.shape)
        term = jnp.where(lane < counts[t], term, 0.0)
        ctx_grad[:, t] = term[:ctx_rows].T[:slots].astype(jnp.bfloat16)
        qry_grad[t] = term[ctx_rows:, :slots].astype(jnp.bfloat16)

    wait(tail_row())
    emb1[...] = tile_sum([emb_in1[p].astype(jnp.float32) for p in range(row_size)]).astype(jnp.bfloat16)
    sums1[...] = tile_sum([sums_in1[p] for p in range(row_size)])
    start(tail_y())
    link(1, 3)
    wait(tail_y())
    emb2[...] = emb1[...] + emb_in2[...]
    sums_all = sums1[...] + sums_in2[...]
    start(tail_all())
    emb3[row, :, at_core] = emb2[...]
    link(0, 4)
    link(1, 4)
    for i in range(2):
        parts = []
        for n in range(3):
            for g in range(groups):
                for h in range(heads):
                    which = h // (heads - 1)
                    each = HEAD_DIM if which else (heads - 1) * HEAD_DIM
                    first = n * each + (0 if which else h * HEAD_DIM)
                    parts.append(chains[which][5][i, g][:, first : first + HEAD_DIM])
        qkv_all[i * (shard // 2) : (i + 1) * (shard // 2)] = jnp.concatenate(parts, axis=1)
    wait(to_core(0))
    wait(to_core(1))
    results = {"up": up_all, "down": down_all, "out": out_all}
    for (_, source, rows, cols, _), last in zip(plan, lasts):
        deep, wide = last.shape[2:]
        half_rows = sources[source].shape[1]
        for i in range(2):
            for j in range(2):
                down_at, across = i * half_rows + rows[0], cols[0] + j * wide
                results[source][down_at : down_at + deep, across : across + wide] = last[i, j]
    wait(tail_all())
    slot_count = emb_all.shape[0]
    whole_emb = jnp.concatenate([emb3[p] for p in range(row_size)], axis=0).astype(jnp.float32)
    emb_all[...] = whole_emb[:slot_count]
    vec = whole_emb[slots_all - vectors.shape[0] :]
    dmodel = vec.shape[1]
    wide = (vectors.shape[0] - 4) * dmodel // row_size
    own_vec, own_up = vec[:4, :shard], vec[4:5, :wide]
    for p in range(1, row_size):
        at = p * wide
        own_vec = jnp.where(row == p, vec[:4, p * shard : (p + 1) * shard], own_vec)
        piece = vec[4 + at // dmodel : 5 + at // dmodel, at % dmodel : at % dmodel + wide]
        own_up = jnp.where(row == p, piece, own_up)
    own_all[...] = jnp.zeros_like(own_all)
    own_all[:4, :shard] = own_vec
    own_all[4:5] = own_up
    rms = jnp.sqrt(sums_all / (sums_all[:1, 4:5] * dmodel))
    own_all[5:6, :LANES] = rms[:1]


def back(counts, halves, queries, keys, values, outs, attn_in, g_in, feat, w_emb, w_mine, gain, bias, own_feat, d_branch,
         vectors, sums, slot_count, ctx_rows, groups, chunk, collective_id):
    row_size, local_rows, slots = feat.shape
    heads, total, _ = keys.shape
    all_rows = queries.shape[1]
    dmodel = w_emb.shape[1]
    width = heads * HEAD_DIM
    x_size = 2
    z_size = row_size // x_size
    shapes = [(2 * h.shape[1], h.shape[2]) for h in halves]
    bf16 = lambda *shape: pltpu.VMEM(shape, jnp.bfloat16)
    f32 = lambda *shape: pltpu.VMEM(shape, jnp.float32)
    plan = plan_streams([h.shape[1:] for h in halves])
    landings = []
    for _, _, rows, cols, order in plan:
        lead, wide, first = 8, cols[1], None
        for axis in order:
            lead, wide = (lead, wide // 2) if axis == "y" else (lead // 2, wide)
            shape = (2,) * (lead.bit_length() - 1) + (rows[1], wide)
            first = first or shape
            landings.append(bf16(*shape))
        landings += [bf16(*first), bf16(2, 2, rows[1], wide)]
    by_head = bf16(heads, all_rows, LANES)
    shard, emb_rows = dmodel // row_size, slots // row_size
    inputs = [by_head, bf16(*keys.shape), bf16(*keys.shape), by_head]
    inputs += [bf16(*a.shape) for a in (attn_in, g_in, feat, w_mine, d_branch)]
    attention = [
        by_head, bf16(heads, all_rows, HEAD_DIM), bf16(HEAD_DIM, all_rows),
        f32(heads, HEAD_DIM, total), f32(heads, HEAD_DIM, total),
        bf16(heads, total, HEAD_DIM), bf16(heads, total, HEAD_DIM),
        bf16(z_size, x_size, local_rows, slots), bf16(z_size, local_rows, slots), bf16(2, local_rows, slots),
        bf16(local_rows, slots),
        f32(slots, dmodel), f32(1, dmodel), f32(1, dmodel),
    ]
    half_emb = (row_size, emb_rows, dmodel // 2)
    tail = [
        bf16(row_size, emb_rows, dmodel), bf16(*half_emb), f32(*sums.shape), f32(*sums.shape),
        bf16(*half_emb), f32(row_size, *sums.shape), bf16(emb_rows, dmodel // 2), f32(*sums.shape),
        bf16(emb_rows, dmodel // 2), f32(*sums.shape), bf16(emb_rows, dmodel // 2), bf16(row_size, emb_rows, dmodel),
    ]
    for each in (heads - 1, 1):
        wide = -(-3 * each * HEAD_DIM // LANES) * LANES
        mine, ours = (row_size, shard // 2, wide), (groups, shard // 2, wide)
        tail += [bf16(row_size, shard, wide), bf16(*mine), bf16(*mine), bf16(*ours), bf16(*ours), bf16(2, *ours)]
    sends = 7 * len(plan) + 18 + 6 * (row_size - 1)
    vmem = pl.BlockSpec(memory_space=pltpu.VMEM)
    anywhere = pl.BlockSpec(memory_space=pl.ANY)
    f32_out = lambda *shape: jax.ShapeDtypeStruct(shape, jnp.float32)
    bf16_out = lambda *shape: jax.ShapeDtypeStruct(shape, jnp.bfloat16)
    return pl.pallas_call(
        functools.partial(back_kernel, (row_size, x_size, chunk, ctx_rows, local_rows, plan)),
        out_shape=[
            bf16_out(slot_count, own_feat.shape[0], ctx_rows),
            bf16_out(own_feat.shape[0], local_rows - ctx_rows, slot_count),
            f32_out(slot_count, dmodel),
            f32_out(8, (vectors.shape[0] - 4) * dmodel // row_size),
            bf16_out(shard, 3 * dmodel),
            bf16_out(*shapes[2]),
            bf16_out(*shapes[0]),
            bf16_out(*shapes[1]),
        ],
        in_specs=[pl.BlockSpec(memory_space=pltpu.SMEM)] + [anywhere] * 12 + [vmem] * 6,
        out_specs=[vmem] * 8,
        scratch_shapes=inputs + attention + tail + landings + [
            pltpu.SemaphoreType.DMA((9 + len(plan),)),
            pltpu.SemaphoreType.DMA((sends,)),
            pltpu.SemaphoreType.DMA((sends,)),
        ],
        compiler_params=pltpu.CompilerParams(
            collective_id=collective_id, has_side_effects=True, vmem_limit_bytes=62 * 2**20
        ),
        name="back",
    )(counts, *halves, queries, keys, values, outs, attn_in, g_in, feat, w_mine, d_branch, w_emb, gain, bias, own_feat,
      vectors, sums)


def finish(own, lengths, kept, widened):
    sources = [*kept, *widened]
    count = len(sources)

    def kernel(own_ref, *refs):
        vectors, refs = refs[count : count + len(lengths)], refs[:count] + refs[count + len(lengths) :]
        ins, outs, held = refs[:count], refs[count : 2 * count], refs[2 * count : 3 * count]
        wide, (in_sem, out_sem) = refs[3 * count : -2], refs[-2:]
        loads = [pltpu.make_async_copy(ins[i], held[i], in_sem.at[i]) for i in range(count)]
        for load in loads:
            load.start()
        for i, size in enumerate(lengths):
            vectors[i][...] = own_ref[i, :size]
        stores = []
        for i, load in enumerate(loads):
            load.wait()
            ready = held[i]
            if i >= len(kept):
                ready = wide[i - len(kept)]
                ready[...] = held[i][...].astype(jnp.float32)
            stores.append(pltpu.make_async_copy(ready, outs[i], out_sem.at[i]))
            stores[-1].start()
        for store in stores:
            store.wait()

    return pl.pallas_call(
        kernel,
        out_shape=[jax.ShapeDtypeStruct((size,), jnp.float32) for size in lengths]
        + [jax.ShapeDtypeStruct(a.shape, a.dtype) for a in kept]
        + [jax.ShapeDtypeStruct(a.shape, jnp.float32) for a in widened],
        in_specs=[pl.BlockSpec(memory_space=pltpu.VMEM)] + [pl.BlockSpec(memory_space=pl.ANY)] * count,
        out_specs=[pl.BlockSpec(memory_space=pltpu.VMEM)] * len(lengths) + [pl.BlockSpec(memory_space=pl.ANY)] * count,
        scratch_shapes=[pltpu.VMEM(a.shape, a.dtype) for a in sources]
        + [pltpu.VMEM(a.shape, jnp.float32) for a in widened]
        + [pltpu.SemaphoreType.DMA((count,))] * 2,
        compiler_params=pltpu.CompilerParams(vmem_limit_bytes=62 * 2**20),
        name="finish",
    )(own, *sources)


def local_by_heads(
    ctx_feat,
    qry_feat,
    feat_count,
    ctx_count,
    qry_count,
    w_emb,
    ln1_gain,
    ln1_bias,
    w_qkv,
    w_out,
    ln2_gain,
    ln2_bias,
    w_up,
    b_up,
    w_down,
    ctx_cot,
    qry_cot,
):
    table_count, slot_count, ctx_rows = ctx_feat.shape
    qry_rows = qry_feat.shape[2]
    local_rows = ctx_rows + qry_rows
    dmodel = w_out.shape[0]
    head_count = dmodel // HEAD_DIM
    row_size = lax.axis_size("row")
    total_ctx = ctx_rows * row_size
    groups = row_size // table_count
    heads = head_count // groups
    packed, back_queries, keys, values, outs, table_feat, w_mine, attn_in, by_row, w_emb_pad = front(
        feat_count,
        ctx_count,
        jnp.transpose(ctx_feat, (1, 0, 2)),
        jnp.transpose(qry_feat, (0, 2, 1)),
        w_emb,
        ln1_gain,
        ln1_bias,
        w_qkv,
        total_ctx,
        heads,
        groups,
        math.gcd(total_ctx, 1024),
        0,
    )
    ctx_out, qry_out, g_in, up_half, down_half, out_half, d_branch, vectors, sums = middle(
        ctx_count,
        qry_count,
        by_row,
        w_emb_pad,
        ln2_gain,
        ln2_bias,
        b_up[None],
        packed,
        w_out,
        w_up,
        w_down,
        ctx_cot,
        qry_cot,
        groups,
        heads,
        math.gcd(w_up.shape[1], 1024),
        1,
    )
    ctx_feat_grad, qry_feat_grad, grad_w_emb, own, qkv_all, out_all, up_all, down_all = back(
        feat_count,
        (up_half, down_half, out_half),
        back_queries,
        keys,
        values,
        outs,
        attn_in,
        g_in,
        table_feat,
        w_emb_pad,
        w_mine,
        ln1_gain,
        ln1_bias,
        by_row,
        d_branch,
        vectors,
        sums,
        slot_count,
        ctx_rows,
        groups,
        math.gcd(total_ctx, 512),
        2,
    )
    shard = dmodel // row_size
    (
        gain1_all, bias1_all, gain2_all, bias2_all, upbias_all, rms,
        ctx_out, qry_out, ctx_feat_grad, qry_feat_grad, grad_w_emb, up_all, down_all, qkv_all, out_all,
    ) = finish(
        own, (shard,) * 4 + (w_up.shape[1] // row_size, 4),
        (ctx_out, qry_out, ctx_feat_grad, qry_feat_grad, grad_w_emb), (up_all, down_all, qkv_all, out_all)
    )
    ctx_feat_grad = jnp.transpose(ctx_feat_grad, (1, 0, 2))
    qry_feat_grad = jnp.transpose(qry_feat_grad, (0, 2, 1))
    return (
        ctx_out,
        qry_out,
        ctx_feat_grad,
        qry_feat_grad,
        grad_w_emb,
        gain1_all,
        bias1_all,
        qkv_all,
        out_all,
        gain2_all,
        bias2_all,
        up_all,
        upbias_all,
        down_all,
        rms,
    )


def local(ctx_feat, qry_feat, *rest):
    table_count, slot_count, ctx_rows = ctx_feat.shape
    qry_rows = qry_feat.shape[2]
    head_count = rest[6].shape[0] // HEAD_DIM
    row_size = lax.axis_size("row")
    even = row_size % table_count == 0 and head_count % (row_size // table_count) == 0 and head_count // (row_size // table_count) > 1
    whole = slot_count + 4 + rest[10].shape[1] // rest[6].shape[0] <= LANES and row_size == 8 and table_count == 2 and ctx_rows % LANES == 0 and qry_rows % 32 == 0
    inner = local_by_heads if even and whole else local_by_rows
    return inner(ctx_feat, qry_feat, *rest)


def solution(mesh):
    in_specs = (
        P("tab", None, "row"),
        P("tab", None, "row"),
        P("tab"),
        P("tab"),
        P("tab"),
        P(),
        P(),
        P(),
        P(),
        P(),
        P(),
        P(),
        P(),
        P(),
        P(),
        P("tab", "row", None),
        P("tab", "row", None),
    )
    out_specs = (
        P("tab", "row", None),
        P("tab", "row", None),
        P("tab", None, "row"),
        P("tab", None, "row"),
        P(),
        P("row"),
        P("row"),
        P("row", None),
        P("row", None),
        P("row"),
        P("row"),
        P("row", None),
        P("row"),
        P("row", None),
        P(),
    )
    return jax.shard_map(local, mesh=mesh, in_specs=in_specs, out_specs=out_specs, check_vma=False)
```
